128 devices in a mesh: gx: 8 (over x_lo, z), gy: 16 (over x_hi, y, core).
Axes of the slice: x: 4 (x_hi: 2, x_lo: 2; x = x_hi * 2 + x_lo), y: 4, z: 4, core: 2. Of those that a mesh axis runs over, the one named last changes fastest.
Arguments:
- ocean_forcing: float32 [16384, 4, 8, 128], P(('gx', 'gy')), may hold values from -3 to 3
- route: int32 [16384], replicated, may hold values from 0 to 16383, as said below
- land_mask: int32 [2048, 8192], P('gy', 'gx'), may hold values 0 or 1
- mass: float32 [2048, 8192], P('gy', 'gx'), may hold values from 2 to 4
- strength: float32 [2048, 8192], P('gy', 'gx'), may hold values from 1 to 2
- velocity_start: float32 [2, 2048, 8192], P(None, 'gy', 'gx'), may hold values from -4 to 4
- stress_start: float32 [3, 2048, 8192], P(None, 'gy', 'gx'), may hold values from -4 to 4
Outputs:
- ocean_velocity: float32 [16384, 2, 8, 128], P(('gx', 'gy'))
- ice_stress: float32 [3, 2048, 8192], P(None, 'gy', 'gx')
The draws below stay inside these ranges and needn't reach their ends.
Inputs may be any that keep to these rules, and one draw needn't show every extreme that they name: route is a permutation of the 16384 tile numbers; the 128 tiles of each ocean device (aligned blocks of 128 entries) go exactly 2 each to 64 ice blocks (ice block route[t] // 128) and to no others.
All inputs are finite; a program needn't handle non-finite values. No bound on the sum of `land_mask` on one device may be relied on, other than what follows from the above.
Results may differ from the reference program's by a relative error of at most 0.00002.
Values sent between devices are 32-bit elements; how exact they have to be, the bound alone decides.
A program may use at most 64 MiB of HBM per device.

```python
import jax
import jax.numpy as jnp

TY = 8
TX = 128
TCX = 8
TRY = 16
ITERS = 16
TPD = 128
BLOCKS = 128
CAP = 2
TILES = 16384
NY = 2048
NX = 8192
N_GX = 8
N_GY = 16


def draw_route(key, part):
    keys = jax.random.split(jax.random.fold_in(key, 17), 5)
    groups = BLOCKS // 2
    shifts = jax.random.permutation(keys[0], BLOCKS)[:groups]
    relabel_out = jax.random.permutation(keys[1], BLOCKS)
    relabel_in = jax.random.permutation(keys[2], BLOCKS)
    sources = jnp.arange(BLOCKS, dtype=jnp.int32)
    dest = relabel_out[(relabel_in[sources][:, None] + shifts[None, :]) % BLOCKS]
    local_perms = jax.vmap(lambda k: jax.random.permutation(k, TPD))(jax.random.split(keys[3], BLOCKS))
    member = jnp.arange(groups, dtype=jnp.int32)[:, None] * CAP + jnp.arange(CAP, dtype=jnp.int32)[None, :]
    dest_full = jnp.broadcast_to(dest[:, :, None], (BLOCKS, groups, CAP))
    member_full = jnp.broadcast_to(member[None, :, :], (BLOCKS, groups, CAP))
    local = local_perms[dest_full, member_full]
    values = (dest_full * TPD + local).reshape(BLOCKS, TPD)
    order = jax.vmap(lambda k: jax.random.permutation(k, TPD))(jax.random.split(keys[4], BLOCKS))
    shuffled = jnp.take_along_axis(values, order, axis=1)
    return shuffled.reshape(-1).astype(jnp.int32)


def log_between(key, low, high):
    unit = jax.random.uniform(key, (NY, NX), jnp.float32)
    start = jnp.log(jnp.float32(low))
    stop = jnp.log(jnp.float32(high))
    return jnp.clip(jnp.exp(start + unit * (stop - start)), low, high).astype(jnp.float32)


def draw_mass(key, part):
    key = jax.random.fold_in(key, 29)
    return log_between(key, 2.0, 4.0)


def draw_strength(key, part):
    key = jax.random.fold_in(key, 31)
    return log_between(key, 1.0, 2.0)


def place_ends(drawn, rng, low, top_value):
    place = [jax.random.randint(jax.random.fold_in(rng, axis), (), 0, length) for axis, length in enumerate(drawn.shape)]
    widest = drawn.shape.index(max(drawn.shape))
    beside = place[:widest] + [(place[widest] + 1) % drawn.shape[widest]] + place[widest + 1:]
    return drawn.at[tuple(place)].set(low).at[tuple(beside)].set(top_value)


def block_levels(rng, dims, pieces, least, high):
    gain = 1.0
    for dim, parts in pieces:
        draws = jax.random.uniform(jax.random.fold_in(jax.random.fold_in(rng, 6), dim), (parts,), jnp.float32, least / len(pieces), high / len(pieces))
        gain = gain * jnp.repeat(jnp.exp(draws), dims[dim] // parts).reshape((-1,) + (1,) * (len(dims) - 1 - dim))
    return gain


def noise(key, extent, deviation, most, cuts=(), kind=jnp.bfloat16):
    level = block_levels(key, extent, cuts, -0.22, 0.18) if cuts else 1.0
    values = jax.random.normal(key, extent, jnp.float32) * deviation * level
    return jnp.minimum(jnp.maximum(values, -most), most).astype(kind)


def setup_inputs(seed: int = 0) -> dict:
    streams_of = jax.random.split(jax.random.key(seed), 8)
    return {
        "ocean_forcing": noise(streams_of[0], (TILES, 4, TY, TX), 0.5, 3.0, ((0, 128),), jnp.float32),
        "route": draw_route(jax.random.fold_in(streams_of[7], 71), 0),
        "land_mask": place_ends((jax.random.randint(streams_of[2], (NY, NX), 0, 4) < 3).astype(jnp.int32), jax.random.fold_in(streams_of[2], 1), 0, 1),
        "mass": draw_mass(jax.random.fold_in(streams_of[7], 71), 0),
        "strength": draw_strength(jax.random.fold_in(streams_of[7], 71), 0),
        "velocity_start": noise(streams_of[5], (2, NY, NX), 1.0, 4.0, ((1, 16), (2, 8)), jnp.float32),
        "stress_start": noise(streams_of[6], (3, NY, NX), 1.0, 4.0, ((1, 16), (2, 8)), jnp.float32),
    }


relax_rate = 0.1
floor_square = 1.0
drag_rate = 0.5
turn_rate = 0.3
tilt_weight = 0.05

def advance(extended, strength_ext, mass, force_x, force_y, share):
    zonal = extended[0]
    merid = extended[1]
    stress_sum = extended[2]
    stress_diff = extended[3]
    stress_shear = extended[4]
    zonal_dx = 0.5 * (zonal[1:-1, 2:] - zonal[1:-1, :-2])
    zonal_dy = 0.5 * (zonal[2:, 1:-1] - zonal[:-2, 1:-1])
    merid_dx = 0.5 * (merid[1:-1, 2:] - merid[1:-1, :-2])
    merid_dy = 0.5 * (merid[2:, 1:-1] - merid[:-2, 1:-1])
    divergence = zonal_dx + merid_dy
    tension = zonal_dx - merid_dy
    shearing = zonal_dy + merid_dx
    strain_size = jnp.sqrt(divergence * divergence + 0.25 * (tension * tension + shearing * shearing) + floor_square)
    viscous = relax_rate * strength_ext[1:-1, 1:-1] / strain_size
    new_sum = (stress_sum[1:-1, 1:-1] + viscous * (divergence - strain_size)) / (1.0 + relax_rate)
    new_diff = (stress_diff[1:-1, 1:-1] + 0.25 * viscous * tension) / (1.0 + relax_rate)
    new_shear = (stress_shear[1:-1, 1:-1] + 0.125 * viscous * shearing) / (1.0 + relax_rate)
    normal_xx = 0.5 * (new_sum + new_diff)
    normal_yy = 0.5 * (new_sum - new_diff)
    push_x = 0.5 * (normal_xx[1:-1, 2:] - normal_xx[1:-1, :-2]) + 0.5 * (new_shear[2:, 1:-1] - new_shear[:-2, 1:-1])
    push_y = 0.5 * (new_shear[1:-1, 2:] - new_shear[1:-1, :-2]) + 0.5 * (normal_yy[2:, 1:-1] - normal_yy[:-2, 1:-1])
    right_x = mass * zonal[2:-2, 2:-2] + push_x + force_x
    right_y = mass * merid[2:-2, 2:-2] + push_y + force_y
    damping = mass + drag_rate
    turning = turn_rate * mass
    determinant = damping * damping + turning * turning
    zonal_new = (damping * right_x + turning * right_y) / determinant * share
    merid_new = (damping * right_y - turning * right_x) / determinant * share
    return jnp.stack([zonal_new, merid_new, new_sum[1:-1, 1:-1], new_diff[1:-1, 1:-1], new_shear[1:-1, 1:-1]])

def extend(field, signs):
    cycle = jnp.concatenate([field[:, :, -2:], field, field[:, :, :2]], axis=2)
    folded = jnp.flip(cycle[:, -2:, :], axis=(1, 2)) * signs[:, None, None]
    south = jnp.zeros((field.shape[0], 2, cycle.shape[2]), field.dtype)
    return jnp.concatenate([south, cycle, folded], axis=1)

def to_grid(tiles):
    comps = tiles.shape[1]
    shaped = tiles.reshape(N_GX, N_GY, TRY, TCX, comps, TY, TX)
    return shaped.transpose(4, 1, 2, 5, 0, 3, 6).reshape(comps, NY, NX)

def to_tiles(grid):
    comps = grid.shape[0]
    shaped = grid.reshape(comps, N_GY, TRY, TY, N_GX, TCX, TX)
    return shaped.transpose(4, 1, 2, 5, 0, 3, 6).reshape(TILES, comps, TY, TX)

def reference(ocean_forcing, route, land_mask, mass, strength, velocity_start, stress_start):
    anchor = jnp.zeros((TILES,), jnp.int32).at[route].set(jnp.arange(TILES, dtype=jnp.int32))
    ice_forcing = to_grid(ocean_forcing[anchor])
    force_x = ice_forcing[0] + tilt_weight * mass * ice_forcing[2]
    force_y = ice_forcing[1] + tilt_weight * mass * ice_forcing[3]
    share = land_mask.astype(jnp.float32)
    strength_ext = extend(strength[None], jnp.ones((1,), jnp.float32))[0]
    signs = jnp.array([-1.0, -1.0, 1.0, 1.0, 1.0], jnp.float32)
    state = jnp.concatenate([velocity_start * share[None], stress_start], axis=0)
    for sweep in range(ITERS):
        state = advance(extend(state, signs), strength_ext, mass, force_x, force_y, share)
    ocean_velocity = to_tiles(state[:2])[route]
    return (ocean_velocity, state[2:])
```

```python
import functools

import jax
import jax.numpy as jnp
from jax import lax
from jax.experimental import pallas as pl
from jax.experimental.pallas import tpu as pltpu
from jax.sharding import PartitionSpec as P

MESH = pl.DeviceIdType.MESH
ITERS = 16
RELAX = 0.1
DRAG = 0.5
TURN = 0.3
TILT = 0.05
KEEP = 1.0 / (1.0 + RELAX)

N_GX = 8
N_GY = 16
N_DEV = 128
HALO = 2 * ITERS
ROWS = 128
EXT = ROWS + 2 * HALO
STEP = EXT // 8
TILES_X = 8
CT = TILES_X + 1

MASS, STRENGTH, ZONAL, MERID, SUM, DIFF, SHEAR, FORCE_X, FORCE_Y = range(9)
STATIC = 7
CU, CV, CXX, CYY, CSH, CSTR = range(6)
KS, KM, KFX, KFY, KA, KB = range(6)


def peers():
    order = []
    for n in range(32):
        j = (n * 13) % 32
        dx, dy, dc = j // 8, (j // 2) % 4, j % 2
        off = (n + n // 4 + 3 * dx + dy) % 4 if (dx, dy, dc) != (0, 0, 0) else 0
        order.append((dx, dy, dc, off))
    return order


def each_peer(visit):
    gx = lax.axis_index("gx")
    gy = lax.axis_index("gy")
    z, x_lo = gx % 4, gx // 4
    x_hi, y, core = gy // 8, (gy // 2) % 4, gy % 2
    x = x_hi * 2 + x_lo
    xs = [(x + d) % 4 for d in range(4)]
    part_gx = [(v % 2) * 4 for v in xs]
    part_gy = [(v // 2) * 8 for v in xs]
    ys = [((y + d) % 4) * 2 for d in range(4)]
    cores = [core, 1 - core]
    zs = tuple((z + d) % 4 for d in range(4))

    def turn(q, zs):
        for dx, dy, dc, off in peers():
            there = (part_gx[dx] + zs[off], part_gy[dx] + ys[dy] + cores[dc])
            if (dx, dy, dc) == (0, 0, 0):
                pl.when(q > 0)(functools.partial(visit, *there))
            else:
                visit(*there)
        return zs[1:] + zs[:1]

    lax.fori_loop(0, 4, turn, zs)


def wait_for(ref, sem):
    pltpu.make_async_copy(ref, ref, sem).wait()


def left_right(row, lane):
    n = len(row)
    left = [pltpu.roll(jnp.where(lane == 127, row[j - 1], row[j]), 1, 1) for j in range(n)]
    right = [pltpu.roll(jnp.where(lane == 0, row[(j + 1) % n], row[j]), 127, 1) for j in range(n)]
    return left, right


def kernel(
    send_tile, recv_slot, back_tile, back_slot,
    ocean, mask, mass, strength, velocity, stress,
    out_velocity, out_stress,
    tiles, returning, arrived_back, oc, outgoing, arrived, ext, ext_mask, side_w, side_e, mask_w, mask_e, side_fw, side_fe,
    state, const, in_sem, a2a_sem, halo_sem,
):
    gx = lax.axis_index("gx")
    gy = lax.axis_index("gy")
    me = gx * N_GY + gy
    top = gy == N_GY - 1
    inner = pl.ds(HALO, ROWS)
    lane = lax.broadcasted_iota(jnp.int32, (8, 128), 1)

    pltpu.make_async_copy(ocean, oc, in_sem.at[0]).start()
    for j in range(TILES_X):
        cols = pl.ds(j * 128, 128)
        pltpu.make_async_copy(mass.at[:, cols], ext.at[MASS, j, inner], in_sem.at[1]).start()
        pltpu.make_async_copy(strength.at[:, cols], ext.at[STRENGTH, j, inner], in_sem.at[1]).start()
        pltpu.make_async_copy(velocity.at[:, :, cols], ext.at[pl.ds(ZONAL, 2), j, inner], in_sem.at[1]).start()
        pltpu.make_async_copy(stress.at[:, :, cols], ext.at[pl.ds(SUM, 3), j, inner], in_sem.at[1]).start()
        pltpu.make_async_copy(mask.at[:, cols], ext_mask.at[j, inner], in_sem.at[2]).start()

    barrier = pltpu.get_barrier_semaphore()

    def greet(a, b):
        pl.semaphore_signal(barrier, inc=1, device_id=(a, b), device_id_type=MESH)

    each_peer(greet)

    wait_for(oc, in_sem.at[0])

    def pack(i, carry):
        for h in range(8):
            outgoing[i * 8 + h] = oc[send_tile[i * 8 + h]]
        return carry

    lax.fori_loop(0, 2 * N_DEV // 8, pack, 0)
    pl.semaphore_wait(barrier, N_DEV - 1)

    def send_forcing(a, b):
        pltpu.make_async_remote_copy(
            outgoing.at[pl.ds((a * N_GY + b) * 2, 2)], arrived.at[pl.ds(me * 2, 2)],
            a2a_sem.at[0], a2a_sem.at[1], device_id=(a, b), device_id_type=MESH,
        ).start()

    wait_for(ext.at[pl.ds(0, STATIC), pl.ds(0, TILES_X), inner], in_sem.at[1])
    wait_for(ext_mask.at[pl.ds(0, TILES_X), inner], in_sem.at[2])
    east = ((gx + 1) % N_GX, gy)
    west = ((gx + N_GX - 1) % N_GX, gy)

    def columns(first, count, to_west, to_east, sems):
        a = pltpu.make_async_remote_copy(
            ext.at[pl.ds(first, count), TILES_X - 1, inner], to_west,
            halo_sem.at[sems], halo_sem.at[sems + 1], device_id=east, device_id_type=MESH)
        b = pltpu.make_async_remote_copy(
            ext.at[pl.ds(first, count), 0, inner], to_east,
            halo_sem.at[sems + 2], halo_sem.at[sems + 3], device_id=west, device_id_type=MESH)
        return a, b

    def mask_columns(sems):
        a = pltpu.make_async_remote_copy(
            ext_mask.at[TILES_X - 1, inner], mask_w,
            halo_sem.at[sems], halo_sem.at[sems + 1], device_id=east, device_id_type=MESH)
        b = pltpu.make_async_remote_copy(
            ext_mask.at[0, inner], mask_e,
            halo_sem.at[sems + 2], halo_sem.at[sems + 3], device_id=west, device_id_type=MESH)
        return a, b

    def merge(first, count, from_west, from_east):
        def body(i, carry):
            rows = pl.ds(pl.multiple_of(i * 8, 8), 8)
            there = pl.ds(pl.multiple_of(HALO + i * 8, 8), 8)
            for f in range(count):
                ext[first + f, TILES_X, there] = jnp.where(lane < 64, from_east[f, rows], from_west[f, rows])
            return carry
        lax.fori_loop(0, ROWS // 8, body, 0)

    north_gy = jnp.minimum(gy + 1, N_GY - 1)
    south_gy = jnp.maximum(gy - 1, 0)

    def rows_start(ref, sems):
        to_north = pltpu.make_async_remote_copy(
            ref(pl.ds(ROWS, HALO)), ref(pl.ds(0, HALO)),
            halo_sem.at[sems], halo_sem.at[sems + 1], device_id=(gx, north_gy), device_id_type=MESH)
        to_partner = pltpu.make_async_remote_copy(
            ref(pl.ds(ROWS, HALO)), ref(pl.ds(HALO + ROWS, HALO)),
            halo_sem.at[sems], halo_sem.at[sems + 3], device_id=(N_GX - 1 - gx, gy), device_id_type=MESH)
        to_south = pltpu.make_async_remote_copy(
            ref(pl.ds(HALO, HALO)), ref(pl.ds(HALO + ROWS, HALO)),
            halo_sem.at[sems + 2], halo_sem.at[sems + 3], device_id=(gx, south_gy), device_id_type=MESH)
        pl.when(jnp.logical_not(top))(to_north.start)
        pl.when(top)(to_partner.start)
        pl.when(gy > 0)(to_south.start)

    def rows_wait(ref, sems):
        wait_for(ref(pl.ds(HALO + ROWS, HALO)), halo_sem.at[sems + 3])
        wait_for(ref(pl.ds(ROWS, HALO)), halo_sem.at[sems])

        @pl.when(gy > 0)
        def _():
            wait_for(ref(pl.ds(0, HALO)), halo_sem.at[sems + 1])
            wait_for(ref(pl.ds(HALO, HALO)), halo_sem.at[sems + 2])

    def static_ref(rows):
        return ext.at[pl.ds(0, STATIC), :, rows]

    def mask_ref(rows):
        return ext_mask.at[:, rows]

    def force_ref(rows):
        return ext.at[pl.ds(FORCE_X, 2), :, rows]

    back_sub = 7 - lax.broadcasted_iota(jnp.int32, (8, 128), 0)
    back_lane = 127 - lane

    def turned(x):
        x = jnp.take_along_axis(x, back_lane, axis=1)
        return jnp.take_along_axis(x, back_sub, axis=0)

    def fold(get, put):
        def body(p, carry):
            here = pl.ds(pl.multiple_of(HALO + ROWS + p * 8, 8), 8)
            there = pl.ds(pl.multiple_of(HALO + ROWS + HALO - 8 - p * 8, 8), 8)
            for j in range(TILES_X // 2):
                a, b = get(j, here), get(TILES_X - 1 - j, there)
                put(j, here, turned(b))
                put(TILES_X - 1 - j, there, turned(a))
            return carry
        lax.fori_loop(0, HALO // 8, body, 0)

        def last(p, carry):
            here = pl.ds(pl.multiple_of(HALO + ROWS + p * 8, 8), 8)
            there = pl.ds(pl.multiple_of(HALO + ROWS + HALO - 8 - p * 8, 8), 8)
            a, b = get(TILES_X, here), get(TILES_X, there)
            put(TILES_X, here, turned(b))
            put(TILES_X, there, turned(a))
            return carry
        lax.fori_loop(0, HALO // 16, last, 0)

    def fold_field(f, sign):
        def put(j, rows, x):
            ext[f, j, rows] = x * sign
        fold(lambda j, rows: ext[f, j, rows], put)

    def fold_mask():
        def put(j, rows, x):
            ext_mask[j, rows] = x
        fold(lambda j, rows: ext_mask[j, rows], put)

    static_cols = columns(0, STATIC, side_w, side_e, 0)
    mask_cols = mask_columns(4)
    for copy in static_cols + mask_cols:
        copy.start()
    each_peer(send_forcing)
    for h in range(2):
        arrived[me * 2 + h] = outgoing[me * 2 + h]
    for copy in static_cols + mask_cols:
        copy.wait()
    merge(0, STATIC, side_w, side_e)

    def merge_mask(i, carry):
        rows = pl.ds(pl.multiple_of(i * 8, 8), 8)
        there = pl.ds(pl.multiple_of(HALO + i * 8, 8), 8)
        ext_mask[TILES_X, there] = jnp.where(lane < 64, mask_e[rows], mask_w[rows])
        return carry

    lax.fori_loop(0, ROWS // 8, merge_mask, 0)
    rows_start(static_ref, 8)
    rows_start(mask_ref, 12)

    @pl.when(gy == 0)
    def _():
        zero = jnp.zeros((8, 128), jnp.float32)
        for p in range(HALO // 8):
            rows = pl.ds(p * 8, 8)

            def clear(j, carry):
                for f in range(9):
                    ext[f, j, rows] = zero + 1.0 if f == MASS else zero
                ext_mask[j, rows] = jnp.zeros((8, 128), jnp.int32)
                return carry

            lax.fori_loop(0, CT, clear, 0)

    rows_wait(static_ref, 8)
    rows_wait(mask_ref, 12)

    @pl.when(top)
    def _():
        for f in range(STATIC):
            fold_field(f, -1.0 if f in (ZONAL, MERID) else 1.0)
        fold_mask()

    def arrange(r, carry):
        rows = pl.ds(r, 8, stride=STEP)
        for j in range(CT):
            share = ext_mask[j, rows].astype(jnp.float32)
            m = ext[MASS, j, rows]
            strong = ext[STRENGTH, j, rows]
            a = m + DRAG
            b = TURN * m
            scale = share / (a * a + b * b)
            const[KM, r, j] = m
            const[KA, r, j] = a * scale
            const[KB, r, j] = b * scale
            const[KS, r, j] = (0.0125 * KEEP) * strong
            state[CSTR, r + 1, j] = strong
            state[CU, r + 1, j] = ext[ZONAL, j, rows] * share
            state[CV, r + 1, j] = ext[MERID, j, rows] * share
            both = 0.25 * (ext[SUM, j, rows] + strong)
            apart = 0.25 * ext[DIFF, j, rows]
            state[CXX, r + 1, j] = both + apart
            state[CYY, r + 1, j] = both - apart
            state[CSH, r + 1, j] = 0.5 * ext[SHEAR, j, rows]
        return carry

    lax.fori_loop(0, STEP, arrange, 0)

    def ghosts(names):
        for c in names:
            for j in range(CT):
                state[c, 0, j] = pltpu.roll(state[c, STEP, j], 1, 0)
                state[c, STEP + 1, j] = pltpu.roll(state[c, 1, j], 7, 0)

    ghosts((CU, CV, CSTR))

    wait_for(arrived.at[pl.ds(0, 2 * N_DEV - 2)], a2a_sem.at[1])
    wait_for(outgoing.at[pl.ds(0, 2 * N_DEV - 2)], a2a_sem.at[0])

    def forces(i, carry):
        rows = pl.ds(pl.multiple_of(HALO + i * 8, 8), 8)
        for j in range(TILES_X):
            tile = arrived[recv_slot[i * TILES_X + j]]
            m = TILT * ext[MASS, j, rows]
            ext[FORCE_X, j, rows] = tile[0] + m * tile[2]
            ext[FORCE_Y, j, rows] = tile[1] + m * tile[3]
        return carry

    lax.fori_loop(0, ROWS // 8, forces, 0)
    force_cols = columns(FORCE_X, 2, side_fw, side_fe, 16)
    for copy in force_cols:
        copy.start()
    for copy in force_cols:
        copy.wait()
    merge(FORCE_X, 2, side_fw, side_fe)
    rows_start(force_ref, 20)
    rows_wait(force_ref, 20)

    @pl.when(top)
    def _():
        fold_field(FORCE_X, -1.0)
        fold_field(FORCE_Y, -1.0)

    def arrange_forces(r, carry):
        rows = pl.ds(r, 8, stride=STEP)
        left, right = left_right([state[CSTR, r + 1, j] for j in range(CT)], lane)
        for j in range(CT):
            const[KFX, r, j] = ext[FORCE_X, j, rows] - 0.25 * (right[j] - left[j])
            const[KFY, r, j] = ext[FORCE_Y, j, rows] - 0.25 * (state[CSTR, r + 2, j] - state[CSTR, r, j])
        return carry

    lax.fori_loop(0, STEP, arrange_forces, 0)

    def stresses(r, carry):
        u_left, u_right = left_right([state[CU, r + 1, j] for j in range(CT)], lane)
        v_left, v_right = left_right([state[CV, r + 1, j] for j in range(CT)], lane)
        for j in range(CT):
            ux = u_right[j] - u_left[j]
            vx = v_right[j] - v_left[j]
            uy = state[CU, r + 2, j] - state[CU, r, j]
            vy = state[CV, r + 2, j] - state[CV, r, j]
            div = ux + vy
            ten = ux - vy
            shr = uy + vx
            div2 = div + div
            w = const[KS, r, j] * lax.rsqrt(div2 * div2 + ten * ten + shr * shr + 16.0)
            div4 = div2 + div2
            state[CXX, r + 1, j] = KEEP * state[CXX, r + 1, j] + w * (div4 + ten)
            state[CYY, r + 1, j] = KEEP * state[CYY, r + 1, j] + w * (div4 - ten)
            state[CSH, r + 1, j] = KEEP * state[CSH, r + 1, j] + w * shr
        return carry

    def momentum(r, carry):
        xx_left, xx_right = left_right([state[CXX, r + 1, j] for j in range(CT)], lane)
        sh_left, sh_right = left_right([state[CSH, r + 1, j] for j in range(CT)], lane)
        for j in range(CT):
            px = (xx_right[j] - xx_left[j]) + (state[CSH, r + 2, j] - state[CSH, r, j])
            py = (sh_right[j] - sh_left[j]) + (state[CYY, r + 2, j] - state[CYY, r, j])
            m = const[KM, r, j]
            rx = m * state[CU, r + 1, j] + (px + const[KFX, r, j])
            ry = m * state[CV, r + 1, j] + (py + const[KFY, r, j])
            a = const[KA, r, j]
            b = const[KB, r, j]
            state[CU, r + 1, j] = a * rx + b * ry
            state[CV, r + 1, j] = a * ry - b * rx
        return carry

    def subcycle(t, carry):
        lax.fori_loop(0, STEP, stresses, 0)
        ghosts((CYY, CSH))
        lax.fori_loop(0, STEP, momentum, 0)
        ghosts((CU, CV))
        return carry

    lax.fori_loop(0, ITERS, subcycle, 0)

    def restore(r, carry):
        rows = pl.ds(r, 8, stride=STEP)
        for j in range(TILES_X):
            ext[ZONAL, j, rows] = state[CU, r + 1, j]
            ext[MERID, j, rows] = state[CV, r + 1, j]
            xx = state[CXX, r + 1, j]
            yy = state[CYY, r + 1, j]
            ext[SUM, j, rows] = 2.0 * (xx + yy) - state[CSTR, r + 1, j]
            ext[DIFF, j, rows] = 2.0 * (xx - yy)
            ext[SHEAR, j, rows] = 2.0 * state[CSH, r + 1, j]
        return carry

    lax.fori_loop(0, STEP, restore, 0)
    for j in range(TILES_X):
        cols = pl.ds(j * 128, 128)
        pltpu.make_async_copy(ext.at[pl.ds(SUM, 3), j, inner], out_stress.at[:, :, cols], in_sem.at[1]).start()

    def to_tiles(i, carry):
        rows = pl.ds(pl.multiple_of(HALO + i * 8, 8), 8)
        for j in range(TILES_X):
            tiles[i * TILES_X + j, 0] = ext[ZONAL, j, rows]
            tiles[i * TILES_X + j, 1] = ext[MERID, j, rows]
        return carry

    lax.fori_loop(0, ROWS // 8, to_tiles, 0)

    def pack_back(i, carry):
        for h in range(8):
            returning[i * 8 + h] = tiles[back_tile[i * 8 + h]]
        return carry

    lax.fori_loop(0, 2 * N_DEV // 8, pack_back, 0)

    def send_back(a, b):
        pltpu.make_async_remote_copy(
            returning.at[pl.ds((a * N_GY + b) * 2, 2)], arrived_back.at[pl.ds(me * 2, 2)],
            a2a_sem.at[2], a2a_sem.at[3], device_id=(a, b), device_id_type=MESH,
        ).start()

    each_peer(send_back)
    for h in range(2):
        arrived_back[me * 2 + h] = returning[me * 2 + h]
    wait_for(arrived_back.at[pl.ds(0, 2 * N_DEV - 2)], a2a_sem.at[3])
    wait_for(arrived_back.at[pl.ds(0, 2 * N_DEV - 2)], a2a_sem.at[2])

    def unpack(i, carry):
        for h in range(8):
            out_velocity[i * 8 + h] = arrived_back[back_slot[i * 8 + h]]
        return carry

    lax.fori_loop(0, N_DEV // 8, unpack, 0)
    wait_for(ext.at[pl.ds(SUM, 3), pl.ds(0, TILES_X), inner], in_sem.at[1])


def tables(route):
    me = lax.axis_index("gx") * N_GY + lax.axis_index("gy")
    table = route.reshape(N_DEV, N_DEV)
    number = jnp.arange(N_DEV, dtype=jnp.int32)
    mine = lax.dynamic_index_in_dim(table, me, 0, keepdims=False) // N_DEV
    hits = mine[None, :] == number[:, None]
    first = jnp.min(jnp.where(hits, number[None, :], N_DEV - 1), axis=1)
    second = jnp.max(jnp.where(hits, number[None, :], 0), axis=1)
    send_tile = jnp.stack([first, second], axis=1).reshape(-1)
    rank = jnp.sum(jnp.where(hits & (second[:, None] == number[None, :]), 1, 0), axis=0)
    back_slot = mine * 2 + rank
    here = table // N_DEV == me
    early = jnp.min(jnp.where(here, number[None, :], N_DEV), axis=1)
    late = jnp.max(jnp.where(here, number[None, :], -1), axis=1)
    inside = table % N_DEV
    k_early = jnp.sum(jnp.where(number[None, :] == early[:, None], inside + 1, 0), axis=1) - 1
    k_late = jnp.sum(jnp.where(number[None, :] == late[:, None], inside + 1, 0), axis=1) - 1
    recv_slot = jnp.sum(
        jnp.where(k_early[None, :] == number[:, None], 2 * number[None, :], 0)
        + jnp.where(k_late[None, :] == number[:, None], 2 * number[None, :] + 1, 0), axis=1)
    back_tile = jnp.maximum(jnp.stack([k_early, k_late], axis=1).reshape(-1), 0)
    return send_tile, recv_slot, back_tile, back_slot


def local(ocean_forcing, route, land_mask, mass, strength, velocity_start, stress_start):
    send_tile, recv_slot, back_tile, back_slot = tables(route)
    f32 = jnp.float32
    smem = pl.BlockSpec(memory_space=pltpu.SMEM)
    hbm = pl.BlockSpec(memory_space=pl.ANY)
    return pl.pallas_call(
        kernel,
        out_shape=(
            jax.ShapeDtypeStruct((N_DEV, 2, 8, 128), f32),
            jax.ShapeDtypeStruct((3, ROWS, TILES_X * 128), f32),
        ),
        in_specs=[smem] * 4 + [hbm] * 6,
        out_specs=(pl.BlockSpec(memory_space=pltpu.VMEM), hbm),
        scratch_shapes=[
            pltpu.VMEM((N_DEV, 2, 8, 128), f32),
            pltpu.VMEM((2 * N_DEV, 2, 8, 128), f32),
            pltpu.VMEM((2 * N_DEV, 2, 8, 128), f32),
            pltpu.VMEM((N_DEV, 4, 8, 128), f32),
            pltpu.VMEM((2 * N_DEV, 4, 8, 128), f32),
            pltpu.VMEM((2 * N_DEV, 4, 8, 128), f32),
            pltpu.VMEM((9, CT, EXT, 128), f32),
            pltpu.VMEM((CT, EXT, 128), jnp.int32),
            pltpu.VMEM((STATIC, ROWS, 128), f32),
            pltpu.VMEM((STATIC, ROWS, 128), f32),
            pltpu.VMEM((ROWS, 128), jnp.int32),
            pltpu.VMEM((ROWS, 128), jnp.int32),
            pltpu.VMEM((2, ROWS, 128), f32),
            pltpu.VMEM((2, ROWS, 128), f32),
            pltpu.VMEM((6, STEP + 2, CT, 8, 128), f32),
            pltpu.VMEM((6, STEP, CT, 8, 128), f32),
            pltpu.SemaphoreType.DMA((3,)),
            pltpu.SemaphoreType.DMA((4,)),
            pltpu.SemaphoreType.DMA((24,)),
        ],
        compiler_params=pltpu.CompilerParams(
            collective_id=0, has_side_effects=True, vmem_limit_bytes=56 * 1024 * 1024),
    )(send_tile, recv_slot, back_tile, back_slot, ocean_forcing, land_mask, mass, strength, velocity_start, stress_start)


def solution(mesh):
    placed = (
        P(("gx", "gy"), None, None, None),
        P(),
        P("gy", "gx"),
        P("gy", "gx"),
        P("gy", "gx"),
        P(None, "gy", "gx"),
        P(None, "gy", "gx"),
    )
    return jax.shard_map(
        local,
        mesh=mesh,
        in_specs=placed,
        out_specs=(P(("gx", "gy"), None, None, None), P(None, "gy", "gx")),
        check_vma=False,
    )
```

```python
import functools

import jax
import jax.numpy as jnp
from jax import lax
from jax.experimental import pallas as pl
from jax.experimental.pallas import tpu as pltpu
from jax.sharding import PartitionSpec as P

MESH = pl.DeviceIdType.MESH
ITERS = 16
RELAX = 0.1
DRAG = 0.5
TURN = 0.3
TILT = 0.05
KEEP = 1.0 / (1.0 + RELAX)

N_GX = 8
N_GY = 16
N_DEV = 128
LEGS = 2
HALO = 2 * ITERS // LEGS
SIDE = 2 * ITERS
ROWS = 128
EXT = ROWS + 2 * HALO
STEP = EXT // 8
TILES_X = 8
CT = TILES_X + 1
UNROLL = 2

MASS, STRENGTH, ZONAL, MERID, SUM, DIFF, SHEAR, SHARE, FORCE_X, FORCE_Y = range(10)
STATIC = 8
FIELDS = 10
FIRST, SECOND, BACK_SLOT, RECV_SLOT, EARLY, LATE = range(6)


def peers():
    order = []
    for n in range(32):
        j = (n * 13) % 32
        dx, dy, dc = j // 8, (j // 2) % 4, j % 2
        off = (n + n // 4 + 3 * dx + dy) % 4 if (dx, dy, dc) != (0, 0, 0) else 0
        order.append((dx, dy, dc, off))
    return order


def each_peer(visit, first=0, last=4):
    gx = lax.axis_index("gx")
    gy = lax.axis_index("gy")
    z, x_lo = gx % 4, gx // 4
    x_hi, y, core = gy // 8, (gy // 2) % 4, gy % 2
    x = x_hi * 2 + x_lo
    xs = [(x + d) % 4 for d in range(4)]
    part_gx = [(v % 2) * 4 for v in xs]
    part_gy = [(v // 2) * 8 for v in xs]
    ys = [((y + d) % 4) * 2 for d in range(4)]
    cores = [core, 1 - core]
    zs = tuple((z + d + first) % 4 for d in range(4))

    def turn(q, zs):
        for dx, dy, dc, off in peers():
            there = (part_gx[dx] + zs[off], part_gy[dx] + ys[dy] + cores[dc])
            if (dx, dy, dc) == (0, 0, 0):
                pl.when(q > 0)(functools.partial(visit, *there))
            else:
                visit(*there)
        return zs[1:] + zs[:1]

    lax.fori_loop(first, last, turn, zs)


def wait_for(ref, sem):
    pltpu.make_async_copy(ref, ref, sem).wait()


def aligned(start, size=8):
    return pl.ds(pl.multiple_of(start, 8), size)


def left_right(row, lane):
    n = len(row)
    left = [pltpu.roll(jnp.where(lane == 127, row[j - 1], row[j]), 1, 1) for j in range(n)]
    right = [pltpu.roll(jnp.where(lane == 0, row[(j + 1) % n], row[j]), 127, 1) for j in range(n)]
    return left, right


def fill_table(route, table, me):
    shape = (N_DEV, N_DEV)
    sub = lax.broadcasted_iota(jnp.int32, shape, 0)
    lane = lax.broadcasted_iota(jnp.int32, shape, 1)
    diagonal = sub == lane

    def to_column(row):
        return jnp.sum(jnp.where(diagonal, row, 0), axis=1, keepdims=True)

    def to_row(column):
        return jnp.sum(jnp.where(diagonal, column, 0), axis=0, keepdims=True)

    mine = jnp.right_shift(route[pl.ds(me, 1), :], 7)
    column = to_column(mine)
    hit = column == lane
    table[pl.ds(FIRST, 1), :] = jnp.min(jnp.where(hit, sub, N_DEV - 1), axis=0, keepdims=True)
    table[pl.ds(SECOND, 1), :] = jnp.max(jnp.where(hit, sub, 0), axis=0, keepdims=True)
    rank = jnp.max(jnp.where((column == mine) & (sub < lane), 1, 0), axis=0, keepdims=True)
    table[pl.ds(BACK_SLOT, 1), :] = mine * 2 + rank
    ids = route[...]
    here = jnp.right_shift(ids, 7) == me
    inside = jnp.bitwise_and(ids, N_DEV - 1)
    first = jnp.min(jnp.where(here, lane, N_DEV), axis=1, keepdims=True)
    second = jnp.max(jnp.where(here, lane, -1), axis=1, keepdims=True)
    early = jnp.sum(jnp.where(lane == first, inside + 1, 0), axis=1, keepdims=True) - 1
    late = jnp.sum(jnp.where(lane == second, inside + 1, 0), axis=1, keepdims=True) - 1
    slot = jnp.where(late == lane, 2 * sub + 1, jnp.where(early == lane, 2 * sub, 0))
    table[pl.ds(RECV_SLOT, 1), :] = jnp.max(slot, axis=0, keepdims=True)
    table[pl.ds(EARLY, 1), :] = to_row(jnp.maximum(early, 0))
    table[pl.ds(LATE, 1), :] = to_row(jnp.maximum(late, 0))
    table[pl.ds(6, 2), :] = jnp.zeros((2, N_DEV), jnp.int32)


def kernel(
    route, ocean, mask, mass, strength, velocity, stress,
    out_velocity, out_stress,
    routes, table, place, oc, outgoing, arrived, ext, ext_mask,
    to_east, to_west, from_west, from_east, force_to_east, force_to_west, force_from_west, force_from_east,
    nat, from_south, from_north, final, tiles, returning, arrived_back,
    cu, cv, cxx, cyy, csh, cstr, ks, km, kfx, kfy, ka, kb,
    in_sem, a2a_sem, halo_sem,
):
    gx = lax.axis_index("gx")
    gy = lax.axis_index("gy")
    me = gx * N_GY + gy
    top = gy == N_GY - 1
    inner = pl.ds(HALO, ROWS)
    lane = lax.broadcasted_iota(jnp.int32, (8, 128), 1)

    pltpu.make_async_copy(route, routes, in_sem.at[3]).start()
    pltpu.make_async_copy(ocean, oc, in_sem.at[0]).start()
    for j in range(TILES_X):
        cols = pl.ds(j * 128, 128)
        pltpu.make_async_copy(mass.at[:, cols], ext.at[MASS, j, inner], in_sem.at[1]).start()
        pltpu.make_async_copy(strength.at[:, cols], ext.at[STRENGTH, j, inner], in_sem.at[1]).start()
        pltpu.make_async_copy(velocity.at[:, :, cols], ext.at[pl.ds(ZONAL, 2), j, inner], in_sem.at[1]).start()
        pltpu.make_async_copy(stress.at[:, :, cols], ext.at[pl.ds(SUM, 3), j, inner], in_sem.at[1]).start()
        pltpu.make_async_copy(mask.at[:, cols], ext_mask.at[j], in_sem.at[2]).start()

    barrier = pltpu.get_barrier_semaphore()

    def greet(a, b):
        pl.semaphore_signal(barrier, inc=1, device_id=(a, b), device_id_type=MESH)

    each_peer(greet)

    wait_for(routes, in_sem.at[3])
    fill_table(routes, table, me)
    to_place = pltpu.make_async_copy(table, place, in_sem.at[4])
    to_place.start()

    wait_for(ext_mask, in_sem.at[2])

    def shares(i, carry):
        for j in range(TILES_X):
            ext[SHARE, j, aligned(HALO + i * 8)] = ext_mask[j, aligned(i * 8)].astype(jnp.float32)
        return carry

    lax.fori_loop(0, ROWS // 8, shares, 0)
    wait_for(ext.at[pl.ds(0, STATIC - 1), pl.ds(0, TILES_X), inner], in_sem.at[1])

    def gather_columns(first, count, east_out, west_out):
        def body(i, carry):
            rows = aligned(HALO + i * 8)
            for g in range((count + 3) // 4):
                e = w = None
                for q in range(min(4, count - 4 * g)):
                    f = first + 4 * g + q
                    a = pltpu.roll(ext[f, TILES_X - 1, rows], (SIDE * (q + 1)) % 128, 1)
                    b = ext[f, 0, rows]
                    if q:
                        b = pltpu.roll(b, SIDE * q, 1)
                    e = a if q == 0 else jnp.where(lane < SIDE * q, e, a)
                    w = b if q == 0 else jnp.where(lane < SIDE * q, w, b)
                east_out[g, aligned(i * 8)] = e
                west_out[g, aligned(i * 8)] = w
            return carry

        lax.fori_loop(0, ROWS // 8, body, 0)

    def spread_columns(first, count, west_in, east_in):
        def body(i, carry):
            rows = aligned(HALO + i * 8)
            for g in range((count + 3) // 4):
                e = east_in[g, aligned(i * 8)]
                w = west_in[g, aligned(i * 8)]
                for q in range(min(4, count - 4 * g)):
                    right = pltpu.roll(e, 128 - SIDE * q, 1) if q else e
                    left = pltpu.roll(w, 128 - SIDE * (q + 1), 1) if q < 3 else w
                    ext[first + 4 * g + q, TILES_X, rows] = jnp.where(lane < 64, right, left)
            return carry

        lax.fori_loop(0, ROWS // 8, body, 0)

    def columns(east_out, west_out, west_in, east_in, sems):
        a = pltpu.make_async_remote_copy(
            east_out, west_in, halo_sem.at[sems], halo_sem.at[sems + 1],
            device_id=((gx + 1) % N_GX, gy), device_id_type=MESH)
        b = pltpu.make_async_remote_copy(
            west_out, east_in, halo_sem.at[sems + 2], halo_sem.at[sems + 3],
            device_id=((gx + N_GX - 1) % N_GX, gy), device_id_type=MESH)
        return a, b

    north_gy = jnp.minimum(gy + 1, N_GY - 1)
    south_gy = jnp.maximum(gy - 1, 0)

    def rows_start(upper, lower, south, north, sems):
        to_north = pltpu.make_async_remote_copy(
            upper, south, halo_sem.at[sems], halo_sem.at[sems + 1],
            device_id=(gx, north_gy), device_id_type=MESH)
        to_partner = pltpu.make_async_remote_copy(
            upper, north, halo_sem.at[sems], halo_sem.at[sems + 3],
            device_id=(N_GX - 1 - gx, gy), device_id_type=MESH)
        to_south = pltpu.make_async_remote_copy(
            lower, north, halo_sem.at[sems + 2], halo_sem.at[sems + 3],
            device_id=(gx, south_gy), device_id_type=MESH)
        pl.when(jnp.logical_not(top))(to_north.start)
        pl.when(top)(to_partner.start)
        pl.when(gy > 0)(to_south.start)

    def rows_wait(upper, lower, south, north, sems):
        wait_for(north, halo_sem.at[sems + 3])
        wait_for(upper, halo_sem.at[sems])

        @pl.when(gy > 0)
        def _():
            wait_for(south, halo_sem.at[sems + 1])
            wait_for(lower, halo_sem.at[sems + 2])

    def strips(first, count):
        return tuple(
            ext.at[pl.ds(first, count), :, pl.ds(at, HALO)] for at in (ROWS, HALO, 0, HALO + ROWS))

    back_sub = 7 - lax.broadcasted_iota(jnp.int32, (8, 128), 0)
    back_lane = 127 - lane

    def turned(x):
        x = jnp.take_along_axis(x, back_lane, axis=1)
        return jnp.take_along_axis(x, back_sub, axis=0)

    def fold(ref, f, base, sign):
        for p in range(HALO // 16):
            here = pl.ds(base + p * 8, 8)
            there = pl.ds(base + HALO - 8 - p * 8, 8)

            def body(j, carry):
                a, b = ref[f, j, here], ref[f, TILES_X - 1 - j, there]
                ref[f, j, here] = turned(b) * sign
                ref[f, TILES_X - 1 - j, there] = turned(a) * sign
                return carry

            lax.fori_loop(0, TILES_X, body, 0)
            a, b = ref[f, TILES_X, here], ref[f, TILES_X, there]
            ref[f, TILES_X, here] = turned(b) * sign
            ref[f, TILES_X, there] = turned(a) * sign

    static_cols = columns(to_east, to_west, from_west, from_east, 0)
    force_cols = columns(force_to_east, force_to_west, force_from_west, force_from_east, 4)
    static_rows = strips(0, STATIC)
    force_rows = strips(FORCE_X, 2)

    gather_columns(0, STATIC, to_east, to_west)

    to_place.wait()
    wait_for(oc, in_sem.at[0])

    def pack(i, carry):
        for h in range(4):
            outgoing[i * 8 + 2 * h] = oc[place[FIRST, i * 4 + h]]
            outgoing[i * 8 + 2 * h + 1] = oc[place[SECOND, i * 4 + h]]
        return carry

    lax.fori_loop(0, N_DEV // 4, pack, 0)
    pl.semaphore_wait(barrier, N_DEV - 1)

    def send_forcing(a, b):
        pltpu.make_async_remote_copy(
            outgoing.at[pl.ds((a * N_GY + b) * 2, 2)], arrived.at[pl.ds(me * 2, 2)],
            a2a_sem.at[0], a2a_sem.at[1], device_id=(a, b), device_id_type=MESH,
        ).start()

    for copy in static_cols:
        copy.start()
    each_peer(send_forcing, 0, 1)
    for copy in static_cols:
        copy.wait()
    spread_columns(0, STATIC, from_west, from_east)
    rows_start(*static_rows, 8)
    each_peer(send_forcing, 1, 4)
    for h in range(2):
        arrived[me * 2 + h] = outgoing[me * 2 + h]

    @pl.when(gy == 0)
    def _():
        zero = jnp.zeros((8, 128), jnp.float32)

        def clear(j, carry):
            for p in range(HALO // 8):
                for f in range(FIELDS):
                    ext[f, j, pl.ds(p * 8, 8)] = zero + 1.0 if f == MASS else zero
            return carry

        lax.fori_loop(0, CT, clear, 0)

    rows_wait(*static_rows, 8)

    @pl.when(top)
    def _():
        for f in range(STATIC):
            fold(ext, f, HALO + ROWS, -1.0 if f in (ZONAL, MERID) else 1.0)

    def arrange(r, carry):
        rows = pl.ds(r, 8, stride=STEP)
        for j in range(CT):
            share = ext[SHARE, j, rows]
            m = ext[MASS, j, rows]
            strong = ext[STRENGTH, j, rows]
            a = m + DRAG
            b = TURN * m
            scale = share / (a * a + b * b)
            km[r, j] = m
            ka[r, j] = a * scale
            kb[r, j] = b * scale
            ks[r, j] = (0.0125 * KEEP) * strong
            cstr[r + 1, j] = strong
            cu[r + 1, j] = ext[ZONAL, j, rows] * share
            cv[r + 1, j] = ext[MERID, j, rows] * share
            both = 0.25 * (ext[SUM, j, rows] + strong)
            apart = 0.25 * ext[DIFF, j, rows]
            cxx[r + 1, j] = both + apart
            cyy[r + 1, j] = both - apart
            csh[r + 1, j] = 0.5 * ext[SHEAR, j, rows]
        return carry

    lax.fori_loop(0, STEP, arrange, 0)

    def ghosts(*refs):
        for ref in refs:
            for j in range(CT):
                ref[0, j] = pltpu.roll(ref[STEP, j], 1, 0)
                ref[STEP + 1, j] = pltpu.roll(ref[1, j], 7, 0)

    ghosts(cu, cv, cstr)

    wait_for(arrived.at[pl.ds(0, 2 * N_DEV - 2)], a2a_sem.at[1])
    wait_for(outgoing.at[pl.ds(0, 2 * N_DEV - 2)], a2a_sem.at[0])

    def forces(i, carry):
        rows = aligned(HALO + i * 8)
        for j in range(TILES_X):
            tile = arrived[place[RECV_SLOT, i * TILES_X + j]]
            m = TILT * ext[MASS, j, rows]
            ext[FORCE_X, j, rows] = tile[0] + m * tile[2]
            ext[FORCE_Y, j, rows] = tile[1] + m * tile[3]
        return carry

    lax.fori_loop(0, ROWS // 8, forces, 0)
    gather_columns(FORCE_X, 2, force_to_east, force_to_west)
    for copy in force_cols:
        copy.start()
    for copy in force_cols:
        copy.wait()
    spread_columns(FORCE_X, 2, force_from_west, force_from_east)
    rows_start(*force_rows, 12)
    rows_wait(*force_rows, 12)

    @pl.when(top)
    def _():
        fold(ext, FORCE_X, HALO + ROWS, -1.0)
        fold(ext, FORCE_Y, HALO + ROWS, -1.0)

    def arrange_forces(r, carry):
        rows = pl.ds(r, 8, stride=STEP)
        left, right = left_right([cstr[r + 1, j] for j in range(CT)], lane)
        for j in range(CT):
            kfx[r, j] = ext[FORCE_X, j, rows] - 0.25 * (right[j] - left[j])
            kfy[r, j] = ext[FORCE_Y, j, rows] - 0.25 * (cstr[r + 2, j] - cstr[r, j])
        return carry

    lax.fori_loop(0, STEP, arrange_forces, 0)

    def stresses(i, carry):
        for r in [i * UNROLL + h for h in range(UNROLL)]:
            u_left, u_right = left_right([cu[r + 1, j] for j in range(CT)], lane)
            v_left, v_right = left_right([cv[r + 1, j] for j in range(CT)], lane)
            for j in range(CT):
                ux = u_right[j] - u_left[j]
                vx = v_right[j] - v_left[j]
                uy = cu[r + 2, j] - cu[r, j]
                vy = cv[r + 2, j] - cv[r, j]
                div = ux + vy
                ten = ux - vy
                shr = uy + vx
                div2 = div + div
                w = ks[r, j] * lax.rsqrt(div2 * div2 + ten * ten + shr * shr + 16.0)
                div4 = div2 + div2
                cxx[r + 1, j] = KEEP * cxx[r + 1, j] + w * (div4 + ten)
                cyy[r + 1, j] = KEEP * cyy[r + 1, j] + w * (div4 - ten)
                csh[r + 1, j] = KEEP * csh[r + 1, j] + w * shr
        return carry

    def momentum(i, carry):
        for r in [i * UNROLL + h for h in range(UNROLL)]:
            xx_left, xx_right = left_right([cxx[r + 1, j] for j in range(CT)], lane)
            sh_left, sh_right = left_right([csh[r + 1, j] for j in range(CT)], lane)
            for j in range(CT):
                px = (xx_right[j] - xx_left[j]) + (csh[r + 2, j] - csh[r, j])
                py = (sh_right[j] - sh_left[j]) + (cyy[r + 2, j] - cyy[r, j])
                m = km[r, j]
                rx = m * cu[r + 1, j] + (px + kfx[r, j])
                ry = m * cv[r + 1, j] + (py + kfy[r, j])
                a = ka[r, j]
                b = kb[r, j]
                cu[r + 1, j] = a * rx + b * ry
                cv[r + 1, j] = a * ry - b * rx
        return carry

    def subcycle(t, carry):
        lax.fori_loop(0, STEP // UNROLL, stresses, 0)
        ghosts(cyy, csh)
        lax.fori_loop(0, STEP // UNROLL, momentum, 0)
        ghosts(cu, cv)
        return carry

    carried = (cu, cv, cxx, cyy, csh)

    def to_grid_order(r, carry):
        for f, ref in enumerate(carried):
            for j in range(CT):
                nat[f, j, pl.ds(r, 8, stride=STEP)] = ref[r + 1, j]
        return carry

    def from_grid_order(r, carry):
        for f, ref in enumerate(carried):
            for j in range(CT):
                ref[r + 1, j] = nat[f, j, pl.ds(r, 8, stride=STEP)]
        return carry

    lax.fori_loop(0, ITERS // LEGS, subcycle, 0)
    lax.fori_loop(0, STEP, to_grid_order, 0)
    state_rows = (nat.at[:, :, pl.ds(ROWS, HALO)], nat.at[:, :, pl.ds(HALO, HALO)], from_south, from_north)
    rows_start(*state_rows, 16)
    rows_wait(*state_rows, 16)

    @pl.when(top)
    def _():
        for f in range(5):
            fold(from_north, f, 0, -1.0 if f < 2 else 1.0)

    def take_rows(j, carry):
        for f in range(5):
            for p in range(HALO // 8):
                nat[f, j, pl.ds(HALO + ROWS + p * 8, 8)] = from_north[f, j, pl.ds(p * 8, 8)]
        return carry

    def take_south_rows(j, carry):
        for f in range(5):
            for p in range(HALO // 8):
                nat[f, j, pl.ds(p * 8, 8)] = from_south[f, j, pl.ds(p * 8, 8)]
        return carry

    lax.fori_loop(0, CT, take_rows, 0)

    @pl.when(gy > 0)
    def _():
        lax.fori_loop(0, CT, take_south_rows, 0)

    lax.fori_loop(0, STEP, from_grid_order, 0)
    ghosts(cu, cv)
    lax.fori_loop(0, ITERS // LEGS, subcycle, 0)
    lax.fori_loop(0, STEP, to_grid_order, 0)

    def to_tiles(i, carry):
        rows = aligned(HALO + i * 8)
        for j in range(TILES_X):
            tiles[i * TILES_X + j, 0] = nat[0, j, rows]
            tiles[i * TILES_X + j, 1] = nat[1, j, rows]
        return carry

    lax.fori_loop(0, ROWS // 8, to_tiles, 0)

    def pack_back(i, carry):
        for h in range(4):
            returning[i * 8 + 2 * h] = tiles[place[EARLY, i * 4 + h]]
            returning[i * 8 + 2 * h + 1] = tiles[place[LATE, i * 4 + h]]
        return carry

    lax.fori_loop(0, N_DEV // 4, pack_back, 0)

    def send_back(a, b):
        pltpu.make_async_remote_copy(
            returning.at[pl.ds((a * N_GY + b) * 2, 2)], arrived_back.at[pl.ds(me * 2, 2)],
            a2a_sem.at[2], a2a_sem.at[3], device_id=(a, b), device_id_type=MESH,
        ).start()

    each_peer(send_back)
    for h in range(2):
        arrived_back[me * 2 + h] = returning[me * 2 + h]

    def finish(i, carry):
        rows = aligned(HALO + i * 8)
        for j in range(TILES_X):
            xx = nat[2, j, rows]
            yy = nat[3, j, rows]
            final[0, j, aligned(i * 8)] = 2.0 * (xx + yy) - ext[STRENGTH, j, rows]
            final[1, j, aligned(i * 8)] = 2.0 * (xx - yy)
            final[2, j, aligned(i * 8)] = 2.0 * nat[4, j, rows]
        return carry

    lax.fori_loop(0, ROWS // 8, finish, 0)
    for j in range(TILES_X):
        pltpu.make_async_copy(final.at[:, j], out_stress.at[:, :, pl.ds(j * 128, 128)], in_sem.at[1]).start()

    wait_for(arrived_back.at[pl.ds(0, 2 * N_DEV - 2)], a2a_sem.at[3])
    wait_for(returning.at[pl.ds(0, 2 * N_DEV - 2)], a2a_sem.at[2])

    def unpack(i, carry):
        for h in range(8):
            out_velocity[i * 8 + h] = arrived_back[place[BACK_SLOT, i * 8 + h]]
        return carry

    lax.fori_loop(0, N_DEV // 8, unpack, 0)
    wait_for(final, in_sem.at[1])


def local(ocean_forcing, route, land_mask, mass, strength, velocity_start, stress_start):
    f32, i32 = jnp.float32, jnp.int32
    hbm = pl.BlockSpec(memory_space=pl.ANY)
    ghosted = pltpu.VMEM((STEP + 2, CT, 8, 128), f32)
    plain = pltpu.VMEM((STEP, CT, 8, 128), f32)
    side = pltpu.VMEM((STATIC // 4, ROWS, 128), f32)
    force_side = pltpu.VMEM((1, ROWS, 128), f32)
    strip = pltpu.VMEM((5, CT, HALO, 128), f32)
    return pl.pallas_call(
        kernel,
        out_shape=(
            jax.ShapeDtypeStruct((N_DEV, 2, 8, 128), f32),
            jax.ShapeDtypeStruct((3, ROWS, TILES_X * 128), f32),
        ),
        in_specs=[hbm] * 7,
        out_specs=(pl.BlockSpec(memory_space=pltpu.VMEM), hbm),
        scratch_shapes=[
            pltpu.VMEM((N_DEV, N_DEV), i32),
            pltpu.VMEM((8, N_DEV), i32),
            pltpu.SMEM((8, N_DEV), i32),
            pltpu.VMEM((N_DEV, 4, 8, 128), f32),
            pltpu.VMEM((2 * N_DEV, 4, 8, 128), f32),
            pltpu.VMEM((2 * N_DEV, 4, 8, 128), f32),
            pltpu.VMEM((FIELDS, CT, EXT, 128), f32),
            pltpu.VMEM((TILES_X, ROWS, 128), i32),
            side, side, side, side,
            force_side, force_side, force_side, force_side,
            pltpu.VMEM((5, CT, EXT, 128), f32),
            strip, strip,
            pltpu.VMEM((3, TILES_X, ROWS, 128), f32),
            pltpu.VMEM((N_DEV, 2, 8, 128), f32),
            pltpu.VMEM((2 * N_DEV, 2, 8, 128), f32),
            pltpu.VMEM((2 * N_DEV, 2, 8, 128), f32),
            ghosted, ghosted, ghosted, ghosted, ghosted, ghosted,
            plain, plain, plain, plain, plain, plain,
            pltpu.SemaphoreType.DMA((5,)),
            pltpu.SemaphoreType.DMA((4,)),
            pltpu.SemaphoreType.DMA((20,)),
        ],
        compiler_params=pltpu.CompilerParams(
            collective_id=0, has_side_effects=True, vmem_limit_bytes=56 * 1024 * 1024),
    )(route.reshape(N_DEV, N_DEV), ocean_forcing, land_mask, mass, strength, velocity_start, stress_start)


def solution(mesh):
    placed = (
        P(("gx", "gy"), None, None, None),
        P(),
        P("gy", "gx"),
        P("gy", "gx"),
        P("gy", "gx"),
        P(None, "gy", "gx"),
        P(None, "gy", "gx"),
    )
    return jax.shard_map(
        local,
        mesh=mesh,
        in_specs=placed,
        out_specs=(P(("gx", "gy"), None, None, None), P(None, "gy", "gx")),
        check_vma=False,
    )
```

```python
import functools

import jax
import jax.numpy as jnp
from jax import lax
from jax.experimental import pallas as pl
from jax.experimental.pallas import tpu as pltpu
from jax.sharding import PartitionSpec as P

MESH = pl.DeviceIdType.MESH
ITERS = 16
RELAX = 0.1
DRAG = 0.5
TURN = 0.3
TILT = 0.05
KEEP = 1.0 / (1.0 + RELAX)

N_GX = 8
N_GY = 16
N_DEV = 128
LEGS = 2
HALO = 2 * ITERS // LEGS
SIDE = 2 * ITERS
ROWS = 128
EXT = ROWS + 2 * HALO
STEP = EXT // 8
TILES_X = 8
CT = TILES_X + 1
UNROLL = 10

MASS, STRENGTH, ZONAL, MERID, SUM, DIFF, SHEAR, SHARE, FORCE_X, FORCE_Y = range(10)
STATIC = 8
FIELDS = 10
FIRST, SECOND, BACK_SLOT, RECV_SLOT, EARLY, LATE = range(6)


def peers():
    order = []
    for n in range(32):
        j = (n * 13) % 32
        dx, dy, dc = j // 8, (j // 2) % 4, j % 2
        off = (n + n // 4 + 3 * dx + dy) % 4 if (dx, dy, dc) != (0, 0, 0) else 0
        order.append((dx, dy, dc, off))
    return order


def each_peer(visit, first=0, last=4):
    gx = lax.axis_index("gx")
    gy = lax.axis_index("gy")
    z, x_lo = gx % 4, gx // 4
    x_hi, y, core = gy // 8, (gy // 2) % 4, gy % 2
    x = x_hi * 2 + x_lo
    xs = [(x + d) % 4 for d in range(4)]
    part_gx = [(v % 2) * 4 for v in xs]
    part_gy = [(v // 2) * 8 for v in xs]
    ys = [((y + d) % 4) * 2 for d in range(4)]
    cores = [core, 1 - core]
    zs = tuple((z + d + first) % 4 for d in range(4))

    def turn(q, zs):
        for dx, dy, dc, off in peers():
            there = (part_gx[dx] + zs[off], part_gy[dx] + ys[dy] + cores[dc])
            if (dx, dy, dc) == (0, 0, 0):
                pl.when(q > 0)(functools.partial(visit, *there))
            else:
                visit(*there)
        return zs[1:] + zs[:1]

    lax.fori_loop(first, last, turn, zs)


def wait_for(ref, sem):
    pltpu.make_async_copy(ref, ref, sem).wait()


def aligned(start, size=8):
    return pl.ds(pl.multiple_of(start, 8), size)


def left_right(row, lane):
    n = len(row)
    left = [pltpu.roll(jnp.where(lane == 127, row[j - 1], row[j]), 1, 1) for j in range(n)]
    right = [pltpu.roll(jnp.where(lane == 0, row[(j + 1) % n], row[j]), 127, 1) for j in range(n)]
    return left, right


def fill_table(route, table, me):
    shape = (N_DEV, N_DEV)
    sub = lax.broadcasted_iota(jnp.int32, shape, 0)
    lane = lax.broadcasted_iota(jnp.int32, shape, 1)
    diagonal = sub == lane

    def to_column(row):
        return jnp.sum(jnp.where(diagonal, row, 0), axis=1, keepdims=True)

    def to_row(column):
        return jnp.sum(jnp.where(diagonal, column, 0), axis=0, keepdims=True)

    mine = jnp.right_shift(route[pl.ds(me, 1), :], 7)
    column = to_column(mine)
    hit = column == lane
    table[pl.ds(FIRST, 1), :] = jnp.min(jnp.where(hit, sub, N_DEV - 1), axis=0, keepdims=True)
    table[pl.ds(SECOND, 1), :] = jnp.max(jnp.where(hit, sub, 0), axis=0, keepdims=True)
    rank = jnp.max(jnp.where((column == mine) & (sub < lane), 1, 0), axis=0, keepdims=True)
    table[pl.ds(BACK_SLOT, 1), :] = mine * 2 + rank
    ids = route[...]
    here = jnp.right_shift(ids, 7) == me
    inside = jnp.bitwise_and(ids, N_DEV - 1)
    first = jnp.min(jnp.where(here, lane, N_DEV), axis=1, keepdims=True)
    second = jnp.max(jnp.where(here, lane, -1), axis=1, keepdims=True)
    early = jnp.sum(jnp.where(lane == first, inside + 1, 0), axis=1, keepdims=True) - 1
    late = jnp.sum(jnp.where(lane == second, inside + 1, 0), axis=1, keepdims=True) - 1
    slot = jnp.where(late == lane, 2 * sub + 1, jnp.where(early == lane, 2 * sub, 0))
    table[pl.ds(RECV_SLOT, 1), :] = jnp.max(slot, axis=0, keepdims=True)
    table[pl.ds(EARLY, 1), :] = to_row(jnp.maximum(early, 0))
    table[pl.ds(LATE, 1), :] = to_row(jnp.maximum(late, 0))
    table[pl.ds(6, 2), :] = jnp.zeros((2, N_DEV), jnp.int32)


def kernel(
    route, ocean, mask, mass, strength, velocity, stress,
    out_velocity, out_stress,
    routes, table, place, oc, outgoing, arrived, ext, ext_mask,
    to_east, to_west, from_west, from_east, force_to_east, force_to_west, force_from_west, force_from_east,
    nat, from_south, from_north, final, tiles, returning, arrived_back,
    cu, cv, cxx, cyy, csh, cstr, ks, km, kfx, kfy, ka, kb,
    in_sem, a2a_sem, halo_sem,
):
    gx = lax.axis_index("gx")
    gy = lax.axis_index("gy")
    me = gx * N_GY + gy
    top = gy == N_GY - 1
    inner = pl.ds(HALO, ROWS)
    lane = lax.broadcasted_iota(jnp.int32, (8, 128), 1)

    pltpu.make_async_copy(route, routes, in_sem.at[3]).start()
    pltpu.make_async_copy(ocean, oc, in_sem.at[0]).start()
    for j in range(TILES_X):
        cols = pl.ds(j * 128, 128)
        pltpu.make_async_copy(mass.at[:, cols], ext.at[MASS, j, inner], in_sem.at[1]).start()
        pltpu.make_async_copy(strength.at[:, cols], ext.at[STRENGTH, j, inner], in_sem.at[1]).start()
        pltpu.make_async_copy(velocity.at[:, :, cols], ext.at[pl.ds(ZONAL, 2), j, inner], in_sem.at[1]).start()
        pltpu.make_async_copy(stress.at[:, :, cols], ext.at[pl.ds(SUM, 3), j, inner], in_sem.at[1]).start()
        pltpu.make_async_copy(mask.at[:, cols], ext_mask.at[j], in_sem.at[2]).start()

    barrier = pltpu.get_barrier_semaphore()

    def greet(a, b):
        pl.semaphore_signal(barrier, inc=1, device_id=(a, b), device_id_type=MESH)

    each_peer(greet)

    wait_for(routes, in_sem.at[3])
    fill_table(routes, table, me)
    to_place = pltpu.make_async_copy(table, place, in_sem.at[4])
    to_place.start()

    wait_for(ext_mask, in_sem.at[2])

    def shares(i, carry):
        for j in range(TILES_X):
            ext[SHARE, j, aligned(HALO + i * 8)] = ext_mask[j, aligned(i * 8)].astype(jnp.float32)
        return carry

    lax.fori_loop(0, ROWS // 8, shares, 0)
    wait_for(ext.at[pl.ds(0, STATIC - 1), pl.ds(0, TILES_X), inner], in_sem.at[1])

    def gather_columns(first, count, east_out, west_out):
        def body(i, carry):
            rows = aligned(HALO + i * 8)
            for g in range((count + 3) // 4):
                e = w = None
                for q in range(min(4, count - 4 * g)):
                    f = first + 4 * g + q
                    a = pltpu.roll(ext[f, TILES_X - 1, rows], (SIDE * (q + 1)) % 128, 1)
                    b = ext[f, 0, rows]
                    if q:
                        b = pltpu.roll(b, SIDE * q, 1)
                    e = a if q == 0 else jnp.where(lane < SIDE * q, e, a)
                    w = b if q == 0 else jnp.where(lane < SIDE * q, w, b)
                east_out[g, aligned(i * 8)] = e
                west_out[g, aligned(i * 8)] = w
            return carry

        lax.fori_loop(0, ROWS // 8, body, 0)

    def spread_columns(first, count, west_in, east_in):
        def body(i, carry):
            rows = aligned(HALO + i * 8)
            for g in range((count + 3) // 4):
                e = east_in[g, aligned(i * 8)]
                w = west_in[g, aligned(i * 8)]
                for q in range(min(4, count - 4 * g)):
                    right = pltpu.roll(e, 128 - SIDE * q, 1) if q else e
                    left = pltpu.roll(w, 128 - SIDE * (q + 1), 1) if q < 3 else w
                    ext[first + 4 * g + q, TILES_X, rows] = jnp.where(lane < 64, right, left)
            return carry

        lax.fori_loop(0, ROWS // 8, body, 0)

    def columns(east_out, west_out, west_in, east_in, sems):
        a = pltpu.make_async_remote_copy(
            east_out, west_in, halo_sem.at[sems], halo_sem.at[sems + 1],
            device_id=((gx + 1) % N_GX, gy), device_id_type=MESH)
        b = pltpu.make_async_remote_copy(
            west_out, east_in, halo_sem.at[sems + 2], halo_sem.at[sems + 3],
            device_id=((gx + N_GX - 1) % N_GX, gy), device_id_type=MESH)
        return a, b

    north_gy = jnp.minimum(gy + 1, N_GY - 1)
    south_gy = jnp.maximum(gy - 1, 0)

    def rows_start(upper, lower, south, north, sems):
        to_north = pltpu.make_async_remote_copy(
            upper, south, halo_sem.at[sems], halo_sem.at[sems + 1],
            device_id=(gx, north_gy), device_id_type=MESH)
        to_partner = pltpu.make_async_remote_copy(
            upper, north, halo_sem.at[sems], halo_sem.at[sems + 3],
            device_id=(N_GX - 1 - gx, gy), device_id_type=MESH)
        to_south = pltpu.make_async_remote_copy(
            lower, north, halo_sem.at[sems + 2], halo_sem.at[sems + 3],
            device_id=(gx, south_gy), device_id_type=MESH)
        pl.when(jnp.logical_not(top))(to_north.start)
        pl.when(top)(to_partner.start)
        pl.when(gy > 0)(to_south.start)

    def rows_wait(upper, lower, south, north, sems):
        wait_for(north, halo_sem.at[sems + 3])
        wait_for(upper, halo_sem.at[sems])

        @pl.when(gy > 0)
        def _():
            wait_for(south, halo_sem.at[sems + 1])
            wait_for(lower, halo_sem.at[sems + 2])

    def strips(first, count):
        return tuple(
            ext.at[pl.ds(first, count), :, pl.ds(at, HALO)] for at in (ROWS, HALO, 0, HALO + ROWS))

    back_sub = 7 - lax.broadcasted_iota(jnp.int32, (8, 128), 0)
    back_lane = 127 - lane

    def turned(x):
        x = jnp.take_along_axis(x, back_lane, axis=1)
        return jnp.take_along_axis(x, back_sub, axis=0)

    def fold(ref, f, base, sign):
        for p in range(HALO // 16):
            here = pl.ds(base + p * 8, 8)
            there = pl.ds(base + HALO - 8 - p * 8, 8)

            def body(j, carry):
                a, b = ref[f, j, here], ref[f, TILES_X - 1 - j, there]
                ref[f, j, here] = turned(b) * sign
                ref[f, TILES_X - 1 - j, there] = turned(a) * sign
                return carry

            lax.fori_loop(0, TILES_X, body, 0)
            a, b = ref[f, TILES_X, here], ref[f, TILES_X, there]
            ref[f, TILES_X, here] = turned(b) * sign
            ref[f, TILES_X, there] = turned(a) * sign

    static_cols = columns(to_east, to_west, from_west, from_east, 0)
    force_cols = columns(force_to_east, force_to_west, force_from_west, force_from_east, 4)
    static_rows = strips(0, STATIC)
    force_rows = strips(FORCE_X, 2)

    gather_columns(0, STATIC, to_east, to_west)

    to_place.wait()
    wait_for(oc, in_sem.at[0])

    def pack(i, carry):
        for h in range(4):
            outgoing[i * 8 + 2 * h] = oc[place[FIRST, i * 4 + h]]
            outgoing[i * 8 + 2 * h + 1] = oc[place[SECOND, i * 4 + h]]
        return carry

    lax.fori_loop(0, N_DEV // 4, pack, 0)
    pl.semaphore_wait(barrier, N_DEV - 1)

    def send_forcing(a, b):
        pltpu.make_async_remote_copy(
            outgoing.at[pl.ds((a * N_GY + b) * 2, 2)], arrived.at[pl.ds(me * 2, 2)],
            a2a_sem.at[0], a2a_sem.at[1], device_id=(a, b), device_id_type=MESH,
        ).start()

    for copy in static_cols:
        copy.start()
    each_peer(send_forcing, 0, 1)
    for copy in static_cols:
        copy.wait()
    spread_columns(0, STATIC, from_west, from_east)
    rows_start(*static_rows, 8)
    each_peer(send_forcing, 1, 4)
    for h in range(2):
        arrived[me * 2 + h] = outgoing[me * 2 + h]

    @pl.when(gy == 0)
    def _():
        zero = jnp.zeros((8, 128), jnp.float32)

        def clear(j, carry):
            for p in range(HALO // 8):
                for f in range(FIELDS):
                    ext[f, j, pl.ds(p * 8, 8)] = zero + 1.0 if f == MASS else zero
            return carry

        lax.fori_loop(0, CT, clear, 0)

    rows_wait(*static_rows, 8)

    @pl.when(top)
    def _():
        for f in range(STATIC):
            fold(ext, f, HALO + ROWS, -1.0 if f in (ZONAL, MERID) else 1.0)

    def arrange(r, carry):
        rows = pl.ds(r, 8, stride=STEP)
        for j in range(CT):
            share = ext[SHARE, j, rows]
            m = ext[MASS, j, rows]
            strong = ext[STRENGTH, j, rows]
            a = m + DRAG
            b = TURN * m
            scale = share / (a * a + b * b)
            km[r, j] = m
            ka[r, j] = a * scale
            kb[r, j] = b * scale
            ks[r, j] = (0.0125 * KEEP) * strong
            cstr[r + 1, j] = strong
            cu[r + 1, j] = ext[ZONAL, j, rows] * share
            cv[r + 1, j] = ext[MERID, j, rows] * share
            both = 0.25 * (ext[SUM, j, rows] + strong)
            apart = 0.25 * ext[DIFF, j, rows]
            cxx[r + 1, j] = both + apart
            cyy[r + 1, j] = both - apart
            csh[r + 1, j] = 0.5 * ext[SHEAR, j, rows]
        return carry

    lax.fori_loop(0, STEP, arrange, 0)

    def ghosts(*refs):
        for ref in refs:
            for j in range(CT):
                ref[0, j] = pltpu.roll(ref[STEP, j], 1, 0)
                ref[STEP + 1, j] = pltpu.roll(ref[1, j], 7, 0)

    ghosts(cu, cv, cstr)

    wait_for(arrived.at[pl.ds(0, 2 * N_DEV - 2)], a2a_sem.at[1])
    wait_for(outgoing.at[pl.ds(0, 2 * N_DEV - 2)], a2a_sem.at[0])

    def forces(i, carry):
        rows = aligned(HALO + i * 8)
        for j in range(TILES_X):
            tile = arrived[place[RECV_SLOT, i * TILES_X + j]]
            m = TILT * ext[MASS, j, rows]
            ext[FORCE_X, j, rows] = tile[0] + m * tile[2]
            ext[FORCE_Y, j, rows] = tile[1] + m * tile[3]
        return carry

    lax.fori_loop(0, ROWS // 8, forces, 0)
    gather_columns(FORCE_X, 2, force_to_east, force_to_west)
    for copy in force_cols:
        copy.start()
    for copy in force_cols:
        copy.wait()
    spread_columns(FORCE_X, 2, force_from_west, force_from_east)
    rows_start(*force_rows, 12)
    rows_wait(*force_rows, 12)

    @pl.when(top)
    def _():
        fold(ext, FORCE_X, HALO + ROWS, -1.0)
        fold(ext, FORCE_Y, HALO + ROWS, -1.0)

    def arrange_forces(r, carry):
        rows = pl.ds(r, 8, stride=STEP)
        left, right = left_right([cstr[r + 1, j] for j in range(CT)], lane)
        for j in range(CT):
            kfx[r, j] = ext[FORCE_X, j, rows] - 0.25 * (right[j] - left[j])
            kfy[r, j] = ext[FORCE_Y, j, rows] - 0.25 * (cstr[r + 2, j] - cstr[r, j])
        return carry

    lax.fori_loop(0, STEP, arrange_forces, 0)

    def shifted(ref, r):
        def left(j):
            return pltpu.roll(jnp.where(lane == 127, ref[r, (j - 1) % CT], ref[r, j]), 1, 1)

        def right(j):
            return pltpu.roll(jnp.where(lane == 0, ref[r, (j + 1) % CT], ref[r, j]), 127, 1)

        return left, right

    def stresses(i, carry):
        for r in [i * UNROLL + h for h in range(UNROLL)]:
            u_left, u_right = shifted(cu, r + 1)
            v_left, v_right = shifted(cv, r + 1)
            for j in range(CT):
                ux = u_right(j) - u_left(j)
                vx = v_right(j) - v_left(j)
                uy = cu[r + 2, j] - cu[r, j]
                vy = cv[r + 2, j] - cv[r, j]
                div = ux + vy
                ten = ux - vy
                shr = uy + vx
                div2 = div + div
                w = ks[r, j] * lax.rsqrt(div2 * div2 + ten * ten + shr * shr + 16.0)
                div4 = div2 + div2
                cxx[r + 1, j] = KEEP * cxx[r + 1, j] + w * (div4 + ten)
                cyy[r + 1, j] = KEEP * cyy[r + 1, j] + w * (div4 - ten)
                csh[r + 1, j] = KEEP * csh[r + 1, j] + w * shr
        return carry

    def momentum(i, carry):
        for r in [i * UNROLL + h for h in range(UNROLL)]:
            xx_left, xx_right = shifted(cxx, r + 1)
            sh_left, sh_right = shifted(csh, r + 1)
            for j in range(CT):
                px = (xx_right(j) - xx_left(j)) + (csh[r + 2, j] - csh[r, j])
                py = (sh_right(j) - sh_left(j)) + (cyy[r + 2, j] - cyy[r, j])
                m = km[r, j]
                rx = m * cu[r + 1, j] + (px + kfx[r, j])
                ry = m * cv[r + 1, j] + (py + kfy[r, j])
                a = ka[r, j]
                b = kb[r, j]
                cu[r + 1, j] = a * rx + b * ry
                cv[r + 1, j] = a * ry - b * rx
        return carry

    carried = (cu, cv, cxx, cyy, csh)

    def to_grid_order(r, carry):
        for f, ref in enumerate(carried):
            for j in range(CT):
                nat[f, j, pl.ds(r, 8, stride=STEP)] = ref[r + 1, j]
        return carry

    def from_grid_order(r, carry):
        for f, ref in enumerate(carried):
            for j in range(CT):
                ref[r + 1, j] = nat[f, j, pl.ds(r, 8, stride=STEP)]
        return carry

    state_rows = (nat.at[:, :, pl.ds(ROWS, HALO)], nat.at[:, :, pl.ds(HALO, HALO)], from_south, from_north)

    def take(strip, base):
        def body(j, carry):
            for f in range(5):
                for p in range(HALO // 8):
                    nat[f, j, pl.ds(base + p * 8, 8)] = strip[f, j, pl.ds(p * 8, 8)]
            return carry

        lax.fori_loop(0, CT, body, 0)

    def exchange_rows():
        lax.fori_loop(0, STEP, to_grid_order, 0)
        rows_start(*state_rows, 16)
        rows_wait(*state_rows, 16)

        @pl.when(top)
        def _():
            for f in range(5):
                fold(from_north, f, 0, -1.0 if f < 2 else 1.0)

        take(from_north, HALO + ROWS)

        @pl.when(gy > 0)
        def _():
            take(from_south, 0)

        lax.fori_loop(0, STEP, from_grid_order, 0)
        ghosts(cu, cv)

    def subcycle(t, carry):
        pl.when(t == ITERS // LEGS)(exchange_rows)
        lax.fori_loop(0, STEP // UNROLL, stresses, 0)
        ghosts(cyy, csh)
        lax.fori_loop(0, STEP // UNROLL, momentum, 0)
        ghosts(cu, cv)
        return carry

    lax.fori_loop(0, ITERS, subcycle, 0)
    lax.fori_loop(0, STEP, to_grid_order, 0)

    def to_tiles(i, carry):
        rows = aligned(HALO + i * 8)
        for j in range(TILES_X):
            tiles[i * TILES_X + j, 0] = nat[0, j, rows]
            tiles[i * TILES_X + j, 1] = nat[1, j, rows]
        return carry

    lax.fori_loop(0, ROWS // 8, to_tiles, 0)

    def pack_back(i, carry):
        for h in range(4):
            returning[i * 8 + 2 * h] = tiles[place[EARLY, i * 4 + h]]
            returning[i * 8 + 2 * h + 1] = tiles[place[LATE, i * 4 + h]]
        return carry

    lax.fori_loop(0, N_DEV // 4, pack_back, 0)

    def send_back(a, b):
        pltpu.make_async_remote_copy(
            returning.at[pl.ds((a * N_GY + b) * 2, 2)], arrived_back.at[pl.ds(me * 2, 2)],
            a2a_sem.at[2], a2a_sem.at[3], device_id=(a, b), device_id_type=MESH,
        ).start()

    each_peer(send_back)
    for h in range(2):
        arrived_back[me * 2 + h] = returning[me * 2 + h]

    def finish(i, carry):
        rows = aligned(HALO + i * 8)
        for j in range(TILES_X):
            xx = nat[2, j, rows]
            yy = nat[3, j, rows]
            final[0, j, aligned(i * 8)] = 2.0 * (xx + yy) - ext[STRENGTH, j, rows]
            final[1, j, aligned(i * 8)] = 2.0 * (xx - yy)
            final[2, j, aligned(i * 8)] = 2.0 * nat[4, j, rows]
        return carry

    lax.fori_loop(0, ROWS // 8, finish, 0)
    for j in range(TILES_X):
        pltpu.make_async_copy(final.at[:, j], out_stress.at[:, :, pl.ds(j * 128, 128)], in_sem.at[1]).start()

    wait_for(arrived_back.at[pl.ds(0, 2 * N_DEV - 2)], a2a_sem.at[3])
    wait_for(returning.at[pl.ds(0, 2 * N_DEV - 2)], a2a_sem.at[2])

    def unpack(i, carry):
        for h in range(8):
            out_velocity[i * 8 + h] = arrived_back[place[BACK_SLOT, i * 8 + h]]
        return carry

    lax.fori_loop(0, N_DEV // 8, unpack, 0)
    wait_for(final, in_sem.at[1])


def local(ocean_forcing, route, land_mask, mass, strength, velocity_start, stress_start):
    f32, i32 = jnp.float32, jnp.int32
    hbm = pl.BlockSpec(memory_space=pl.ANY)
    ghosted = pltpu.VMEM((STEP + 2, CT, 8, 128), f32)
    plain = pltpu.VMEM((STEP, CT, 8, 128), f32)
    side = pltpu.VMEM((STATIC // 4, ROWS, 128), f32)
    force_side = pltpu.VMEM((1, ROWS, 128), f32)
    strip = pltpu.VMEM((5, CT, HALO, 128), f32)
    return pl.pallas_call(
        kernel,
        out_shape=(
            jax.ShapeDtypeStruct((N_DEV, 2, 8, 128), f32),
            jax.ShapeDtypeStruct((3, ROWS, TILES_X * 128), f32),
        ),
        in_specs=[hbm] * 7,
        out_specs=(pl.BlockSpec(memory_space=pltpu.VMEM), hbm),
        scratch_shapes=[
            pltpu.VMEM((N_DEV, N_DEV), i32),
            pltpu.VMEM((8, N_DEV), i32),
            pltpu.SMEM((8, N_DEV), i32),
            pltpu.VMEM((N_DEV, 4, 8, 128), f32),
            pltpu.VMEM((2 * N_DEV, 4, 8, 128), f32),
            pltpu.VMEM((2 * N_DEV, 4, 8, 128), f32),
            pltpu.VMEM((FIELDS, CT, EXT, 128), f32),
            pltpu.VMEM((TILES_X, ROWS, 128), i32),
            side, side, side, side,
            force_side, force_side, force_side, force_side,
            pltpu.VMEM((5, CT, EXT, 128), f32),
            strip, strip,
            pltpu.VMEM((3, TILES_X, ROWS, 128), f32),
            pltpu.VMEM((N_DEV, 2, 8, 128), f32),
            pltpu.VMEM((2 * N_DEV, 2, 8, 128), f32),
            pltpu.VMEM((2 * N_DEV, 2, 8, 128), f32),
            ghosted, ghosted, ghosted, ghosted, ghosted, ghosted,
            plain, plain, plain, plain, plain, plain,
            pltpu.SemaphoreType.DMA((5,)),
            pltpu.SemaphoreType.DMA((4,)),
            pltpu.SemaphoreType.DMA((20,)),
        ],
        compiler_params=pltpu.CompilerParams(
            collective_id=0, has_side_effects=True, vmem_limit_bytes=56 * 1024 * 1024),
    )(route.reshape(N_DEV, N_DEV), ocean_forcing, land_mask, mass, strength, velocity_start, stress_start)


def solution(mesh):
    placed = (
        P(("gx", "gy"), None, None, None),
        P(),
        P("gy", "gx"),
        P("gy", "gx"),
        P("gy", "gx"),
        P(None, "gy", "gx"),
        P(None, "gy", "gx"),
    )
    return jax.shard_map(
        local,
        mesh=mesh,
        in_specs=placed,
        out_specs=(P(("gx", "gy"), None, None, None), P(None, "gy", "gx")),
        check_vma=False,
    )
```

```python
import functools

import jax
import jax.numpy as jnp
from jax import lax
from jax.experimental import pallas as pl
from jax.experimental.pallas import tpu as pltpu
from jax.sharding import PartitionSpec as P

MESH = pl.DeviceIdType.MESH
ITERS = 16
RELAX = 0.1
DRAG = 0.5
TURN = 0.3
TILT = 0.05
KEEP = 1.0 / (1.0 + RELAX)

N_GX = 8
N_GY = 16
N_DEV = 128
LEGS = 2
HALO = 2 * ITERS // LEGS
SIDE = 2 * ITERS
ROWS = 128
EXT = ROWS + 2 * HALO
STEP = EXT // 8
TILES_X = 8
CT = TILES_X + 1
UNROLL = 10

MASS, STRENGTH, ZONAL, MERID, SUM, DIFF, SHEAR, SHARE, FORCE_X, FORCE_Y = range(10)
STATIC = 8
FIELDS = 10
FIRST, SECOND, BACK_SLOT, RECV_SLOT, EARLY, LATE = range(6)


def peers():
    order = []
    for n in range(32):
        j = (n * 13) % 32
        dx, dy, dc = j // 8, (j // 2) % 4, j % 2
        off = (n + n // 4 + 3 * dx + dy) % 4 if (dx, dy, dc) != (0, 0, 0) else 0
        order.append((dx, dy, dc, off))
    return order


def each_peer(visit, first=0, last=4):
    gx = lax.axis_index("gx")
    gy = lax.axis_index("gy")
    z, x_lo = gx % 4, gx // 4
    x_hi, y, core = gy // 8, (gy // 2) % 4, gy % 2
    x = x_hi * 2 + x_lo
    xs = [(x + d) % 4 for d in range(4)]
    part_gx = [(v % 2) * 4 for v in xs]
    part_gy = [(v // 2) * 8 for v in xs]
    ys = [((y + d) % 4) * 2 for d in range(4)]
    cores = [core, 1 - core]
    zs = tuple((z + d + first) % 4 for d in range(4))

    def turn(q, zs):
        for dx, dy, dc, off in peers():
            there = (part_gx[dx] + zs[off], part_gy[dx] + ys[dy] + cores[dc])
            if (dx, dy, dc) == (0, 0, 0):
                pl.when(q > 0)(functools.partial(visit, *there))
            else:
                visit(*there)
        return zs[1:] + zs[:1]

    lax.fori_loop(first, last, turn, zs)


def wait_for(ref, sem):
    pltpu.make_async_copy(ref, ref, sem).wait()


def aligned(start, size=8):
    return pl.ds(pl.multiple_of(start, 8), size)


def left_right(row, lane):
    n = len(row)
    left = [pltpu.roll(jnp.where(lane == 127, row[j - 1], row[j]), 1, 1) for j in range(n)]
    right = [pltpu.roll(jnp.where(lane == 0, row[(j + 1) % n], row[j]), 127, 1) for j in range(n)]
    return left, right


def fill_table(route, table, me):
    shape = (N_DEV, N_DEV)
    sub = lax.broadcasted_iota(jnp.int32, shape, 0)
    lane = lax.broadcasted_iota(jnp.int32, shape, 1)
    diagonal = sub == lane

    def to_column(row):
        return jnp.sum(jnp.where(diagonal, row, 0), axis=1, keepdims=True)

    def to_row(column):
        return jnp.sum(jnp.where(diagonal, column, 0), axis=0, keepdims=True)

    mine = jnp.right_shift(route[pl.ds(me, 1), :], 7)
    column = to_column(mine)
    hit = column == lane
    table[pl.ds(FIRST, 1), :] = jnp.min(jnp.where(hit, sub, N_DEV - 1), axis=0, keepdims=True)
    table[pl.ds(SECOND, 1), :] = jnp.max(jnp.where(hit, sub, 0), axis=0, keepdims=True)
    rank = jnp.max(jnp.where((column == mine) & (sub < lane), 1, 0), axis=0, keepdims=True)
    table[pl.ds(BACK_SLOT, 1), :] = mine * 2 + rank
    ids = route[...]
    here = jnp.right_shift(ids, 7) == me
    inside = jnp.bitwise_and(ids, N_DEV - 1)
    first = jnp.min(jnp.where(here, lane, N_DEV), axis=1, keepdims=True)
    second = jnp.max(jnp.where(here, lane, -1), axis=1, keepdims=True)
    early = jnp.sum(jnp.where(lane == first, inside + 1, 0), axis=1, keepdims=True) - 1
    late = jnp.sum(jnp.where(lane == second, inside + 1, 0), axis=1, keepdims=True) - 1
    slot = jnp.where(late == lane, 2 * sub + 1, jnp.where(early == lane, 2 * sub, 0))
    table[pl.ds(RECV_SLOT, 1), :] = jnp.max(slot, axis=0, keepdims=True)
    table[pl.ds(EARLY, 1), :] = to_row(jnp.maximum(early, 0))
    table[pl.ds(LATE, 1), :] = to_row(jnp.maximum(late, 0))
    table[pl.ds(6, 2), :] = jnp.zeros((2, N_DEV), jnp.int32)


def kernel(
    route, ocean, mask, mass, strength, velocity, stress,
    out_velocity, out_stress,
    routes, table, place, oc, mass_tiles, mass_out, mass_in, outgoing, arrived, ext, ext_mask,
    to_east, to_west, from_west, from_east, force_to_east, force_to_west, force_from_west, force_from_east,
    nat, from_south, from_north, final, tiles, returning, arrived_back,
    cu, cv, cxx, cyy, csh, cstr, ks, km, kfx, kfy, ka, kb,
    in_sem, a2a_sem, halo_sem,
):
    gx = lax.axis_index("gx")
    gy = lax.axis_index("gy")
    me = gx * N_GY + gy
    top = gy == N_GY - 1
    inner = pl.ds(HALO, ROWS)
    lane = lax.broadcasted_iota(jnp.int32, (8, 128), 1)

    pltpu.make_async_copy(route, routes, in_sem.at[3]).start()
    for j in range(TILES_X):
        pltpu.make_async_copy(mass.at[:, pl.ds(j * 128, 128)], ext.at[MASS, j, inner], in_sem.at[5]).start()
    for j in range(TILES_X):
        cols = pl.ds(j * 128, 128)
        pltpu.make_async_copy(strength.at[:, cols], ext.at[STRENGTH, j, inner], in_sem.at[1]).start()
        pltpu.make_async_copy(velocity.at[:, :, cols], ext.at[pl.ds(ZONAL, 2), j, inner], in_sem.at[1]).start()
        pltpu.make_async_copy(stress.at[:, :, cols], ext.at[pl.ds(SUM, 3), j, inner], in_sem.at[1]).start()
        pltpu.make_async_copy(mask.at[:, cols], ext_mask.at[j], in_sem.at[2]).start()

    pltpu.make_async_copy(ocean, oc, in_sem.at[0]).start()
    barrier = pltpu.get_barrier_semaphore()

    def greet(a, b):
        pl.semaphore_signal(barrier, inc=1, device_id=(a, b), device_id_type=MESH)

    each_peer(greet)

    wait_for(routes, in_sem.at[3])
    fill_table(routes, table, me)
    to_place = pltpu.make_async_copy(table, place, in_sem.at[4])
    to_place.start()

    wait_for(ext.at[MASS, pl.ds(0, TILES_X), inner], in_sem.at[5])

    def to_mass_tiles(i, carry):
        for j in range(TILES_X):
            mass_tiles[i * TILES_X + j] = ext[MASS, j, aligned(HALO + i * 8)]
        return carry

    lax.fori_loop(0, ROWS // 8, to_mass_tiles, 0)
    to_place.wait()

    def pack_mass(i, carry):
        for h in range(8):
            mass_out[i * 16 + 2 * h] = mass_tiles[place[EARLY, i * 8 + h]]
            mass_out[i * 16 + 2 * h + 1] = mass_tiles[place[LATE, i * 8 + h]]
        return carry

    lax.fori_loop(0, N_DEV // 8, pack_mass, 0)

    wait_for(ext_mask, in_sem.at[2])

    def shares(i, carry):
        for j in range(TILES_X):
            ext[SHARE, j, aligned(HALO + i * 8)] = ext_mask[j, aligned(i * 8)].astype(jnp.float32)
        return carry

    lax.fori_loop(0, ROWS // 8, shares, 0)
    wait_for(ext.at[pl.ds(STRENGTH, STATIC - 2), pl.ds(0, TILES_X), inner], in_sem.at[1])

    def gather_columns(first, count, east_out, west_out):
        def body(i, carry):
            rows = aligned(HALO + i * 8)
            for g in range((count + 3) // 4):
                e = w = None
                for q in range(min(4, count - 4 * g)):
                    f = first + 4 * g + q
                    a = pltpu.roll(ext[f, TILES_X - 1, rows], (SIDE * (q + 1)) % 128, 1)
                    b = ext[f, 0, rows]
                    if q:
                        b = pltpu.roll(b, SIDE * q, 1)
                    e = a if q == 0 else jnp.where(lane < SIDE * q, e, a)
                    w = b if q == 0 else jnp.where(lane < SIDE * q, w, b)
                east_out[g, aligned(i * 8)] = e
                west_out[g, aligned(i * 8)] = w
            return carry

        lax.fori_loop(0, ROWS // 8, body, 0)

    def spread_columns(first, count, west_in, east_in):
        def body(i, carry):
            rows = aligned(HALO + i * 8)
            for g in range((count + 3) // 4):
                e = east_in[g, aligned(i * 8)]
                w = west_in[g, aligned(i * 8)]
                for q in range(min(4, count - 4 * g)):
                    right = pltpu.roll(e, 128 - SIDE * q, 1) if q else e
                    left = pltpu.roll(w, 128 - SIDE * (q + 1), 1) if q < 3 else w
                    ext[first + 4 * g + q, TILES_X, rows] = jnp.where(lane < 64, right, left)
            return carry

        lax.fori_loop(0, ROWS // 8, body, 0)

    def columns(east_out, west_out, west_in, east_in, sems):
        a = pltpu.make_async_remote_copy(
            east_out, west_in, halo_sem.at[sems], halo_sem.at[sems + 1],
            device_id=((gx + 1) % N_GX, gy), device_id_type=MESH)
        b = pltpu.make_async_remote_copy(
            west_out, east_in, halo_sem.at[sems + 2], halo_sem.at[sems + 3],
            device_id=((gx + N_GX - 1) % N_GX, gy), device_id_type=MESH)
        return a, b

    north_gy = jnp.minimum(gy + 1, N_GY - 1)
    south_gy = jnp.maximum(gy - 1, 0)

    def rows_start(upper, lower, south, north, sems):
        to_north = pltpu.make_async_remote_copy(
            upper, south, halo_sem.at[sems], halo_sem.at[sems + 1],
            device_id=(gx, north_gy), device_id_type=MESH)
        to_partner = pltpu.make_async_remote_copy(
            upper, north, halo_sem.at[sems], halo_sem.at[sems + 3],
            device_id=(N_GX - 1 - gx, gy), device_id_type=MESH)
        to_south = pltpu.make_async_remote_copy(
            lower, north, halo_sem.at[sems + 2], halo_sem.at[sems + 3],
            device_id=(gx, south_gy), device_id_type=MESH)
        pl.when(jnp.logical_not(top))(to_north.start)
        pl.when(top)(to_partner.start)
        pl.when(gy > 0)(to_south.start)

    def rows_wait(upper, lower, south, north, sems):
        wait_for(north, halo_sem.at[sems + 3])
        wait_for(upper, halo_sem.at[sems])

        @pl.when(gy > 0)
        def _():
            wait_for(south, halo_sem.at[sems + 1])
            wait_for(lower, halo_sem.at[sems + 2])

    def strips(first, count):
        return tuple(
            ext.at[pl.ds(first, count), :, pl.ds(at, HALO)] for at in (ROWS, HALO, 0, HALO + ROWS))

    back_sub = 7 - lax.broadcasted_iota(jnp.int32, (8, 128), 0)
    back_lane = 127 - lane

    def turned(x):
        x = jnp.take_along_axis(x, back_lane, axis=1)
        return jnp.take_along_axis(x, back_sub, axis=0)

    def fold(ref, first, count, base, odd):
        tall = HALO // 8

        def body(f, carry):
            sign = jnp.where((f >= odd[0]) & (f < odd[1]), -1.0, 1.0)
            for j in range(TILES_X // 2 + 1):
                pair = (j, TILES_X - 1 - j) if j < TILES_X // 2 else (TILES_X,)
                old = [[ref[f, c, pl.ds(base + p * 8, 8)] for c in pair] for p in range(tall)]
                for p in range(tall):
                    for n, c in enumerate(pair):
                        ref[f, c, pl.ds(base + p * 8, 8)] = turned(old[tall - 1 - p][len(pair) - 1 - n]) * sign
            return carry

        lax.fori_loop(first, first + count, body, 0)

    static_cols = columns(to_east, to_west, from_west, from_east, 0)
    force_cols = columns(force_to_east, force_to_west, force_from_west, force_from_east, 4)
    static_rows = strips(0, STATIC)
    force_rows = strips(FORCE_X, 2)

    gather_columns(0, STATIC, to_east, to_west)

    pl.semaphore_wait(barrier, N_DEV - 1)

    def send_mass(a, b):
        pltpu.make_async_remote_copy(
            mass_out.at[pl.ds((a * N_GY + b) * 2, 2)], mass_in.at[pl.ds(me * 2, 2)],
            a2a_sem.at[4], a2a_sem.at[5], device_id=(a, b), device_id_type=MESH,
        ).start()

    def pack_forces(d):
        for h in range(2):
            tile = oc[place[FIRST + h, d]]
            m = TILT * mass_in[d * 2 + h]
            outgoing[d * 2 + h, 0] = tile[0] + m * tile[2]
            outgoing[d * 2 + h, 1] = tile[1] + m * tile[3]

    def send_forces(a, b):
        d = a * N_GY + b
        pack_forces(d)
        pltpu.make_async_remote_copy(
            outgoing.at[pl.ds(d * 2, 2)], arrived.at[pl.ds(me * 2, 2)],
            a2a_sem.at[0], a2a_sem.at[1], device_id=(a, b), device_id_type=MESH,
        ).start()

    for copy in static_cols:
        copy.start()
    each_peer(send_mass)
    for h in range(2):
        mass_in[me * 2 + h] = mass_out[me * 2 + h]
    for copy in static_cols:
        copy.wait()
    spread_columns(0, STATIC, from_west, from_east)
    rows_start(*static_rows, 8)

    wait_for(oc, in_sem.at[0])
    wait_for(mass_in.at[pl.ds(0, 2 * N_DEV - 2)], a2a_sem.at[5])
    each_peer(send_forces)
    pack_forces(me)
    for h in range(2):
        arrived[me * 2 + h] = outgoing[me * 2 + h]
    wait_for(mass_out.at[pl.ds(0, 2 * N_DEV - 2)], a2a_sem.at[4])

    @pl.when(gy == 0)
    def _():
        zero = jnp.zeros((8, 128), jnp.float32)

        def clear(j, carry):
            for p in range(HALO // 8):
                for f in range(FIELDS):
                    ext[f, j, pl.ds(p * 8, 8)] = zero + 1.0 if f == MASS else zero
            return carry

        lax.fori_loop(0, CT, clear, 0)

    rows_wait(*static_rows, 8)

    @pl.when(top)
    def _():
        fold(ext, 0, STATIC, HALO + ROWS, (ZONAL, MERID + 1))

    def arrange(r, carry):
        rows = pl.ds(r, 8, stride=STEP)
        for j in range(CT):
            share = ext[SHARE, j, rows]
            m = ext[MASS, j, rows]
            strong = ext[STRENGTH, j, rows]
            a = m + DRAG
            b = TURN * m
            scale = share / (a * a + b * b)
            km[r, j] = m
            ka[r, j] = a * scale
            kb[r, j] = b * scale
            ks[r, j] = (0.0125 * KEEP) * strong
            cstr[r + 1, j] = strong
            cu[r + 1, j] = ext[ZONAL, j, rows] * share
            cv[r + 1, j] = ext[MERID, j, rows] * share
            both = 0.25 * (ext[SUM, j, rows] + strong)
            apart = 0.25 * ext[DIFF, j, rows]
            cxx[r + 1, j] = both + apart
            cyy[r + 1, j] = both - apart
            csh[r + 1, j] = 0.5 * ext[SHEAR, j, rows]
        return carry

    lax.fori_loop(0, STEP, arrange, 0)

    def ghosts(*refs):
        for ref in refs:
            for j in range(CT):
                ref[0, j] = pltpu.roll(ref[STEP, j], 1, 0)
                ref[STEP + 1, j] = pltpu.roll(ref[1, j], 7, 0)

    ghosts(cu, cv, cstr)

    wait_for(arrived.at[pl.ds(0, 2 * N_DEV - 2)], a2a_sem.at[1])
    wait_for(outgoing.at[pl.ds(0, 2 * N_DEV - 2)], a2a_sem.at[0])

    def forces(i, carry):
        rows = aligned(HALO + i * 8)
        for j in range(TILES_X):
            tile = arrived[place[RECV_SLOT, i * TILES_X + j]]
            ext[FORCE_X, j, rows] = tile[0]
            ext[FORCE_Y, j, rows] = tile[1]
        return carry

    lax.fori_loop(0, ROWS // 8, forces, 0)
    gather_columns(FORCE_X, 2, force_to_east, force_to_west)
    for copy in force_cols:
        copy.start()
    for copy in force_cols:
        copy.wait()
    spread_columns(FORCE_X, 2, force_from_west, force_from_east)
    rows_start(*force_rows, 12)
    rows_wait(*force_rows, 12)

    @pl.when(top)
    def _():
        fold(ext, FORCE_X, 2, HALO + ROWS, (FORCE_X, FORCE_Y + 1))

    def arrange_forces(r, carry):
        rows = pl.ds(r, 8, stride=STEP)
        left, right = left_right([cstr[r + 1, j] for j in range(CT)], lane)
        for j in range(CT):
            kfx[r, j] = ext[FORCE_X, j, rows] - 0.25 * (right[j] - left[j])
            kfy[r, j] = ext[FORCE_Y, j, rows] - 0.25 * (cstr[r + 2, j] - cstr[r, j])
        return carry

    lax.fori_loop(0, STEP, arrange_forces, 0)

    def shifted(ref, r):
        def left(j):
            return pltpu.roll(jnp.where(lane == 127, ref[r, (j - 1) % CT], ref[r, j]), 1, 1)

        def right(j):
            return pltpu.roll(jnp.where(lane == 0, ref[r, (j + 1) % CT], ref[r, j]), 127, 1)

        return left, right

    def stresses(i, carry):
        for r in [i * UNROLL + h for h in range(UNROLL)]:
            u_left, u_right = shifted(cu, r + 1)
            v_left, v_right = shifted(cv, r + 1)
            for j in range(CT):
                ux = u_right(j) - u_left(j)
                vx = v_right(j) - v_left(j)
                uy = cu[r + 2, j] - cu[r, j]
                vy = cv[r + 2, j] - cv[r, j]
                div = ux + vy
                ten = ux - vy
                shr = uy + vx
                div2 = div + div
                w = ks[r, j] * lax.rsqrt(div2 * div2 + ten * ten + shr * shr + 16.0)
                div4 = div2 + div2
                cxx[r + 1, j] = KEEP * cxx[r + 1, j] + w * (div4 + ten)
                cyy[r + 1, j] = KEEP * cyy[r + 1, j] + w * (div4 - ten)
                csh[r + 1, j] = KEEP * csh[r + 1, j] + w * shr
        return carry

    def momentum(i, carry):
        for r in [i * UNROLL + h for h in range(UNROLL)]:
            xx_left, xx_right = shifted(cxx, r + 1)
            sh_left, sh_right = shifted(csh, r + 1)
            for j in range(CT):
                px = (xx_right(j) - xx_left(j)) + (csh[r + 2, j] - csh[r, j])
                py = (sh_right(j) - sh_left(j)) + (cyy[r + 2, j] - cyy[r, j])
                m = km[r, j]
                rx = m * cu[r + 1, j] + (px + kfx[r, j])
                ry = m * cv[r + 1, j] + (py + kfy[r, j])
                a = ka[r, j]
                b = kb[r, j]
                cu[r + 1, j] = a * rx + b * ry
                cv[r + 1, j] = a * ry - b * rx
        return carry

    carried = (cu, cv, cxx, cyy, csh)

    def to_grid_order(first, count):
        def body(r, carry):
            for f in range(first, first + count):
                for j in range(CT):
                    nat[f, j, pl.ds(r, 8, stride=STEP)] = carried[f][r + 1, j]
            return carry

        lax.fori_loop(0, STEP, body, 0)

    def from_grid_order(r, carry):
        for f, ref in enumerate(carried):
            for j in range(CT):
                ref[r + 1, j] = nat[f, j, pl.ds(r, 8, stride=STEP)]
        return carry

    state_rows = (nat.at[:, :, pl.ds(ROWS, HALO)], nat.at[:, :, pl.ds(HALO, HALO)], from_south, from_north)

    def take(strip, base):
        def body(j, carry):
            for f in range(5):
                for p in range(HALO // 8):
                    nat[f, j, pl.ds(base + p * 8, 8)] = strip[f, j, pl.ds(p * 8, 8)]
            return carry

        lax.fori_loop(0, CT, body, 0)

    def exchange_rows():
        to_grid_order(0, 5)
        rows_start(*state_rows, 16)
        rows_wait(*state_rows, 16)

        @pl.when(top)
        def _():
            fold(from_north, 0, 5, 0, (0, 2))

        take(from_north, HALO + ROWS)

        @pl.when(gy > 0)
        def _():
            take(from_south, 0)

        lax.fori_loop(0, STEP, from_grid_order, 0)
        ghosts(cu, cv)

    def subcycle(t, carry):
        pl.when(t == ITERS // LEGS)(exchange_rows)
        lax.fori_loop(0, STEP // UNROLL, stresses, 0)
        ghosts(cyy, csh)
        lax.fori_loop(0, STEP // UNROLL, momentum, 0)
        ghosts(cu, cv)
        return carry

    lax.fori_loop(0, ITERS, subcycle, 0)
    to_grid_order(0, 2)

    def to_tiles(i, carry):
        rows = aligned(HALO + i * 8)
        for j in range(TILES_X):
            tiles[i * TILES_X + j, 0] = nat[0, j, rows]
            tiles[i * TILES_X + j, 1] = nat[1, j, rows]
        return carry

    lax.fori_loop(0, ROWS // 8, to_tiles, 0)

    def pack_back(d):
        returning[d * 2] = tiles[place[EARLY, d]]
        returning[d * 2 + 1] = tiles[place[LATE, d]]

    def send_back(a, b):
        d = a * N_GY + b
        pack_back(d)
        pltpu.make_async_remote_copy(
            returning.at[pl.ds(d * 2, 2)], arrived_back.at[pl.ds(me * 2, 2)],
            a2a_sem.at[2], a2a_sem.at[3], device_id=(a, b), device_id_type=MESH,
        ).start()

    each_peer(send_back)
    pack_back(me)
    for h in range(2):
        arrived_back[me * 2 + h] = returning[me * 2 + h]
    to_grid_order(2, 3)

    def finish(i, carry):
        rows = aligned(HALO + i * 8)
        for j in range(TILES_X):
            xx = nat[2, j, rows]
            yy = nat[3, j, rows]
            final[0, j, aligned(i * 8)] = 2.0 * (xx + yy) - ext[STRENGTH, j, rows]
            final[1, j, aligned(i * 8)] = 2.0 * (xx - yy)
            final[2, j, aligned(i * 8)] = 2.0 * nat[4, j, rows]
        return carry

    lax.fori_loop(0, ROWS // 8, finish, 0)
    for j in range(TILES_X):
        pltpu.make_async_copy(final.at[:, j], out_stress.at[:, :, pl.ds(j * 128, 128)], in_sem.at[1]).start()

    wait_for(arrived_back.at[pl.ds(0, 2 * N_DEV - 2)], a2a_sem.at[3])
    wait_for(returning.at[pl.ds(0, 2 * N_DEV - 2)], a2a_sem.at[2])

    def unpack(i, carry):
        for h in range(8):
            out_velocity[i * 8 + h] = arrived_back[place[BACK_SLOT, i * 8 + h]]
        return carry

    lax.fori_loop(0, N_DEV // 8, unpack, 0)
    wait_for(final, in_sem.at[1])


def local(ocean_forcing, route, land_mask, mass, strength, velocity_start, stress_start):
    f32, i32 = jnp.float32, jnp.int32
    hbm = pl.BlockSpec(memory_space=pl.ANY)
    ghosted = pltpu.VMEM((STEP + 2, CT, 8, 128), f32)
    plain = pltpu.VMEM((STEP, CT, 8, 128), f32)
    side = pltpu.VMEM((STATIC // 4, ROWS, 128), f32)
    force_side = pltpu.VMEM((1, ROWS, 128), f32)
    strip = pltpu.VMEM((5, CT, HALO, 128), f32)
    return pl.pallas_call(
        kernel,
        out_shape=(
            jax.ShapeDtypeStruct((N_DEV, 2, 8, 128), f32),
            jax.ShapeDtypeStruct((3, ROWS, TILES_X * 128), f32),
        ),
        in_specs=[hbm] * 7,
        out_specs=(pl.BlockSpec(memory_space=pltpu.VMEM), hbm),
        scratch_shapes=[
            pltpu.VMEM((N_DEV, N_DEV), i32),
            pltpu.VMEM((8, N_DEV), i32),
            pltpu.SMEM((8, N_DEV), i32),
            pltpu.VMEM((N_DEV, 4, 8, 128), f32),
            pltpu.VMEM((N_DEV, 8, 128), f32),
            pltpu.VMEM((2 * N_DEV, 8, 128), f32),
            pltpu.VMEM((2 * N_DEV, 8, 128), f32),
            pltpu.VMEM((2 * N_DEV, 2, 8, 128), f32),
            pltpu.VMEM((2 * N_DEV, 2, 8, 128), f32),
            pltpu.VMEM((FIELDS, CT, EXT, 128), f32),
            pltpu.VMEM((TILES_X, ROWS, 128), i32),
            side, side, side, side,
            force_side, force_side, force_side, force_side,
            pltpu.VMEM((5, CT, EXT, 128), f32),
            strip, strip,
            pltpu.VMEM((3, TILES_X, ROWS, 128), f32),
            pltpu.VMEM((N_DEV, 2, 8, 128), f32),
            pltpu.VMEM((2 * N_DEV, 2, 8, 128), f32),
            pltpu.VMEM((2 * N_DEV, 2, 8, 128), f32),
            ghosted, ghosted, ghosted, ghosted, ghosted, ghosted,
            plain, plain, plain, plain, plain, plain,
            pltpu.SemaphoreType.DMA((6,)),
            pltpu.SemaphoreType.DMA((6,)),
            pltpu.SemaphoreType.DMA((20,)),
        ],
        compiler_params=pltpu.CompilerParams(
            collective_id=0, has_side_effects=True, vmem_limit_bytes=56 * 1024 * 1024),
    )(route.reshape(N_DEV, N_DEV), ocean_forcing, land_mask, mass, strength, velocity_start, stress_start)


def solution(mesh):
    placed = (
        P(("gx", "gy"), None, None, None),
        P(),
        P("gy", "gx"),
        P("gy", "gx"),
        P("gy", "gx"),
        P(None, "gy", "gx"),
        P(None, "gy", "gx"),
    )
    return jax.shard_map(
        local,
        mesh=mesh,
        in_specs=placed,
        out_specs=(P(("gx", "gy"), None, None, None), P(None, "gy", "gx")),
        check_vma=False,
    )
```

```python
import functools

import jax
import jax.numpy as jnp
from jax import lax
from jax.experimental import pallas as pl
from jax.experimental.pallas import tpu as pltpu
from jax.sharding import PartitionSpec as P

MESH = pl.DeviceIdType.MESH
ITERS = 16
RELAX = 0.1
DRAG = 0.5
TURN = 0.3
TILT = 0.05
KEEP = 1.0 / (1.0 + RELAX)

N_GX = 8
N_GY = 16
N_DEV = 128
LEGS = 2
HALO = 2 * ITERS // LEGS
SIDE = 2 * ITERS
ROWS = 128
EXT = ROWS + 2 * HALO
STEP = EXT // 8
TILES_X = 8
CT = TILES_X + 1
UNROLL = 10

MASS, STRENGTH, ZONAL, MERID, SUM, DIFF, SHEAR, SHARE, FORCE_X, FORCE_Y = range(10)
STATIC = 8
FIELDS = 10
FIRST, SECOND, BACK_SLOT, RECV_SLOT, EARLY, LATE = range(6)


def peers():
    order = []
    for n in range(32):
        j = (n * 13) % 32
        dx, dy, dc = j // 8, (j // 2) % 4, j % 2
        off = (n + n // 4 + 3 * dx + dy) % 4 if (dx, dy, dc) != (0, 0, 0) else 0
        order.append((dx, dy, dc, off))
    return order


def each_peer(visit, between=()):
    gx = lax.axis_index("gx")
    gy = lax.axis_index("gy")
    z, x_lo = gx % 4, gx // 4
    x_hi, y, core = gy // 8, (gy // 2) % 4, gy % 2
    x = x_hi * 2 + x_lo
    xs = [(x + d) % 4 for d in range(4)]
    part_gx = [(v % 2) * 4 for v in xs]
    part_gy = [(v // 2) * 8 for v in xs]
    ys = [((y + d) % 4) * 2 for d in range(4)]
    cores = [core, 1 - core]
    zs = tuple((z + d) % 4 for d in range(4))

    def turn(q, zs):
        for n, (dx, dy, dc, off) in enumerate(peers()):
            for i, extra in enumerate(between):
                if n == (2 * i + 1) * 16 // len(between):
                    extra(q)
            there = (part_gx[dx] + zs[off], part_gy[dx] + ys[dy] + cores[dc])
            if (dx, dy, dc) == (0, 0, 0):
                pl.when(q > 0)(functools.partial(visit, *there))
            else:
                visit(*there)
        return zs[1:] + zs[:1]

    lax.fori_loop(0, 4, turn, zs)


def wait_for(ref, sem):
    pltpu.make_async_copy(ref, ref, sem).wait()


def aligned(start, size=8):
    return pl.ds(pl.multiple_of(start, 8), size)


def left_right(row, lane):
    n = len(row)
    left = [pltpu.roll(jnp.where(lane == 127, row[j - 1], row[j]), 1, 1) for j in range(n)]
    right = [pltpu.roll(jnp.where(lane == 0, row[(j + 1) % n], row[j]), 127, 1) for j in range(n)]
    return left, right


def fill_table(route, table, me):
    shape = (N_DEV, N_DEV)
    sub = lax.broadcasted_iota(jnp.int32, shape, 0)
    lane = lax.broadcasted_iota(jnp.int32, shape, 1)
    diagonal = sub == lane

    def to_column(row):
        return jnp.sum(jnp.where(diagonal, row, 0), axis=1, keepdims=True)

    def to_row(column):
        return jnp.sum(jnp.where(diagonal, column, 0), axis=0, keepdims=True)

    mine = jnp.right_shift(route[pl.ds(me, 1), :], 7)
    column = to_column(mine)
    hit = column == lane
    table[pl.ds(FIRST, 1), :] = jnp.min(jnp.where(hit, sub, N_DEV - 1), axis=0, keepdims=True)
    table[pl.ds(SECOND, 1), :] = jnp.max(jnp.where(hit, sub, 0), axis=0, keepdims=True)
    rank = jnp.max(jnp.where((column == mine) & (sub < lane), 1, 0), axis=0, keepdims=True)
    table[pl.ds(BACK_SLOT, 1), :] = mine * 2 + rank
    ids = route[...]
    here = jnp.right_shift(ids, 7) == me
    inside = jnp.bitwise_and(ids, N_DEV - 1)
    first = jnp.min(jnp.where(here, lane, N_DEV), axis=1, keepdims=True)
    second = jnp.max(jnp.where(here, lane, -1), axis=1, keepdims=True)
    early = jnp.sum(jnp.where(lane == first, inside + 1, 0), axis=1, keepdims=True) - 1
    late = jnp.sum(jnp.where(lane == second, inside + 1, 0), axis=1, keepdims=True) - 1
    slot = jnp.where(late == lane, 2 * sub + 1, jnp.where(early == lane, 2 * sub, 0))
    table[pl.ds(RECV_SLOT, 1), :] = jnp.max(slot, axis=0, keepdims=True)
    table[pl.ds(EARLY, 1), :] = to_row(jnp.maximum(early, 0))
    table[pl.ds(LATE, 1), :] = to_row(jnp.maximum(late, 0))
    table[pl.ds(6, 2), :] = jnp.zeros((2, N_DEV), jnp.int32)


def kernel(
    route, ocean, mask, mass, strength, velocity, stress,
    out_velocity, out_stress,
    routes, table, place, oc, mass_tiles, mass_out, mass_in, outgoing, arrived, ext, ext_mask,
    to_east, to_west, from_west, from_east, force_to_east, force_to_west, force_from_west, force_from_east,
    nat, from_south, from_north, final, tiles, returning, arrived_back,
    cu, cv, cxx, cyy, csh, cstr, ks, km, kfx, kfy, ka, kb,
    in_sem, a2a_sem, halo_sem,
):
    gx = lax.axis_index("gx")
    gy = lax.axis_index("gy")
    me = gx * N_GY + gy
    top = gy == N_GY - 1
    inner = pl.ds(HALO, ROWS)
    lane = lax.broadcasted_iota(jnp.int32, (8, 128), 1)

    pltpu.make_async_copy(route, routes, in_sem.at[3]).start()
    for j in range(TILES_X):
        pltpu.make_async_copy(mass.at[:, pl.ds(j * 128, 128)], ext.at[MASS, j, inner], in_sem.at[5]).start()
    for j in range(TILES_X):
        cols = pl.ds(j * 128, 128)
        pltpu.make_async_copy(strength.at[:, cols], ext.at[STRENGTH, j, inner], in_sem.at[1]).start()
        pltpu.make_async_copy(velocity.at[:, :, cols], ext.at[pl.ds(ZONAL, 2), j, inner], in_sem.at[1]).start()
        pltpu.make_async_copy(stress.at[:, :, cols], ext.at[pl.ds(SUM, 3), j, inner], in_sem.at[1]).start()
        pltpu.make_async_copy(mask.at[:, cols], ext_mask.at[j], in_sem.at[2]).start()

    pltpu.make_async_copy(ocean, oc, in_sem.at[0]).start()
    barrier = pltpu.get_barrier_semaphore()

    def greet(a, b):
        pl.semaphore_signal(barrier, inc=1, device_id=(a, b), device_id_type=MESH)

    each_peer(greet)

    wait_for(routes, in_sem.at[3])
    fill_table(routes, table, me)
    to_place = pltpu.make_async_copy(table, place, in_sem.at[4])
    to_place.start()

    wait_for(ext.at[MASS, pl.ds(0, TILES_X), inner], in_sem.at[5])

    def to_mass_tiles(i, carry):
        for j in range(TILES_X):
            mass_tiles[i * TILES_X + j] = ext[MASS, j, aligned(HALO + i * 8)]
        return carry

    lax.fori_loop(0, ROWS // 8, to_mass_tiles, 0)
    to_place.wait()

    def pack_mass(i, carry):
        for h in range(8):
            mass_out[i * 16 + 2 * h] = mass_tiles[place[EARLY, i * 8 + h]]
            mass_out[i * 16 + 2 * h + 1] = mass_tiles[place[LATE, i * 8 + h]]
        return carry

    lax.fori_loop(0, N_DEV // 8, pack_mass, 0)

    wait_for(ext_mask, in_sem.at[2])

    def shares(i, carry):
        for j in range(TILES_X):
            ext[SHARE, j, aligned(HALO + i * 8)] = ext_mask[j, aligned(i * 8)].astype(jnp.float32)
        return carry

    lax.fori_loop(0, ROWS // 8, shares, 0)
    wait_for(ext.at[pl.ds(STRENGTH, STATIC - 2), pl.ds(0, TILES_X), inner], in_sem.at[1])

    def gather_columns(first, count, east_out, west_out):
        def body(i, carry):
            rows = aligned(HALO + i * 8)
            for g in range((count + 3) // 4):
                e = w = None
                for q in range(min(4, count - 4 * g)):
                    f = first + 4 * g + q
                    a = pltpu.roll(ext[f, TILES_X - 1, rows], (SIDE * (q + 1)) % 128, 1)
                    b = ext[f, 0, rows]
                    if q:
                        b = pltpu.roll(b, SIDE * q, 1)
                    e = a if q == 0 else jnp.where(lane < SIDE * q, e, a)
                    w = b if q == 0 else jnp.where(lane < SIDE * q, w, b)
                east_out[g, aligned(i * 8)] = e
                west_out[g, aligned(i * 8)] = w
            return carry

        lax.fori_loop(0, ROWS // 8, body, 0)

    def spread_columns(first, count, west_in, east_in):
        def body(i, carry):
            rows = aligned(HALO + i * 8)
            for g in range((count + 3) // 4):
                e = east_in[g, aligned(i * 8)]
                w = west_in[g, aligned(i * 8)]
                for q in range(min(4, count - 4 * g)):
                    right = pltpu.roll(e, 128 - SIDE * q, 1) if q else e
                    left = pltpu.roll(w, 128 - SIDE * (q + 1), 1) if q < 3 else w
                    ext[first + 4 * g + q, TILES_X, rows] = jnp.where(lane < 64, right, left)
            return carry

        lax.fori_loop(0, ROWS // 8, body, 0)

    def columns(east_out, west_out, west_in, east_in, sems):
        a = pltpu.make_async_remote_copy(
            east_out, west_in, halo_sem.at[sems], halo_sem.at[sems + 1],
            device_id=((gx + 1) % N_GX, gy), device_id_type=MESH)
        b = pltpu.make_async_remote_copy(
            west_out, east_in, halo_sem.at[sems + 2], halo_sem.at[sems + 3],
            device_id=((gx + N_GX - 1) % N_GX, gy), device_id_type=MESH)
        return a, b

    north_gy = jnp.minimum(gy + 1, N_GY - 1)
    south_gy = jnp.maximum(gy - 1, 0)

    def rows_north(upper, lower, south, north, sems):
        to_north = pltpu.make_async_remote_copy(
            upper, south, halo_sem.at[sems], halo_sem.at[sems + 1],
            device_id=(gx, north_gy), device_id_type=MESH)
        to_partner = pltpu.make_async_remote_copy(
            upper, north, halo_sem.at[sems], halo_sem.at[sems + 3],
            device_id=(N_GX - 1 - gx, gy), device_id_type=MESH)
        pl.when(jnp.logical_not(top))(to_north.start)
        pl.when(top)(to_partner.start)

    def rows_south(upper, lower, south, north, sems):
        to_south = pltpu.make_async_remote_copy(
            lower, north, halo_sem.at[sems + 2], halo_sem.at[sems + 3],
            device_id=(gx, south_gy), device_id_type=MESH)
        pl.when(gy > 0)(to_south.start)

    def rows_start(*args):
        rows_north(*args)
        rows_south(*args)

    def rows_wait(upper, lower, south, north, sems):
        wait_for(north, halo_sem.at[sems + 3])
        wait_for(upper, halo_sem.at[sems])

        @pl.when(gy > 0)
        def _():
            wait_for(south, halo_sem.at[sems + 1])
            wait_for(lower, halo_sem.at[sems + 2])

    def strips(first, count, tile=0, tiles=CT):
        return tuple(
            ext.at[pl.ds(first, count), pl.ds(tile, tiles), pl.ds(at, HALO)]
            for at in (ROWS, HALO, 0, HALO + ROWS))

    back_sub = 7 - lax.broadcasted_iota(jnp.int32, (8, 128), 0)
    back_lane = 127 - lane

    def turned(x):
        x = jnp.take_along_axis(x, back_lane, axis=1)
        return jnp.take_along_axis(x, back_sub, axis=0)

    def fold(ref, first, count, base, odd):
        tall = HALO // 8

        def body(f, carry):
            sign = jnp.where((f >= odd[0]) & (f < odd[1]), -1.0, 1.0)
            for j in range(TILES_X // 2 + 1):
                pair = (j, TILES_X - 1 - j) if j < TILES_X // 2 else (TILES_X,)
                old = [[ref[f, c, pl.ds(base + p * 8, 8)] for c in pair] for p in range(tall)]
                for p in range(tall):
                    for n, c in enumerate(pair):
                        ref[f, c, pl.ds(base + p * 8, 8)] = turned(old[tall - 1 - p][len(pair) - 1 - n]) * sign
            return carry

        lax.fori_loop(first, first + count, body, 0)

    static_cols = columns(to_east, to_west, from_west, from_east, 0)
    force_cols = columns(force_to_east, force_to_west, force_from_west, force_from_east, 4)
    static_rows = strips(0, STATIC)
    force_rows = strips(FORCE_X, 2)

    gather_columns(0, STATIC, to_east, to_west)

    pl.semaphore_wait(barrier, N_DEV - 1)

    def send_mass(a, b):
        pltpu.make_async_remote_copy(
            mass_out.at[pl.ds((a * N_GY + b) * 2, 2)], mass_in.at[pl.ds(me * 2, 2)],
            a2a_sem.at[4], a2a_sem.at[5], device_id=(a, b), device_id_type=MESH,
        ).start()

    def pack_forces(d):
        for h in range(2):
            tile = oc[place[FIRST + h, d]]
            m = TILT * mass_in[d * 2 + h]
            outgoing[d * 2 + h, 0] = tile[0] + m * tile[2]
            outgoing[d * 2 + h, 1] = tile[1] + m * tile[3]

    def send_forces(a, b):
        d = a * N_GY + b
        pack_forces(d)
        pltpu.make_async_remote_copy(
            outgoing.at[pl.ds(d * 2, 2)], arrived.at[pl.ds(me * 2, 2)],
            a2a_sem.at[0], a2a_sem.at[1], device_id=(a, b), device_id_type=MESH,
        ).start()

    for copy in static_cols:
        copy.start()
    each_peer(send_mass, (
        lambda q: rows_north(*strips(q, 1, 0, TILES_X), 8),
        lambda q: rows_south(*strips(q, 1, 0, TILES_X), 8),
    ))
    for h in range(2):
        mass_in[me * 2 + h] = mass_out[me * 2 + h]
    for copy in static_cols:
        copy.wait()
    spread_columns(0, STATIC, from_west, from_east)

    wait_for(oc, in_sem.at[0])
    wait_for(mass_in.at[pl.ds(0, 2 * N_DEV - 2)], a2a_sem.at[5])
    rows_start(*strips(0, STATIC, TILES_X, 1), 8)
    each_peer(send_forces, (
        lambda q: rows_north(*strips(4 + q, 1, 0, TILES_X), 8),
        lambda q: rows_south(*strips(4 + q, 1, 0, TILES_X), 8),
    ))
    pack_forces(me)
    for h in range(2):
        arrived[me * 2 + h] = outgoing[me * 2 + h]
    wait_for(mass_out.at[pl.ds(0, 2 * N_DEV - 2)], a2a_sem.at[4])

    @pl.when(gy == 0)
    def _():
        zero = jnp.zeros((8, 128), jnp.float32)

        def clear(j, carry):
            for p in range(HALO // 8):
                for f in range(FIELDS):
                    ext[f, j, pl.ds(p * 8, 8)] = zero + 1.0 if f == MASS else zero
            return carry

        lax.fori_loop(0, CT, clear, 0)

    rows_wait(*static_rows, 8)

    @pl.when(top)
    def _():
        fold(ext, 0, STATIC, HALO + ROWS, (ZONAL, MERID + 1))

    def arrange(r, carry):
        rows = pl.ds(r, 8, stride=STEP)
        for j in range(CT):
            share = ext[SHARE, j, rows]
            m = ext[MASS, j, rows]
            strong = ext[STRENGTH, j, rows]
            a = m + DRAG
            b = TURN * m
            scale = share / (a * a + b * b)
            km[r, j] = m
            ka[r, j] = a * scale
            kb[r, j] = b * scale
            ks[r, j] = (0.0125 * KEEP) * strong
            cstr[r + 1, j] = strong
            cu[r + 1, j] = ext[ZONAL, j, rows] * share
            cv[r + 1, j] = ext[MERID, j, rows] * share
            both = 0.25 * (ext[SUM, j, rows] + strong)
            apart = 0.25 * ext[DIFF, j, rows]
            cxx[r + 1, j] = both + apart
            cyy[r + 1, j] = both - apart
            csh[r + 1, j] = 0.5 * ext[SHEAR, j, rows]
        return carry

    lax.fori_loop(0, STEP, arrange, 0)

    def ghosts(*refs):
        for ref in refs:
            for j in range(CT):
                ref[0, j] = pltpu.roll(ref[STEP, j], 1, 0)
                ref[STEP + 1, j] = pltpu.roll(ref[1, j], 7, 0)

    ghosts(cu, cv, cstr)

    wait_for(arrived.at[pl.ds(0, 2 * N_DEV - 2)], a2a_sem.at[1])
    wait_for(outgoing.at[pl.ds(0, 2 * N_DEV - 2)], a2a_sem.at[0])

    def forces(i, carry):
        rows = aligned(HALO + i * 8)
        for j in range(TILES_X):
            tile = arrived[place[RECV_SLOT, i * TILES_X + j]]
            ext[FORCE_X, j, rows] = tile[0]
            ext[FORCE_Y, j, rows] = tile[1]
        return carry

    lax.fori_loop(0, ROWS // 8, forces, 0)
    gather_columns(FORCE_X, 2, force_to_east, force_to_west)
    for copy in force_cols:
        copy.start()
    rows_start(*strips(FORCE_X, 2, 0, TILES_X), 12)
    for copy in force_cols:
        copy.wait()
    spread_columns(FORCE_X, 2, force_from_west, force_from_east)
    rows_start(*strips(FORCE_X, 2, TILES_X, 1), 12)
    rows_wait(*force_rows, 12)

    @pl.when(top)
    def _():
        fold(ext, FORCE_X, 2, HALO + ROWS, (FORCE_X, FORCE_Y + 1))

    def arrange_forces(r, carry):
        rows = pl.ds(r, 8, stride=STEP)
        left, right = left_right([cstr[r + 1, j] for j in range(CT)], lane)
        for j in range(CT):
            kfx[r, j] = ext[FORCE_X, j, rows] - 0.25 * (right[j] - left[j])
            kfy[r, j] = ext[FORCE_Y, j, rows] - 0.25 * (cstr[r + 2, j] - cstr[r, j])
        return carry

    lax.fori_loop(0, STEP, arrange_forces, 0)

    def shifted(ref, r):
        def left(j):
            return pltpu.roll(jnp.where(lane == 127, ref[r, (j - 1) % CT], ref[r, j]), 1, 1)

        def right(j):
            return pltpu.roll(jnp.where(lane == 0, ref[r, (j + 1) % CT], ref[r, j]), 127, 1)

        return left, right

    def stresses(i, carry):
        for r in [i * UNROLL + h for h in range(UNROLL)]:
            u_left, u_right = shifted(cu, r + 1)
            v_left, v_right = shifted(cv, r + 1)
            for j in range(CT):
                ux = u_right(j) - u_left(j)
                vx = v_right(j) - v_left(j)
                uy = cu[r + 2, j] - cu[r, j]
                vy = cv[r + 2, j] - cv[r, j]
                div = ux + vy
                ten = ux - vy
                shr = uy + vx
                div2 = div + div
                w = ks[r, j] * lax.rsqrt(div2 * div2 + ten * ten + shr * shr + 16.0)
                div4 = div2 + div2
                cxx[r + 1, j] = KEEP * cxx[r + 1, j] + w * (div4 + ten)
                cyy[r + 1, j] = KEEP * cyy[r + 1, j] + w * (div4 - ten)
                csh[r + 1, j] = KEEP * csh[r + 1, j] + w * shr
        return carry

    def momentum(i, carry):
        for r in [i * UNROLL + h for h in range(UNROLL)]:
            xx_left, xx_right = shifted(cxx, r + 1)
            sh_left, sh_right = shifted(csh, r + 1)
            for j in range(CT):
                px = (xx_right(j) - xx_left(j)) + (csh[r + 2, j] - csh[r, j])
                py = (sh_right(j) - sh_left(j)) + (cyy[r + 2, j] - cyy[r, j])
                m = km[r, j]
                rx = m * cu[r + 1, j] + (px + kfx[r, j])
                ry = m * cv[r + 1, j] + (py + kfy[r, j])
                a = ka[r, j]
                b = kb[r, j]
                cu[r + 1, j] = a * rx + b * ry
                cv[r + 1, j] = a * ry - b * rx
        return carry

    carried = (cu, cv, cxx, cyy, csh)

    def to_grid_order(first, count):
        def body(r, carry):
            for f in range(first, first + count):
                for j in range(CT):
                    nat[f, j, pl.ds(r, 8, stride=STEP)] = carried[f][r + 1, j]
            return carry

        lax.fori_loop(0, STEP, body, 0)

    def from_grid_order(r, carry):
        for f, ref in enumerate(carried):
            for j in range(CT):
                ref[r + 1, j] = nat[f, j, pl.ds(r, 8, stride=STEP)]
        return carry

    state_rows = (nat.at[:, :, pl.ds(ROWS, HALO)], nat.at[:, :, pl.ds(HALO, HALO)], from_south, from_north)

    def take(strip, base):
        def body(j, carry):
            for f in range(5):
                for p in range(HALO // 8):
                    nat[f, j, pl.ds(base + p * 8, 8)] = strip[f, j, pl.ds(p * 8, 8)]
            return carry

        lax.fori_loop(0, CT, body, 0)

    def exchange_rows():
        for f in range(5):
            to_grid_order(f, 1)
            rows_start(
                nat.at[f, :, pl.ds(ROWS, HALO)], nat.at[f, :, pl.ds(HALO, HALO)],
                from_south.at[f], from_north.at[f], 16)
        rows_wait(*state_rows, 16)

        @pl.when(top)
        def _():
            fold(from_north, 0, 5, 0, (0, 2))

        take(from_north, HALO + ROWS)

        @pl.when(gy > 0)
        def _():
            take(from_south, 0)

        lax.fori_loop(0, STEP, from_grid_order, 0)
        ghosts(cu, cv)

    def subcycle(t, carry):
        pl.when(t == ITERS // LEGS)(exchange_rows)
        lax.fori_loop(0, STEP // UNROLL, stresses, 0)
        ghosts(cyy, csh)
        lax.fori_loop(0, STEP // UNROLL, momentum, 0)
        ghosts(cu, cv)
        return carry

    lax.fori_loop(0, ITERS, subcycle, 0)
    to_grid_order(0, 2)

    def to_tiles(i, carry):
        rows = aligned(HALO + i * 8)
        for j in range(TILES_X):
            tiles[i * TILES_X + j, 0] = nat[0, j, rows]
            tiles[i * TILES_X + j, 1] = nat[1, j, rows]
        return carry

    lax.fori_loop(0, ROWS // 8, to_tiles, 0)

    def pack_back(d):
        returning[d * 2] = tiles[place[EARLY, d]]
        returning[d * 2 + 1] = tiles[place[LATE, d]]

    def send_back(a, b):
        d = a * N_GY + b
        pack_back(d)
        pltpu.make_async_remote_copy(
            returning.at[pl.ds(d * 2, 2)], arrived_back.at[pl.ds(me * 2, 2)],
            a2a_sem.at[2], a2a_sem.at[3], device_id=(a, b), device_id_type=MESH,
        ).start()

    each_peer(send_back)
    pack_back(me)
    for h in range(2):
        arrived_back[me * 2 + h] = returning[me * 2 + h]
    to_grid_order(2, 3)

    def finish(i, carry):
        rows = aligned(HALO + i * 8)
        for j in range(TILES_X):
            xx = nat[2, j, rows]
            yy = nat[3, j, rows]
            final[0, j, aligned(i * 8)] = 2.0 * (xx + yy) - ext[STRENGTH, j, rows]
            final[1, j, aligned(i * 8)] = 2.0 * (xx - yy)
            final[2, j, aligned(i * 8)] = 2.0 * nat[4, j, rows]
        return carry

    lax.fori_loop(0, ROWS // 8, finish, 0)
    for j in range(TILES_X):
        pltpu.make_async_copy(final.at[:, j], out_stress.at[:, :, pl.ds(j * 128, 128)], in_sem.at[1]).start()

    wait_for(arrived_back.at[pl.ds(0, 2 * N_DEV - 2)], a2a_sem.at[3])
    wait_for(returning.at[pl.ds(0, 2 * N_DEV - 2)], a2a_sem.at[2])

    def unpack(i, carry):
        for h in range(8):
            out_velocity[i * 8 + h] = arrived_back[place[BACK_SLOT, i * 8 + h]]
        return carry

    lax.fori_loop(0, N_DEV // 8, unpack, 0)
    wait_for(final, in_sem.at[1])


def local(ocean_forcing, route, land_mask, mass, strength, velocity_start, stress_start):
    f32, i32 = jnp.float32, jnp.int32
    hbm = pl.BlockSpec(memory_space=pl.ANY)
    ghosted = pltpu.VMEM((STEP + 2, CT, 8, 128), f32)
    plain = pltpu.VMEM((STEP, CT, 8, 128), f32)
    side = pltpu.VMEM((STATIC // 4, ROWS, 128), f32)
    force_side = pltpu.VMEM((1, ROWS, 128), f32)
    strip = pltpu.VMEM((5, CT, HALO, 128), f32)
    return pl.pallas_call(
        kernel,
        out_shape=(
            jax.ShapeDtypeStruct((N_DEV, 2, 8, 128), f32),
            jax.ShapeDtypeStruct((3, ROWS, TILES_X * 128), f32),
        ),
        in_specs=[hbm] * 7,
        out_specs=(pl.BlockSpec(memory_space=pltpu.VMEM), hbm),
        scratch_shapes=[
            pltpu.VMEM((N_DEV, N_DEV), i32),
            pltpu.VMEM((8, N_DEV), i32),
            pltpu.SMEM((8, N_DEV), i32),
            pltpu.VMEM((N_DEV, 4, 8, 128), f32),
            pltpu.VMEM((N_DEV, 8, 128), f32),
            pltpu.VMEM((2 * N_DEV, 8, 128), f32),
            pltpu.VMEM((2 * N_DEV, 8, 128), f32),
            pltpu.VMEM((2 * N_DEV, 2, 8, 128), f32),
            pltpu.VMEM((2 * N_DEV, 2, 8, 128), f32),
            pltpu.VMEM((FIELDS, CT, EXT, 128), f32),
            pltpu.VMEM((TILES_X, ROWS, 128), i32),
            side, side, side, side,
            force_side, force_side, force_side, force_side,
            pltpu.VMEM((5, CT, EXT, 128), f32),
            strip, strip,
            pltpu.VMEM((3, TILES_X, ROWS, 128), f32),
            pltpu.VMEM((N_DEV, 2, 8, 128), f32),
            pltpu.VMEM((2 * N_DEV, 2, 8, 128), f32),
            pltpu.VMEM((2 * N_DEV, 2, 8, 128), f32),
            ghosted, ghosted, ghosted, ghosted, ghosted, ghosted,
            plain, plain, plain, plain, plain, plain,
            pltpu.SemaphoreType.DMA((6,)),
            pltpu.SemaphoreType.DMA((6,)),
            pltpu.SemaphoreType.DMA((20,)),
        ],
        compiler_params=pltpu.CompilerParams(
            collective_id=0, has_side_effects=True, vmem_limit_bytes=56 * 1024 * 1024),
    )(route.reshape(N_DEV, N_DEV), ocean_forcing, land_mask, mass, strength, velocity_start, stress_start)


def solution(mesh):
    placed = (
        P(("gx", "gy"), None, None, None),
        P(),
        P("gy", "gx"),
        P("gy", "gx"),
        P("gy", "gx"),
        P(None, "gy", "gx"),
        P(None, "gy", "gx"),
    )
    return jax.shard_map(
        local,
        mesh=mesh,
        in_specs=placed,
        out_specs=(P(("gx", "gy"), None, None, None), P(None, "gy", "gx")),
        check_vma=False,
    )
```

```python
import functools

import jax
import jax.numpy as jnp
from jax import lax
from jax.experimental import pallas as pl
from jax.experimental.pallas import tpu as pltpu
from jax.sharding import PartitionSpec as P

MESH = pl.DeviceIdType.MESH
ITERS = 16
RELAX = 0.1
DRAG = 0.5
TURN = 0.3
TILT = 0.05
KEEP = 1.0 / (1.0 + RELAX)

N_GX = 8
N_GY = 16
N_DEV = 128
LEGS = 2
HALO = 2 * ITERS // LEGS
SIDE = 2 * ITERS
ROWS = 128
EXT = ROWS + 2 * HALO
STEP = EXT // 8
TILES_X = 8
CT = TILES_X + 1
UNROLL = 20

MASS, STRENGTH, ZONAL, MERID, SUM, DIFF, SHEAR, SHARE, FORCE_X, FORCE_Y = range(10)
STATIC = 8
FIELDS = 10
FIRST, SECOND, BACK_SLOT, RECV_SLOT, EARLY, LATE = range(6)


def peers():
    order = []
    for n in range(32):
        j = (n * 13) % 32
        dx, dy, dc = j // 8, (j // 2) % 4, j % 2
        off = (n + n // 4 + 3 * dx + dy) % 4 if (dx, dy, dc) != (0, 0, 0) else 0
        order.append((dx, dy, dc, off))
    return order


def each_peer(visit, between=()):
    gx = lax.axis_index("gx")
    gy = lax.axis_index("gy")
    z, x_lo = gx % 4, gx // 4
    x_hi, y, core = gy // 8, (gy // 2) % 4, gy % 2
    x = x_hi * 2 + x_lo
    xs = [(x + d) % 4 for d in range(4)]
    part_gx = [(v % 2) * 4 for v in xs]
    part_gy = [(v // 2) * 8 for v in xs]
    ys = [((y + d) % 4) * 2 for d in range(4)]
    cores = [core, 1 - core]
    zs = tuple((z + d) % 4 for d in range(4))

    def turn(q, zs):
        for n, (dx, dy, dc, off) in enumerate(peers()):
            for i, extra in enumerate(between):
                if n == (2 * i + 1) * 16 // len(between):
                    extra(q)
            there = (part_gx[dx] + zs[off], part_gy[dx] + ys[dy] + cores[dc])
            if (dx, dy, dc) == (0, 0, 0):
                pl.when(q > 0)(functools.partial(visit, *there))
            else:
                visit(*there)
        return zs[1:] + zs[:1]

    lax.fori_loop(0, 4, turn, zs)


def wait_for(ref, sem):
    pltpu.make_async_copy(ref, ref, sem).wait()


def aligned(start, size=8):
    return pl.ds(pl.multiple_of(start, 8), size)


def left_right(row, lane):
    n = len(row)
    left = [pltpu.roll(jnp.where(lane == 127, row[j - 1], row[j]), 1, 1) for j in range(n)]
    right = [pltpu.roll(jnp.where(lane == 0, row[(j + 1) % n], row[j]), 127, 1) for j in range(n)]
    return left, right


def fill_table(route, table, me):
    shape = (N_DEV, N_DEV)
    sub = lax.broadcasted_iota(jnp.int32, shape, 0)
    lane = lax.broadcasted_iota(jnp.int32, shape, 1)
    diagonal = sub == lane

    def to_column(row):
        return jnp.sum(jnp.where(diagonal, row, 0), axis=1, keepdims=True)

    def to_row(column):
        return jnp.sum(jnp.where(diagonal, column, 0), axis=0, keepdims=True)

    mine = jnp.right_shift(route[pl.ds(me, 1), :], 7)
    column = to_column(mine)
    hit = column == lane
    table[pl.ds(FIRST, 1), :] = jnp.min(jnp.where(hit, sub, N_DEV - 1), axis=0, keepdims=True)
    table[pl.ds(SECOND, 1), :] = jnp.max(jnp.where(hit, sub, 0), axis=0, keepdims=True)
    rank = jnp.max(jnp.where((column == mine) & (sub < lane), 1, 0), axis=0, keepdims=True)
    table[pl.ds(BACK_SLOT, 1), :] = mine * 2 + rank
    ids = route[...]
    here = jnp.right_shift(ids, 7) == me
    inside = jnp.bitwise_and(ids, N_DEV - 1)
    first = jnp.min(jnp.where(here, lane, N_DEV), axis=1, keepdims=True)
    second = jnp.max(jnp.where(here, lane, -1), axis=1, keepdims=True)
    early = jnp.sum(jnp.where(lane == first, inside + 1, 0), axis=1, keepdims=True) - 1
    late = jnp.sum(jnp.where(lane == second, inside + 1, 0), axis=1, keepdims=True) - 1
    slot = jnp.where(late == lane, 2 * sub + 1, jnp.where(early == lane, 2 * sub, 0))
    table[pl.ds(RECV_SLOT, 1), :] = jnp.max(slot, axis=0, keepdims=True)
    table[pl.ds(EARLY, 1), :] = to_row(jnp.maximum(early, 0))
    table[pl.ds(LATE, 1), :] = to_row(jnp.maximum(late, 0))
    table[pl.ds(6, 2), :] = jnp.zeros((2, N_DEV), jnp.int32)


def kernel(
    route, ocean, mask, mass, strength, velocity, stress,
    out_velocity, out_stress,
    routes, table, place, oc, mass_tiles, mass_out, mass_in, outgoing, arrived, ext, ext_mask,
    to_east, to_west, from_west, from_east, force_to_east, force_to_west, force_from_west, force_from_east,
    nat, from_south, from_north, final, tiles, returning, arrived_back,
    cu, cv, cxx, cyy, csh, cstr, ks, km, kfx, kfy, ka, kb,
    in_sem, a2a_sem, halo_sem,
):
    gx = lax.axis_index("gx")
    gy = lax.axis_index("gy")
    me = gx * N_GY + gy
    top = gy == N_GY - 1
    inner = pl.ds(HALO, ROWS)
    lane = lax.broadcasted_iota(jnp.int32, (8, 128), 1)

    pltpu.make_async_copy(route, routes, in_sem.at[3]).start()
    for j in range(TILES_X):
        pltpu.make_async_copy(mass.at[:, pl.ds(j * 128, 128)], ext.at[MASS, j, inner], in_sem.at[5]).start()
    for j in range(TILES_X):
        cols = pl.ds(j * 128, 128)
        pltpu.make_async_copy(strength.at[:, cols], ext.at[STRENGTH, j, inner], in_sem.at[1]).start()
        pltpu.make_async_copy(velocity.at[:, :, cols], ext.at[pl.ds(ZONAL, 2), j, inner], in_sem.at[1]).start()
        pltpu.make_async_copy(stress.at[:, :, cols], ext.at[pl.ds(SUM, 3), j, inner], in_sem.at[1]).start()
        pltpu.make_async_copy(mask.at[:, cols], ext_mask.at[j], in_sem.at[2]).start()

    pltpu.make_async_copy(ocean, oc, in_sem.at[0]).start()
    barrier = pltpu.get_barrier_semaphore()

    def greet(a, b):
        pl.semaphore_signal(barrier, inc=1, device_id=(a, b), device_id_type=MESH)

    each_peer(greet)

    wait_for(routes, in_sem.at[3])
    fill_table(routes, table, me)
    to_place = pltpu.make_async_copy(table, place, in_sem.at[4])
    to_place.start()

    wait_for(ext.at[MASS, pl.ds(0, TILES_X), inner], in_sem.at[5])

    def to_mass_tiles(i, carry):
        for j in range(TILES_X):
            mass_tiles[i * TILES_X + j] = ext[MASS, j, aligned(HALO + i * 8)]
        return carry

    lax.fori_loop(0, ROWS // 8, to_mass_tiles, 0)
    to_place.wait()

    def pack_mass(i, carry):
        for h in range(8):
            mass_out[i * 16 + 2 * h] = mass_tiles[place[EARLY, i * 8 + h]]
            mass_out[i * 16 + 2 * h + 1] = mass_tiles[place[LATE, i * 8 + h]]
        return carry

    lax.fori_loop(0, N_DEV // 8, pack_mass, 0)

    wait_for(ext.at[pl.ds(STRENGTH, STATIC - 2), pl.ds(0, TILES_X), inner], in_sem.at[1])

    def gather_columns(first, count, east_out, west_out):
        def body(i, carry):
            rows = aligned(HALO + i * 8)
            for g in range((count + 3) // 4):
                e = w = None
                for q in range(min(4, count - 4 * g)):
                    f = first + 4 * g + q
                    a = pltpu.roll(ext[f, TILES_X - 1, rows], (SIDE * (q + 1)) % 128, 1)
                    b = ext[f, 0, rows]
                    if q:
                        b = pltpu.roll(b, SIDE * q, 1)
                    e = a if q == 0 else jnp.where(lane < SIDE * q, e, a)
                    w = b if q == 0 else jnp.where(lane < SIDE * q, w, b)
                east_out[g, aligned(i * 8)] = e
                west_out[g, aligned(i * 8)] = w
            return carry

        lax.fori_loop(0, ROWS // 8, body, 0)

    def spread_columns(first, count, west_in, east_in):
        def body(i, carry):
            rows = aligned(HALO + i * 8)
            for g in range((count + 3) // 4):
                e = east_in[g, aligned(i * 8)]
                w = west_in[g, aligned(i * 8)]
                for q in range(min(4, count - 4 * g)):
                    right = pltpu.roll(e, 128 - SIDE * q, 1) if q else e
                    left = pltpu.roll(w, 128 - SIDE * (q + 1), 1) if q < 3 else w
                    ext[first + 4 * g + q, TILES_X, rows] = jnp.where(lane < 64, right, left)
            return carry

        lax.fori_loop(0, ROWS // 8, body, 0)

    def columns(east_out, west_out, west_in, east_in, sems):
        a = pltpu.make_async_remote_copy(
            east_out, west_in, halo_sem.at[sems], halo_sem.at[sems + 1],
            device_id=((gx + 1) % N_GX, gy), device_id_type=MESH)
        b = pltpu.make_async_remote_copy(
            west_out, east_in, halo_sem.at[sems + 2], halo_sem.at[sems + 3],
            device_id=((gx + N_GX - 1) % N_GX, gy), device_id_type=MESH)
        return a, b

    north_gy = jnp.minimum(gy + 1, N_GY - 1)
    south_gy = jnp.maximum(gy - 1, 0)

    def rows_north(upper, lower, south, north, sems):
        to_north = pltpu.make_async_remote_copy(
            upper, south, halo_sem.at[sems], halo_sem.at[sems + 1],
            device_id=(gx, north_gy), device_id_type=MESH)
        to_partner = pltpu.make_async_remote_copy(
            upper, north, halo_sem.at[sems], halo_sem.at[sems + 3],
            device_id=(N_GX - 1 - gx, gy), device_id_type=MESH)
        pl.when(jnp.logical_not(top))(to_north.start)
        pl.when(top)(to_partner.start)

    def rows_south(upper, lower, south, north, sems):
        to_south = pltpu.make_async_remote_copy(
            lower, north, halo_sem.at[sems + 2], halo_sem.at[sems + 3],
            device_id=(gx, south_gy), device_id_type=MESH)
        pl.when(gy > 0)(to_south.start)

    def rows_start(*args):
        rows_north(*args)
        rows_south(*args)

    def rows_wait(upper, lower, south, north, sems):
        wait_for(north, halo_sem.at[sems + 3])
        wait_for(upper, halo_sem.at[sems])

        @pl.when(gy > 0)
        def _():
            wait_for(south, halo_sem.at[sems + 1])
            wait_for(lower, halo_sem.at[sems + 2])

    def strips(first, count, tile=0, tiles=CT):
        return tuple(
            ext.at[pl.ds(first, count), pl.ds(tile, tiles), pl.ds(at, HALO)]
            for at in (ROWS, HALO, 0, HALO + ROWS))

    back_sub = 7 - lax.broadcasted_iota(jnp.int32, (8, 128), 0)
    back_lane = 127 - lane

    def turned(x):
        x = jnp.take_along_axis(x, back_lane, axis=1)
        return jnp.take_along_axis(x, back_sub, axis=0)

    def fold(ref, first, count, base, odd):
        tall = HALO // 8

        def body(f, carry):
            sign = jnp.where((f >= odd[0]) & (f < odd[1]), -1.0, 1.0)
            for j in range(TILES_X // 2 + 1):
                pair = (j, TILES_X - 1 - j) if j < TILES_X // 2 else (TILES_X,)
                old = [[ref[f, c, pl.ds(base + p * 8, 8)] for c in pair] for p in range(tall)]
                for p in range(tall):
                    for n, c in enumerate(pair):
                        ref[f, c, pl.ds(base + p * 8, 8)] = turned(old[tall - 1 - p][len(pair) - 1 - n]) * sign
            return carry

        lax.fori_loop(first, first + count, body, 0)

    static_cols = columns(to_east, to_west, from_west, from_east, 0)
    force_cols = columns(force_to_east, force_to_west, force_from_west, force_from_east, 4)
    static_rows = strips(0, STATIC)
    force_rows = strips(FORCE_X, 2)

    pl.semaphore_wait(barrier, N_DEV - 1)

    def send_mass(a, b):
        pltpu.make_async_remote_copy(
            mass_out.at[pl.ds((a * N_GY + b) * 2, 2)], mass_in.at[pl.ds(me * 2, 2)],
            a2a_sem.at[4], a2a_sem.at[5], device_id=(a, b), device_id_type=MESH,
        ).start()

    def pack_forces(d):
        for h in range(2):
            tile = oc[place[FIRST + h, d]]
            m = TILT * mass_in[d * 2 + h]
            outgoing[d * 2 + h, 0] = tile[0] + m * tile[2]
            outgoing[d * 2 + h, 1] = tile[1] + m * tile[3]

    def send_forces(a, b):
        d = a * N_GY + b
        pack_forces(d)
        pltpu.make_async_remote_copy(
            outgoing.at[pl.ds(d * 2, 2)], arrived.at[pl.ds(me * 2, 2)],
            a2a_sem.at[0], a2a_sem.at[1], device_id=(a, b), device_id_type=MESH,
        ).start()

    each_peer(send_mass, (
        lambda q: rows_north(*strips(q, 1, 0, TILES_X), 8),
        lambda q: rows_south(*strips(q, 1, 0, TILES_X), 8),
    ))
    for h in range(2):
        mass_in[me * 2 + h] = mass_out[me * 2 + h]
    wait_for(ext_mask, in_sem.at[2])

    def shares(i, carry):
        for j in range(TILES_X):
            ext[SHARE, j, aligned(HALO + i * 8)] = ext_mask[j, aligned(i * 8)].astype(jnp.float32)
        return carry

    lax.fori_loop(0, ROWS // 8, shares, 0)
    gather_columns(0, STATIC, to_east, to_west)
    for copy in static_cols:
        copy.start()
    for copy in static_cols:
        copy.wait()
    spread_columns(0, STATIC, from_west, from_east)

    wait_for(oc, in_sem.at[0])
    wait_for(mass_in.at[pl.ds(0, 2 * N_DEV - 2)], a2a_sem.at[5])
    rows_start(*strips(0, STATIC, TILES_X, 1), 8)
    each_peer(send_forces, (
        lambda q: rows_north(*strips(4 + q, 1, 0, TILES_X), 8),
        lambda q: rows_south(*strips(4 + q, 1, 0, TILES_X), 8),
    ))
    pack_forces(me)
    for h in range(2):
        arrived[me * 2 + h] = outgoing[me * 2 + h]
    wait_for(mass_out.at[pl.ds(0, 2 * N_DEV - 2)], a2a_sem.at[4])

    @pl.when(gy == 0)
    def _():
        zero = jnp.zeros((8, 128), jnp.float32)

        def clear(j, carry):
            for p in range(HALO // 8):
                for f in range(FIELDS):
                    ext[f, j, pl.ds(p * 8, 8)] = zero + 1.0 if f == MASS else zero
            return carry

        lax.fori_loop(0, CT, clear, 0)

    rows_wait(*static_rows, 8)

    @pl.when(top)
    def _():
        fold(ext, 0, STATIC, HALO + ROWS, (ZONAL, MERID + 1))

    def arrange(r, carry):
        rows = pl.ds(r, 8, stride=STEP)
        for j in range(CT):
            share = ext[SHARE, j, rows]
            m = ext[MASS, j, rows]
            strong = ext[STRENGTH, j, rows]
            a = m + DRAG
            b = TURN * m
            scale = share / (a * a + b * b)
            km[r, j] = m
            ka[r, j] = a * scale
            kb[r, j] = b * scale
            ks[r, j] = (0.0125 * KEEP) * strong
            cstr[r + 1, j] = strong
            cu[r + 1, j] = ext[ZONAL, j, rows] * share
            cv[r + 1, j] = ext[MERID, j, rows] * share
            both = 0.25 * (ext[SUM, j, rows] + strong)
            apart = 0.25 * ext[DIFF, j, rows]
            cxx[r + 1, j] = both + apart
            cyy[r + 1, j] = both - apart
            csh[r + 1, j] = 0.5 * ext[SHEAR, j, rows]
        return carry

    lax.fori_loop(0, STEP, arrange, 0)

    def ghosts(*refs):
        for ref in refs:
            for j in range(CT):
                ref[0, j] = pltpu.roll(ref[STEP, j], 1, 0)
                ref[STEP + 1, j] = pltpu.roll(ref[1, j], 7, 0)

    ghosts(cu, cv, cstr)

    wait_for(arrived.at[pl.ds(0, 2 * N_DEV - 2)], a2a_sem.at[1])
    wait_for(outgoing.at[pl.ds(0, 2 * N_DEV - 2)], a2a_sem.at[0])

    def forces(i, carry):
        rows = aligned(HALO + i * 8)
        for j in range(TILES_X):
            tile = arrived[place[RECV_SLOT, i * TILES_X + j]]
            ext[FORCE_X, j, rows] = tile[0]
            ext[FORCE_Y, j, rows] = tile[1]
        return carry

    lax.fori_loop(0, ROWS // 8, forces, 0)
    gather_columns(FORCE_X, 2, force_to_east, force_to_west)
    for copy in force_cols:
        copy.start()
    rows_start(*strips(FORCE_X, 2, 0, TILES_X), 12)
    for copy in force_cols:
        copy.wait()
    spread_columns(FORCE_X, 2, force_from_west, force_from_east)
    rows_start(*strips(FORCE_X, 2, TILES_X, 1), 12)
    rows_wait(*force_rows, 12)

    @pl.when(top)
    def _():
        fold(ext, FORCE_X, 2, HALO + ROWS, (FORCE_X, FORCE_Y + 1))

    def arrange_forces(r, carry):
        rows = pl.ds(r, 8, stride=STEP)
        left, right = left_right([cstr[r + 1, j] for j in range(CT)], lane)
        for j in range(CT):
            kfx[r, j] = ext[FORCE_X, j, rows] - 0.25 * (right[j] - left[j])
            kfy[r, j] = ext[FORCE_Y, j, rows] - 0.25 * (cstr[r + 2, j] - cstr[r, j])
        return carry

    lax.fori_loop(0, STEP, arrange_forces, 0)

    def shifted(ref, r):
        def left(j):
            return pltpu.roll(jnp.where(lane == 127, ref[r, (j - 1) % CT], ref[r, j]), 1, 1)

        def right(j):
            return pltpu.roll(jnp.where(lane == 0, ref[r, (j + 1) % CT], ref[r, j]), 127, 1)

        return left, right

    def stresses(i, carry):
        for r in [i * UNROLL + h for h in range(UNROLL)]:
            u_left, u_right = shifted(cu, r + 1)
            v_left, v_right = shifted(cv, r + 1)
            for j in range(CT):
                ux = u_right(j) - u_left(j)
                vx = v_right(j) - v_left(j)
                uy = cu[r + 2, j] - cu[r, j]
                vy = cv[r + 2, j] - cv[r, j]
                div = ux + vy
                ten = ux - vy
                shr = uy + vx
                div2 = div + div
                w = ks[r, j] * lax.rsqrt(div2 * div2 + ten * ten + shr * shr + 16.0)
                div4 = div2 + div2
                cxx[r + 1, j] = KEEP * cxx[r + 1, j] + w * (div4 + ten)
                cyy[r + 1, j] = KEEP * cyy[r + 1, j] + w * (div4 - ten)
                csh[r + 1, j] = KEEP * csh[r + 1, j] + w * shr
        return carry

    def momentum(i, carry):
        for r in [i * UNROLL + h for h in range(UNROLL)]:
            xx_left, xx_right = shifted(cxx, r + 1)
            sh_left, sh_right = shifted(csh, r + 1)
            for j in range(CT):
                px = (xx_right(j) - xx_left(j)) + (csh[r + 2, j] - csh[r, j])
                py = (sh_right(j) - sh_left(j)) + (cyy[r + 2, j] - cyy[r, j])
                m = km[r, j]
                rx = m * cu[r + 1, j] + (px + kfx[r, j])
                ry = m * cv[r + 1, j] + (py + kfy[r, j])
                a = ka[r, j]
                b = kb[r, j]
                cu[r + 1, j] = a * rx + b * ry
                cv[r + 1, j] = a * ry - b * rx
        return carry

    carried = (cu, cv, cxx, cyy, csh)

    def to_grid_order(first, count):
        def body(r, carry):
            for f in range(first, first + count):
                for j in range(CT):
                    nat[f, j, pl.ds(r, 8, stride=STEP)] = carried[f][r + 1, j]
            return carry

        lax.fori_loop(0, STEP, body, 0)

    def from_grid_order(r, carry):
        for f, ref in enumerate(carried):
            for j in range(CT):
                ref[r + 1, j] = nat[f, j, pl.ds(r, 8, stride=STEP)]
        return carry

    state_rows = (nat.at[:, :, pl.ds(ROWS, HALO)], nat.at[:, :, pl.ds(HALO, HALO)], from_south, from_north)

    def take(strip, base):
        def body(j, carry):
            for f in range(5):
                for p in range(HALO // 8):
                    nat[f, j, pl.ds(base + p * 8, 8)] = strip[f, j, pl.ds(p * 8, 8)]
            return carry

        lax.fori_loop(0, CT, body, 0)

    def exchange_rows():
        for f in range(5):
            to_grid_order(f, 1)
            rows_start(
                nat.at[f, :, pl.ds(ROWS, HALO)], nat.at[f, :, pl.ds(HALO, HALO)],
                from_south.at[f], from_north.at[f], 16)
        rows_wait(*state_rows, 16)

        @pl.when(top)
        def _():
            fold(from_north, 0, 5, 0, (0, 2))

        take(from_north, HALO + ROWS)

        @pl.when(gy > 0)
        def _():
            take(from_south, 0)

        lax.fori_loop(0, STEP, from_grid_order, 0)
        ghosts(cu, cv)

    def subcycle(t, carry):
        pl.when(t == ITERS // LEGS)(exchange_rows)
        lax.fori_loop(0, STEP // UNROLL, stresses, 0)
        ghosts(cyy, csh)
        lax.fori_loop(0, STEP // UNROLL, momentum, 0)
        ghosts(cu, cv)
        return carry

    lax.fori_loop(0, ITERS, subcycle, 0)
    to_grid_order(0, 2)

    def to_tiles(i, carry):
        rows = aligned(HALO + i * 8)
        for j in range(TILES_X):
            tiles[i * TILES_X + j, 0] = nat[0, j, rows]
            tiles[i * TILES_X + j, 1] = nat[1, j, rows]
        return carry

    lax.fori_loop(0, ROWS // 8, to_tiles, 0)

    def pack_back(d):
        returning[d * 2] = tiles[place[EARLY, d]]
        returning[d * 2 + 1] = tiles[place[LATE, d]]

    def send_back(a, b):
        d = a * N_GY + b
        pack_back(d)
        pltpu.make_async_remote_copy(
            returning.at[pl.ds(d * 2, 2)], arrived_back.at[pl.ds(me * 2, 2)],
            a2a_sem.at[2], a2a_sem.at[3], device_id=(a, b), device_id_type=MESH,
        ).start()

    each_peer(send_back)
    pack_back(me)
    for h in range(2):
        arrived_back[me * 2 + h] = returning[me * 2 + h]
    to_grid_order(2, 3)

    def finish(i, carry):
        rows = aligned(HALO + i * 8)
        for j in range(TILES_X):
            xx = nat[2, j, rows]
            yy = nat[3, j, rows]
            final[0, j, aligned(i * 8)] = 2.0 * (xx + yy) - ext[STRENGTH, j, rows]
            final[1, j, aligned(i * 8)] = 2.0 * (xx - yy)
            final[2, j, aligned(i * 8)] = 2.0 * nat[4, j, rows]
        return carry

    lax.fori_loop(0, ROWS // 8, finish, 0)
    for j in range(TILES_X):
        pltpu.make_async_copy(final.at[:, j], out_stress.at[:, :, pl.ds(j * 128, 128)], in_sem.at[1]).start()

    wait_for(arrived_back.at[pl.ds(0, 2 * N_DEV - 2)], a2a_sem.at[3])
    wait_for(returning.at[pl.ds(0, 2 * N_DEV - 2)], a2a_sem.at[2])

    def unpack(i, carry):
        for h in range(8):
            out_velocity[i * 8 + h] = arrived_back[place[BACK_SLOT, i * 8 + h]]
        return carry

    lax.fori_loop(0, N_DEV // 8, unpack, 0)
    wait_for(final, in_sem.at[1])


def local(ocean_forcing, route, land_mask, mass, strength, velocity_start, stress_start):
    f32, i32 = jnp.float32, jnp.int32
    hbm = pl.BlockSpec(memory_space=pl.ANY)
    ghosted = pltpu.VMEM((STEP + 2, CT, 8, 128), f32)
    plain = pltpu.VMEM((STEP, CT, 8, 128), f32)
    side = pltpu.VMEM((STATIC // 4, ROWS, 128), f32)
    force_side = pltpu.VMEM((1, ROWS, 128), f32)
    strip = pltpu.VMEM((5, CT, HALO, 128), f32)
    return pl.pallas_call(
        kernel,
        out_shape=(
            jax.ShapeDtypeStruct((N_DEV, 2, 8, 128), f32),
            jax.ShapeDtypeStruct((3, ROWS, TILES_X * 128), f32),
        ),
        in_specs=[hbm] * 7,
        out_specs=(pl.BlockSpec(memory_space=pltpu.VMEM), hbm),
        scratch_shapes=[
            pltpu.VMEM((N_DEV, N_DEV), i32),
            pltpu.VMEM((8, N_DEV), i32),
            pltpu.SMEM((8, N_DEV), i32),
            pltpu.VMEM((N_DEV, 4, 8, 128), f32),
            pltpu.VMEM((N_DEV, 8, 128), f32),
            pltpu.VMEM((2 * N_DEV, 8, 128), f32),
            pltpu.VMEM((2 * N_DEV, 8, 128), f32),
            pltpu.VMEM((2 * N_DEV, 2, 8, 128), f32),
            pltpu.VMEM((2 * N_DEV, 2, 8, 128), f32),
            pltpu.VMEM((FIELDS, CT, EXT, 128), f32),
            pltpu.VMEM((TILES_X, ROWS, 128), i32),
            side, side, side, side,
            force_side, force_side, force_side, force_side,
            pltpu.VMEM((5, CT, EXT, 128), f32),
            strip, strip,
            pltpu.VMEM((3, TILES_X, ROWS, 128), f32),
            pltpu.VMEM((N_DEV, 2, 8, 128), f32),
            pltpu.VMEM((2 * N_DEV, 2, 8, 128), f32),
            pltpu.VMEM((2 * N_DEV, 2, 8, 128), f32),
            ghosted, ghosted, ghosted, ghosted, ghosted, ghosted,
            plain, plain, plain, plain, plain, plain,
            pltpu.SemaphoreType.DMA((6,)),
            pltpu.SemaphoreType.DMA((6,)),
            pltpu.SemaphoreType.DMA((20,)),
        ],
        compiler_params=pltpu.CompilerParams(
            collective_id=0, has_side_effects=True, vmem_limit_bytes=56 * 1024 * 1024),
    )(route.reshape(N_DEV, N_DEV), ocean_forcing, land_mask, mass, strength, velocity_start, stress_start)


def solution(mesh):
    placed = (
        P(("gx", "gy"), None, None, None),
        P(),
        P("gy", "gx"),
        P("gy", "gx"),
        P("gy", "gx"),
        P(None, "gy", "gx"),
        P(None, "gy", "gx"),
    )
    return jax.shard_map(
        local,
        mesh=mesh,
        in_specs=placed,
        out_specs=(P(("gx", "gy"), None, None, None), P(None, "gy", "gx")),
        check_vma=False,
    )
```

```python
import functools

import jax
import jax.numpy as jnp
from jax import lax
from jax.experimental import pallas as pl
from jax.experimental.pallas import tpu as pltpu
from jax.sharding import PartitionSpec as P

MESH = pl.DeviceIdType.MESH
ITERS = 16
RELAX = 0.1
DRAG = 0.5
TURN = 0.3
TILT = 0.05
KEEP = 1.0 / (1.0 + RELAX)

N_GX = 8
N_GY = 16
N_DEV = 128
LEGS = 2
HALO = 2 * ITERS // LEGS
SIDE = 2 * ITERS
ROWS = 128
EXT = ROWS + 2 * HALO
STEP = EXT // 8
TILES_X = 8
CT = TILES_X + 1
UNROLL = 20

MASS, STRENGTH, ZONAL, MERID, SUM, DIFF, SHEAR, SHARE, FORCE_X, FORCE_Y = range(10)
STATIC = 8
FIELDS = 10
FIRST, SECOND, BACK_SLOT, RECV_SLOT, EARLY, LATE = range(6)


def peers():
    order = []
    for n in range(32):
        j = (n * 13) % 32
        dx, dy, dc = j // 8, (j // 2) % 4, j % 2
        off = (n + n // 4 + 3 * dx + dy) % 4 if (dx, dy, dc) != (0, 0, 0) else 0
        order.append((dx, dy, dc, off))
    return order


def each_peer(visit, between=()):
    gx = lax.axis_index("gx")
    gy = lax.axis_index("gy")
    z, x_lo = gx % 4, gx // 4
    x_hi, y, core = gy // 8, (gy // 2) % 4, gy % 2
    x = x_hi * 2 + x_lo
    xs = [(x + d) % 4 for d in range(4)]
    part_gx = [(v % 2) * 4 for v in xs]
    part_gy = [(v // 2) * 8 for v in xs]
    ys = [((y + d) % 4) * 2 for d in range(4)]
    cores = [core, 1 - core]
    zs = tuple((z + d) % 4 for d in range(4))

    def turn(q, zs):
        for n, (dx, dy, dc, off) in enumerate(peers()):
            for i, extra in enumerate(between):
                if n == (2 * i + 1) * 16 // len(between):
                    extra(q)
            there = (part_gx[dx] + zs[off], part_gy[dx] + ys[dy] + cores[dc])
            if (dx, dy, dc) == (0, 0, 0):
                pl.when(q > 0)(functools.partial(visit, *there))
            else:
                visit(*there)
        return zs[1:] + zs[:1]

    lax.fori_loop(0, 4, turn, zs)


def wait_for(ref, sem):
    pltpu.make_async_copy(ref, ref, sem).wait()


def aligned(start, size=8):
    return pl.ds(pl.multiple_of(start, 8), size)


def left_right(row, lane):
    n = len(row)
    left = [pltpu.roll(jnp.where(lane == 127, row[j - 1], row[j]), 1, 1) for j in range(n)]
    right = [pltpu.roll(jnp.where(lane == 0, row[(j + 1) % n], row[j]), 127, 1) for j in range(n)]
    return left, right


def fill_table(route, table, me):
    shape = (N_DEV, N_DEV)
    sub = lax.broadcasted_iota(jnp.int32, shape, 0)
    lane = lax.broadcasted_iota(jnp.int32, shape, 1)
    diagonal = sub == lane

    def to_column(row):
        return jnp.sum(jnp.where(diagonal, row, 0), axis=1, keepdims=True)

    def to_row(column):
        return jnp.sum(jnp.where(diagonal, column, 0), axis=0, keepdims=True)

    mine = jnp.right_shift(route[pl.ds(me, 1), :], 7)
    column = to_column(mine)
    hit = column == lane
    table[pl.ds(FIRST, 1), :] = jnp.min(jnp.where(hit, sub, N_DEV - 1), axis=0, keepdims=True)
    table[pl.ds(SECOND, 1), :] = jnp.max(jnp.where(hit, sub, 0), axis=0, keepdims=True)
    rank = jnp.max(jnp.where((column == mine) & (sub < lane), 1, 0), axis=0, keepdims=True)
    table[pl.ds(BACK_SLOT, 1), :] = mine * 2 + rank
    ids = route[...]
    here = jnp.right_shift(ids, 7) == me
    inside = jnp.bitwise_and(ids, N_DEV - 1)
    first = jnp.min(jnp.where(here, lane, N_DEV), axis=1, keepdims=True)
    second = jnp.max(jnp.where(here, lane, -1), axis=1, keepdims=True)
    early = jnp.sum(jnp.where(lane == first, inside + 1, 0), axis=1, keepdims=True) - 1
    late = jnp.sum(jnp.where(lane == second, inside + 1, 0), axis=1, keepdims=True) - 1
    slot = jnp.where(late == lane, 2 * sub + 1, jnp.where(early == lane, 2 * sub, 0))
    table[pl.ds(RECV_SLOT, 1), :] = jnp.max(slot, axis=0, keepdims=True)
    table[pl.ds(EARLY, 1), :] = to_row(jnp.maximum(early, 0))
    table[pl.ds(LATE, 1), :] = to_row(jnp.maximum(late, 0))
    table[pl.ds(6, 2), :] = jnp.zeros((2, N_DEV), jnp.int32)


def kernel(
    route, ocean, mask, mass, strength, velocity, stress,
    out_velocity, out_stress,
    routes, table, place, oc, mass_tiles, mass_out, mass_in, outgoing, arrived, ext, ext_mask,
    to_east, to_west, from_west, from_east, force_to_east, force_to_west, force_from_west, force_from_east,
    nat, from_south, from_north, final, tiles, returning, arrived_back,
    cu, cv, cxx, cyy, csh, cstr, ks, km, kfx, kfy, ka, kb,
    in_sem, a2a_sem, halo_sem,
):
    gx = lax.axis_index("gx")
    gy = lax.axis_index("gy")
    me = gx * N_GY + gy
    top = gy == N_GY - 1
    inner = pl.ds(HALO, ROWS)
    lane = lax.broadcasted_iota(jnp.int32, (8, 128), 1)

    pltpu.make_async_copy(route, routes, in_sem.at[3]).start()
    for j in range(TILES_X):
        pltpu.make_async_copy(mass.at[:, pl.ds(j * 128, 128)], ext.at[MASS, j, inner], in_sem.at[5]).start()
    for j in range(TILES_X):
        cols = pl.ds(j * 128, 128)
        pltpu.make_async_copy(strength.at[:, cols], ext.at[STRENGTH, j, inner], in_sem.at[1]).start()
        pltpu.make_async_copy(velocity.at[:, :, cols], ext.at[pl.ds(ZONAL, 2), j, inner], in_sem.at[1]).start()
        pltpu.make_async_copy(stress.at[:, :, cols], ext.at[pl.ds(SUM, 3), j, inner], in_sem.at[1]).start()
        pltpu.make_async_copy(mask.at[:, cols], ext_mask.at[j], in_sem.at[2]).start()

    pltpu.make_async_copy(ocean, oc, in_sem.at[0]).start()
    barrier = pltpu.get_barrier_semaphore()

    def greet(a, b):
        pl.semaphore_signal(barrier, inc=1, device_id=(a, b), device_id_type=MESH)

    each_peer(greet)

    wait_for(routes, in_sem.at[3])
    fill_table(routes, table, me)
    to_place = pltpu.make_async_copy(table, place, in_sem.at[4])
    to_place.start()

    wait_for(ext.at[MASS, pl.ds(0, TILES_X), inner], in_sem.at[5])

    def to_mass_tiles(i, carry):
        for j in range(TILES_X):
            mass_tiles[i * TILES_X + j] = ext[MASS, j, aligned(HALO + i * 8)]
        return carry

    lax.fori_loop(0, ROWS // 8, to_mass_tiles, 0)
    to_place.wait()

    def pack_mass(i, carry):
        for h in range(8):
            mass_out[i * 16 + 2 * h] = mass_tiles[place[EARLY, i * 8 + h]]
            mass_out[i * 16 + 2 * h + 1] = mass_tiles[place[LATE, i * 8 + h]]
        return carry

    lax.fori_loop(0, N_DEV // 8, pack_mass, 0)

    wait_for(ext_mask, in_sem.at[2])

    def shares(i, carry):
        for j in range(TILES_X):
            ext[SHARE, j, aligned(HALO + i * 8)] = ext_mask[j, aligned(i * 8)].astype(jnp.float32)
        return carry

    lax.fori_loop(0, ROWS // 8, shares, 0)

    wait_for(ext.at[pl.ds(STRENGTH, STATIC - 2), pl.ds(0, TILES_X), inner], in_sem.at[1])

    def gather_columns(first, count, east_out, west_out):
        def body(i, carry):
            rows = aligned(HALO + i * 8)
            for g in range((count + 3) // 4):
                e = w = None
                for q in range(min(4, count - 4 * g)):
                    f = first + 4 * g + q
                    a = pltpu.roll(ext[f, TILES_X - 1, rows], (SIDE * (q + 1)) % 128, 1)
                    b = ext[f, 0, rows]
                    if q:
                        b = pltpu.roll(b, SIDE * q, 1)
                    e = a if q == 0 else jnp.where(lane < SIDE * q, e, a)
                    w = b if q == 0 else jnp.where(lane < SIDE * q, w, b)
                east_out[g, aligned(i * 8)] = e
                west_out[g, aligned(i * 8)] = w
            return carry

        lax.fori_loop(0, ROWS // 8, body, 0)

    def spread_columns(first, count, west_in, east_in):
        def body(i, carry):
            rows = aligned(HALO + i * 8)
            for g in range((count + 3) // 4):
                e = east_in[g, aligned(i * 8)]
                w = west_in[g, aligned(i * 8)]
                for q in range(min(4, count - 4 * g)):
                    right = pltpu.roll(e, 128 - SIDE * q, 1) if q else e
                    left = pltpu.roll(w, 128 - SIDE * (q + 1), 1) if q < 3 else w
                    ext[first + 4 * g + q, TILES_X, rows] = jnp.where(lane < 64, right, left)
            return carry

        lax.fori_loop(0, ROWS // 8, body, 0)

    def columns(east_out, west_out, west_in, east_in, sems):
        a = pltpu.make_async_remote_copy(
            east_out, west_in, halo_sem.at[sems], halo_sem.at[sems + 1],
            device_id=((gx + 1) % N_GX, gy), device_id_type=MESH)
        b = pltpu.make_async_remote_copy(
            west_out, east_in, halo_sem.at[sems + 2], halo_sem.at[sems + 3],
            device_id=((gx + N_GX - 1) % N_GX, gy), device_id_type=MESH)
        return a, b

    north_gy = jnp.minimum(gy + 1, N_GY - 1)
    south_gy = jnp.maximum(gy - 1, 0)

    def rows_north(upper, lower, south, north, sems):
        to_north = pltpu.make_async_remote_copy(
            upper, south, halo_sem.at[sems], halo_sem.at[sems + 1],
            device_id=(gx, north_gy), device_id_type=MESH)
        to_partner = pltpu.make_async_remote_copy(
            upper, north, halo_sem.at[sems], halo_sem.at[sems + 3],
            device_id=(N_GX - 1 - gx, gy), device_id_type=MESH)
        pl.when(jnp.logical_not(top))(to_north.start)
        pl.when(top)(to_partner.start)

    def rows_south(upper, lower, south, north, sems):
        to_south = pltpu.make_async_remote_copy(
            lower, north, halo_sem.at[sems + 2], halo_sem.at[sems + 3],
            device_id=(gx, south_gy), device_id_type=MESH)
        pl.when(gy > 0)(to_south.start)

    def rows_start(*args):
        rows_north(*args)
        rows_south(*args)

    def rows_wait(upper, lower, south, north, sems):
        wait_for(north, halo_sem.at[sems + 3])
        wait_for(upper, halo_sem.at[sems])

        @pl.when(gy > 0)
        def _():
            wait_for(south, halo_sem.at[sems + 1])
            wait_for(lower, halo_sem.at[sems + 2])

    def strips(first, count, tile=0, tiles=CT):
        return tuple(
            ext.at[pl.ds(first, count), pl.ds(tile, tiles), pl.ds(at, HALO)]
            for at in (ROWS, HALO, 0, HALO + ROWS))

    back_sub = 7 - lax.broadcasted_iota(jnp.int32, (8, 128), 0)
    back_lane = 127 - lane

    def turned(x):
        x = jnp.take_along_axis(x, back_lane, axis=1)
        return jnp.take_along_axis(x, back_sub, axis=0)

    def fold(ref, first, count, base, odd):
        tall = HALO // 8

        def body(f, carry):
            sign = jnp.where((f >= odd[0]) & (f < odd[1]), -1.0, 1.0)
            for j in range(TILES_X // 2 + 1):
                pair = (j, TILES_X - 1 - j) if j < TILES_X // 2 else (TILES_X,)
                old = [[ref[f, c, pl.ds(base + p * 8, 8)] for c in pair] for p in range(tall)]
                for p in range(tall):
                    for n, c in enumerate(pair):
                        ref[f, c, pl.ds(base + p * 8, 8)] = turned(old[tall - 1 - p][len(pair) - 1 - n]) * sign
            return carry

        lax.fori_loop(first, first + count, body, 0)

    static_cols = columns(to_east, to_west, from_west, from_east, 0)
    force_cols = columns(force_to_east, force_to_west, force_from_west, force_from_east, 4)
    static_rows = strips(0, STATIC)
    force_rows = strips(FORCE_X, 2)

    pl.semaphore_wait(barrier, N_DEV - 1)

    def send_mass(a, b):
        pltpu.make_async_remote_copy(
            mass_out.at[pl.ds((a * N_GY + b) * 2, 2)], mass_in.at[pl.ds(me * 2, 2)],
            a2a_sem.at[4], a2a_sem.at[5], device_id=(a, b), device_id_type=MESH,
        ).start()

    def pack_forces(d):
        for h in range(2):
            tile = oc[place[FIRST + h, d]]
            m = TILT * mass_in[d * 2 + h]
            outgoing[d * 2 + h, 0] = tile[0] + m * tile[2]
            outgoing[d * 2 + h, 1] = tile[1] + m * tile[3]

    def send_forces(a, b):
        d = a * N_GY + b
        pack_forces(d)
        pltpu.make_async_remote_copy(
            outgoing.at[pl.ds(d * 2, 2)], arrived.at[pl.ds(me * 2, 2)],
            a2a_sem.at[0], a2a_sem.at[1], device_id=(a, b), device_id_type=MESH,
        ).start()

    each_peer(send_mass, (
        lambda q: rows_north(*strips(2 * q, 1, 0, TILES_X), 8),
        lambda q: rows_south(*strips(2 * q, 1, 0, TILES_X), 8),
        lambda q: rows_north(*strips(2 * q + 1, 1, 0, TILES_X), 8),
        lambda q: rows_south(*strips(2 * q + 1, 1, 0, TILES_X), 8),
    ))
    for h in range(2):
        mass_in[me * 2 + h] = mass_out[me * 2 + h]
    gather_columns(0, STATIC, to_east, to_west)
    for copy in static_cols:
        copy.start()
    for copy in static_cols:
        copy.wait()
    spread_columns(0, STATIC, from_west, from_east)

    wait_for(oc, in_sem.at[0])
    wait_for(mass_in.at[pl.ds(0, 2 * N_DEV - 2)], a2a_sem.at[5])
    rows_start(*strips(0, STATIC, TILES_X, 1), 8)
    each_peer(send_forces)
    pack_forces(me)
    for h in range(2):
        arrived[me * 2 + h] = outgoing[me * 2 + h]
    wait_for(mass_out.at[pl.ds(0, 2 * N_DEV - 2)], a2a_sem.at[4])

    @pl.when(gy == 0)
    def _():
        zero = jnp.zeros((8, 128), jnp.float32)

        def clear(j, carry):
            for p in range(HALO // 8):
                for f in range(FIELDS):
                    ext[f, j, pl.ds(p * 8, 8)] = zero + 1.0 if f == MASS else zero
            return carry

        lax.fori_loop(0, CT, clear, 0)

    rows_wait(*static_rows, 8)

    @pl.when(top)
    def _():
        fold(ext, 0, STATIC, HALO + ROWS, (ZONAL, MERID + 1))

    def arrange(r, carry):
        rows = pl.ds(r, 8, stride=STEP)
        for j in range(CT):
            share = ext[SHARE, j, rows]
            m = ext[MASS, j, rows]
            strong = ext[STRENGTH, j, rows]
            a = m + DRAG
            b = TURN * m
            scale = share / (a * a + b * b)
            km[r, j] = m
            ka[r, j] = a * scale
            kb[r, j] = b * scale
            ks[r, j] = (0.0125 * KEEP) * strong
            cstr[r + 1, j] = strong
            cu[r + 1, j] = ext[ZONAL, j, rows] * share
            cv[r + 1, j] = ext[MERID, j, rows] * share
            both = 0.25 * (ext[SUM, j, rows] + strong)
            apart = 0.25 * ext[DIFF, j, rows]
            cxx[r + 1, j] = both + apart
            cyy[r + 1, j] = both - apart
            csh[r + 1, j] = 0.5 * ext[SHEAR, j, rows]
        return carry

    lax.fori_loop(0, STEP, arrange, 0)

    def ghosts(*refs):
        for ref in refs:
            for j in range(CT):
                ref[0, j] = pltpu.roll(ref[STEP, j], 1, 0)
                ref[STEP + 1, j] = pltpu.roll(ref[1, j], 7, 0)

    ghosts(cu, cv, cstr)

    def gradient(r, carry):
        left, right = left_right([cstr[r + 1, j] for j in range(CT)], lane)
        for j in range(CT):
            kfx[r, j] = -0.25 * (right[j] - left[j])
            kfy[r, j] = -0.25 * (cstr[r + 2, j] - cstr[r, j])
        return carry

    lax.fori_loop(0, STEP, gradient, 0)

    wait_for(arrived.at[pl.ds(0, 2 * N_DEV - 2)], a2a_sem.at[1])
    wait_for(outgoing.at[pl.ds(0, 2 * N_DEV - 2)], a2a_sem.at[0])

    def forces(i, carry):
        rows = aligned(HALO + i * 8)
        for j in range(TILES_X):
            tile = arrived[place[RECV_SLOT, i * TILES_X + j]]
            ext[FORCE_X, j, rows] = tile[0]
            ext[FORCE_Y, j, rows] = tile[1]
        return carry

    lax.fori_loop(0, ROWS // 8, forces, 0)
    gather_columns(FORCE_X, 2, force_to_east, force_to_west)
    for copy in force_cols:
        copy.start()
    rows_start(*strips(FORCE_X, 2, 0, TILES_X), 12)
    def arrange_forces(r, carry):
        rows = pl.ds(r, 8, stride=STEP)
        for j in range(CT):
            kfx[r, j] += ext[FORCE_X, j, rows]
            kfy[r, j] += ext[FORCE_Y, j, rows]
        return carry

    def take_forces():
        for copy in force_cols:
            copy.wait()
        spread_columns(FORCE_X, 2, force_from_west, force_from_east)
        rows_start(*strips(FORCE_X, 2, TILES_X, 1), 12)
        rows_wait(*force_rows, 12)

        @pl.when(top)
        def _():
            fold(ext, FORCE_X, 2, HALO + ROWS, (FORCE_X, FORCE_Y + 1))

        lax.fori_loop(0, STEP, arrange_forces, 0)

    def shifted(ref, r):
        def left(j):
            return pltpu.roll(jnp.where(lane == 127, ref[r, (j - 1) % CT], ref[r, j]), 1, 1)

        def right(j):
            return pltpu.roll(jnp.where(lane == 0, ref[r, (j + 1) % CT], ref[r, j]), 127, 1)

        return left, right

    def stresses(i, carry):
        for r in [i * UNROLL + h for h in range(UNROLL)]:
            u_left, u_right = shifted(cu, r + 1)
            v_left, v_right = shifted(cv, r + 1)
            for j in range(CT):
                ux = u_right(j) - u_left(j)
                vx = v_right(j) - v_left(j)
                uy = cu[r + 2, j] - cu[r, j]
                vy = cv[r + 2, j] - cv[r, j]
                div = ux + vy
                ten = ux - vy
                shr = uy + vx
                div2 = div + div
                w = ks[r, j] * lax.rsqrt(div2 * div2 + ten * ten + shr * shr + 16.0)
                div4 = div2 + div2
                cxx[r + 1, j] = KEEP * cxx[r + 1, j] + w * (div4 + ten)
                cyy[r + 1, j] = KEEP * cyy[r + 1, j] + w * (div4 - ten)
                csh[r + 1, j] = KEEP * csh[r + 1, j] + w * shr
        return carry

    def momentum(i, carry):
        for r in [i * UNROLL + h for h in range(UNROLL)]:
            xx_left, xx_right = shifted(cxx, r + 1)
            sh_left, sh_right = shifted(csh, r + 1)
            for j in range(CT):
                px = (xx_right(j) - xx_left(j)) + (csh[r + 2, j] - csh[r, j])
                py = (sh_right(j) - sh_left(j)) + (cyy[r + 2, j] - cyy[r, j])
                m = km[r, j]
                rx = m * cu[r + 1, j] + (px + kfx[r, j])
                ry = m * cv[r + 1, j] + (py + kfy[r, j])
                a = ka[r, j]
                b = kb[r, j]
                cu[r + 1, j] = a * rx + b * ry
                cv[r + 1, j] = a * ry - b * rx
        return carry

    carried = (cu, cv, cxx, cyy, csh)

    def to_grid_order(first, count):
        def body(r, carry):
            for f in range(first, first + count):
                for j in range(CT):
                    nat[f, j, pl.ds(r, 8, stride=STEP)] = carried[f][r + 1, j]
            return carry

        lax.fori_loop(0, STEP, body, 0)

    def from_grid_order(r, carry):
        for f, ref in enumerate(carried):
            for j in range(CT):
                ref[r + 1, j] = nat[f, j, pl.ds(r, 8, stride=STEP)]
        return carry

    state_rows = (nat.at[:, :, pl.ds(ROWS, HALO)], nat.at[:, :, pl.ds(HALO, HALO)], from_south, from_north)

    def take(strip, base):
        def body(j, carry):
            for f in range(5):
                for p in range(HALO // 8):
                    nat[f, j, pl.ds(base + p * 8, 8)] = strip[f, j, pl.ds(p * 8, 8)]
            return carry

        lax.fori_loop(0, CT, body, 0)

    def send_rows(first, count):
        for f in range(first, first + count):
            to_grid_order(f, 1)
            rows_start(
                nat.at[f, :, pl.ds(ROWS, HALO)], nat.at[f, :, pl.ds(HALO, HALO)],
                from_south.at[f], from_north.at[f], 16)

    def exchange_rows():
        send_rows(0, 2)
        rows_wait(*state_rows, 16)

        @pl.when(top)
        def _():
            fold(from_north, 0, 5, 0, (0, 2))

        take(from_north, HALO + ROWS)

        @pl.when(gy > 0)
        def _():
            take(from_south, 0)

        lax.fori_loop(0, STEP, from_grid_order, 0)
        ghosts(cu, cv)

    def subcycle(t, carry):
        lax.fori_loop(0, STEP // UNROLL, stresses, 0)
        pl.when(t == 0)(take_forces)
        pl.when(t == ITERS // LEGS - 1)(lambda: send_rows(2, 3))
        ghosts(cyy, csh)
        lax.fori_loop(0, STEP // UNROLL, momentum, 0)
        ghosts(cu, cv)
        pl.when(t == ITERS // LEGS - 1)(exchange_rows)
        return carry

    lax.fori_loop(0, ITERS, subcycle, 0)
    to_grid_order(0, 2)

    def to_tiles(i, carry):
        rows = aligned(HALO + i * 8)
        for j in range(TILES_X):
            tiles[i * TILES_X + j, 0] = nat[0, j, rows]
            tiles[i * TILES_X + j, 1] = nat[1, j, rows]
        return carry

    lax.fori_loop(0, ROWS // 8, to_tiles, 0)

    def pack_back(d):
        returning[d * 2] = tiles[place[EARLY, d]]
        returning[d * 2 + 1] = tiles[place[LATE, d]]

    def send_back(a, b):
        d = a * N_GY + b
        pack_back(d)
        pltpu.make_async_remote_copy(
            returning.at[pl.ds(d * 2, 2)], arrived_back.at[pl.ds(me * 2, 2)],
            a2a_sem.at[2], a2a_sem.at[3], device_id=(a, b), device_id_type=MESH,
        ).start()

    each_peer(send_back)
    pack_back(me)
    for h in range(2):
        arrived_back[me * 2 + h] = returning[me * 2 + h]
    to_grid_order(2, 3)

    def finish(i, carry):
        rows = aligned(HALO + i * 8)
        for j in range(TILES_X):
            xx = nat[2, j, rows]
            yy = nat[3, j, rows]
            final[0, j, aligned(i * 8)] = 2.0 * (xx + yy) - ext[STRENGTH, j, rows]
            final[1, j, aligned(i * 8)] = 2.0 * (xx - yy)
            final[2, j, aligned(i * 8)] = 2.0 * nat[4, j, rows]
        return carry

    lax.fori_loop(0, ROWS // 8, finish, 0)
    for j in range(TILES_X):
        pltpu.make_async_copy(final.at[:, j], out_stress.at[:, :, pl.ds(j * 128, 128)], in_sem.at[1]).start()

    wait_for(arrived_back.at[pl.ds(0, 2 * N_DEV - 2)], a2a_sem.at[3])
    wait_for(returning.at[pl.ds(0, 2 * N_DEV - 2)], a2a_sem.at[2])

    def unpack(i, carry):
        for h in range(8):
            out_velocity[i * 8 + h] = arrived_back[place[BACK_SLOT, i * 8 + h]]
        return carry

    lax.fori_loop(0, N_DEV // 8, unpack, 0)
    wait_for(final, in_sem.at[1])


def local(ocean_forcing, route, land_mask, mass, strength, velocity_start, stress_start):
    f32, i32 = jnp.float32, jnp.int32
    hbm = pl.BlockSpec(memory_space=pl.ANY)
    ghosted = pltpu.VMEM((STEP + 2, CT, 8, 128), f32)
    plain = pltpu.VMEM((STEP, CT, 8, 128), f32)
    side = pltpu.VMEM((STATIC // 4, ROWS, 128), f32)
    force_side = pltpu.VMEM((1, ROWS, 128), f32)
    strip = pltpu.VMEM((5, CT, HALO, 128), f32)
    return pl.pallas_call(
        kernel,
        out_shape=(
            jax.ShapeDtypeStruct((N_DEV, 2, 8, 128), f32),
            jax.ShapeDtypeStruct((3, ROWS, TILES_X * 128), f32),
        ),
        in_specs=[hbm] * 7,
        out_specs=(pl.BlockSpec(memory_space=pltpu.VMEM), hbm),
        scratch_shapes=[
            pltpu.VMEM((N_DEV, N_DEV), i32),
            pltpu.VMEM((8, N_DEV), i32),
            pltpu.SMEM((8, N_DEV), i32),
            pltpu.VMEM((N_DEV, 4, 8, 128), f32),
            pltpu.VMEM((N_DEV, 8, 128), f32),
            pltpu.VMEM((2 * N_DEV, 8, 128), f32),
            pltpu.VMEM((2 * N_DEV, 8, 128), f32),
            pltpu.VMEM((2 * N_DEV, 2, 8, 128), f32),
            pltpu.VMEM((2 * N_DEV, 2, 8, 128), f32),
            pltpu.VMEM((FIELDS, CT, EXT, 128), f32),
            pltpu.VMEM((TILES_X, ROWS, 128), i32),
            side, side, side, side,
            force_side, force_side, force_side, force_side,
            pltpu.VMEM((5, CT, EXT, 128), f32),
            strip, strip,
            pltpu.VMEM((3, TILES_X, ROWS, 128), f32),
            pltpu.VMEM((N_DEV, 2, 8, 128), f32),
            pltpu.VMEM((2 * N_DEV, 2, 8, 128), f32),
            pltpu.VMEM((2 * N_DEV, 2, 8, 128), f32),
            ghosted, ghosted, ghosted, ghosted, ghosted, ghosted,
            plain, plain, plain, plain, plain, plain,
            pltpu.SemaphoreType.DMA((6,)),
            pltpu.SemaphoreType.DMA((6,)),
            pltpu.SemaphoreType.DMA((20,)),
        ],
        compiler_params=pltpu.CompilerParams(
            collective_id=0, has_side_effects=True, vmem_limit_bytes=56 * 1024 * 1024),
    )(route.reshape(N_DEV, N_DEV), ocean_forcing, land_mask, mass, strength, velocity_start, stress_start)


def solution(mesh):
    placed = (
        P(("gx", "gy"), None, None, None),
        P(),
        P("gy", "gx"),
        P("gy", "gx"),
        P("gy", "gx"),
        P(None, "gy", "gx"),
        P(None, "gy", "gx"),
    )
    return jax.shard_map(
        local,
        mesh=mesh,
        in_specs=placed,
        out_specs=(P(("gx", "gy"), None, None, None), P(None, "gy", "gx")),
        check_vma=False,
    )
```

```python
import functools

import jax
import jax.numpy as jnp
from jax import lax
from jax.experimental import pallas as pl
from jax.experimental.pallas import tpu as pltpu
from jax.sharding import PartitionSpec as P

MESH = pl.DeviceIdType.MESH
ITERS = 16
RELAX = 0.1
DRAG = 0.5
TURN = 0.3
TILT = 0.05
KEEP = 1.0 / (1.0 + RELAX)

N_GX = 8
N_GY = 16
N_DEV = 128
LEGS = 2
HALO = 2 * ITERS // LEGS
SIDE = 2 * ITERS
ROWS = 128
EXT = ROWS + 2 * HALO
STEP = EXT // 8
TILES_X = 8
CT = TILES_X + 1
UNROLL = 20

MASS, STRENGTH, ZONAL, MERID, SUM, DIFF, SHEAR, SHARE, FORCE_X, FORCE_Y = range(10)
STATIC = 8
FIELDS = 10
FIRST, SECOND, BACK_SLOT, RECV_SLOT, EARLY, LATE = range(6)


def peers():
    order = []
    for n in range(32):
        j = (n * 13) % 32
        dx, dy, dc = j // 8, (j // 2) % 4, j % 2
        off = (n + n // 4 + 3 * dx + dy) % 4 if (dx, dy, dc) != (0, 0, 0) else 0
        order.append((dx, dy, dc, off))
    return order


def each_peer(visit, between=()):
    gx = lax.axis_index("gx")
    gy = lax.axis_index("gy")
    z, x_lo = gx % 4, gx // 4
    x_hi, y, core = gy // 8, (gy // 2) % 4, gy % 2
    x = x_hi * 2 + x_lo
    xs = [(x + d) % 4 for d in range(4)]
    part_gx = [(v % 2) * 4 for v in xs]
    part_gy = [(v // 2) * 8 for v in xs]
    ys = [((y + d) % 4) * 2 for d in range(4)]
    cores = [core, 1 - core]
    zs = tuple((z + d) % 4 for d in range(4))

    def turn(q, zs):
        for n, (dx, dy, dc, off) in enumerate(peers()):
            for i, extra in enumerate(between):
                if n == (2 * i + 1) * 16 // len(between):
                    extra(q)
            there = (part_gx[dx] + zs[off], part_gy[dx] + ys[dy] + cores[dc])
            if (dx, dy, dc) == (0, 0, 0):
                pl.when(q > 0)(functools.partial(visit, *there))
            else:
                visit(*there)
        return zs[1:] + zs[:1]

    lax.fori_loop(0, 4, turn, zs)


def wait_for(ref, sem):
    pltpu.make_async_copy(ref, ref, sem).wait()


def steps(count, body, by):
    def several(i, carry):
        for h in range(by):
            body(i * by + h, carry)
        return carry

    lax.fori_loop(0, count // by, several, 0)


def aligned(start, size=8):
    return pl.ds(pl.multiple_of(start, 8), size)


def left_right(row, lane):
    n = len(row)
    left = [pltpu.roll(jnp.where(lane == 127, row[j - 1], row[j]), 1, 1) for j in range(n)]
    right = [pltpu.roll(jnp.where(lane == 0, row[(j + 1) % n], row[j]), 127, 1) for j in range(n)]
    return left, right


def fill_table(route, table, me):
    shape = (N_DEV, N_DEV)
    sub = lax.broadcasted_iota(jnp.int32, shape, 0)
    lane = lax.broadcasted_iota(jnp.int32, shape, 1)
    diagonal = sub == lane

    def to_column(row):
        return jnp.sum(jnp.where(diagonal, row, 0), axis=1, keepdims=True)

    def to_row(column):
        return jnp.sum(jnp.where(diagonal, column, 0), axis=0, keepdims=True)

    mine = jnp.right_shift(route[pl.ds(me, 1), :], 7)
    column = to_column(mine)
    hit = column == lane
    table[pl.ds(FIRST, 1), :] = jnp.min(jnp.where(hit, sub, N_DEV - 1), axis=0, keepdims=True)
    table[pl.ds(SECOND, 1), :] = jnp.max(jnp.where(hit, sub, 0), axis=0, keepdims=True)
    rank = jnp.max(jnp.where((column == mine) & (sub < lane), 1, 0), axis=0, keepdims=True)
    table[pl.ds(BACK_SLOT, 1), :] = mine * 2 + rank
    ids = route[...]
    here = jnp.right_shift(ids, 7) == me
    inside = jnp.bitwise_and(ids, N_DEV - 1)
    first = jnp.min(jnp.where(here, lane, N_DEV), axis=1, keepdims=True)
    second = jnp.max(jnp.where(here, lane, -1), axis=1, keepdims=True)
    early = jnp.sum(jnp.where(lane == first, inside + 1, 0), axis=1, keepdims=True) - 1
    late = jnp.sum(jnp.where(lane == second, inside + 1, 0), axis=1, keepdims=True) - 1
    slot = jnp.where(late == lane, 2 * sub + 1, jnp.where(early == lane, 2 * sub, 0))
    table[pl.ds(RECV_SLOT, 1), :] = jnp.max(slot, axis=0, keepdims=True)
    table[pl.ds(EARLY, 1), :] = to_row(jnp.maximum(early, 0))
    table[pl.ds(LATE, 1), :] = to_row(jnp.maximum(late, 0))
    table[pl.ds(6, 2), :] = jnp.zeros((2, N_DEV), jnp.int32)


def kernel(
    route, ocean, mask, mass, strength, velocity, stress,
    out_velocity, out_stress,
    routes, table, place, oc, mass_tiles, mass_out, mass_in, outgoing, arrived, ext, ext_mask,
    to_east, to_west, from_west, from_east, force_to_east, force_to_west, force_from_west, force_from_east,
    nat, from_south, from_north, final, tiles, returning, arrived_back,
    cu, cv, cxx, cyy, csh, cstr, ks, km, kfx, kfy, ka, kb,
    in_sem, a2a_sem, halo_sem,
):
    gx = lax.axis_index("gx")
    gy = lax.axis_index("gy")
    me = gx * N_GY + gy
    top = gy == N_GY - 1
    inner = pl.ds(HALO, ROWS)
    lane = lax.broadcasted_iota(jnp.int32, (8, 128), 1)

    pltpu.make_async_copy(route, routes, in_sem.at[3]).start()
    for j in range(TILES_X):
        pltpu.make_async_copy(mass.at[:, pl.ds(j * 128, 128)], ext.at[MASS, j, inner], in_sem.at[5]).start()
    for j in range(TILES_X):
        cols = pl.ds(j * 128, 128)
        pltpu.make_async_copy(strength.at[:, cols], ext.at[STRENGTH, j, inner], in_sem.at[1]).start()
        pltpu.make_async_copy(velocity.at[:, :, cols], ext.at[pl.ds(ZONAL, 2), j, inner], in_sem.at[1]).start()
        pltpu.make_async_copy(stress.at[:, :, cols], ext.at[pl.ds(SUM, 3), j, inner], in_sem.at[1]).start()
        pltpu.make_async_copy(mask.at[:, cols], ext_mask.at[j], in_sem.at[2]).start()

    pltpu.make_async_copy(ocean, oc, in_sem.at[0]).start()
    barrier = pltpu.get_barrier_semaphore()

    def greet(a, b):
        pl.semaphore_signal(barrier, inc=1, device_id=(a, b), device_id_type=MESH)

    each_peer(greet)

    wait_for(routes, in_sem.at[3])
    fill_table(routes, table, me)
    to_place = pltpu.make_async_copy(table, place, in_sem.at[4])
    to_place.start()

    wait_for(ext.at[MASS, pl.ds(0, TILES_X), inner], in_sem.at[5])

    def to_mass_tiles(i, carry):
        for j in range(TILES_X):
            mass_tiles[i * TILES_X + j] = ext[MASS, j, aligned(HALO + i * 8)]
        return carry

    steps(ROWS // 8, to_mass_tiles, 4)
    to_place.wait()

    def pack_mass(i, carry):
        for h in range(8):
            mass_out[i * 16 + 2 * h] = mass_tiles[place[EARLY, i * 8 + h]]
            mass_out[i * 16 + 2 * h + 1] = mass_tiles[place[LATE, i * 8 + h]]
        return carry

    steps(N_DEV // 8, pack_mass, 2)

    wait_for(ext_mask, in_sem.at[2])

    def shares(i, carry):
        for j in range(TILES_X):
            ext[SHARE, j, aligned(HALO + i * 8)] = ext_mask[j, aligned(i * 8)].astype(jnp.float32)
        return carry

    steps(ROWS // 8, shares, 4)

    wait_for(ext.at[pl.ds(STRENGTH, STATIC - 2), pl.ds(0, TILES_X), inner], in_sem.at[1])

    def gather_columns(first, count, east_out, west_out):
        def body(i, carry):
            rows = aligned(HALO + i * 8)
            for g in range((count + 3) // 4):
                e = w = None
                for q in range(min(4, count - 4 * g)):
                    f = first + 4 * g + q
                    a = pltpu.roll(ext[f, TILES_X - 1, rows], (SIDE * (q + 1)) % 128, 1)
                    b = ext[f, 0, rows]
                    if q:
                        b = pltpu.roll(b, SIDE * q, 1)
                    e = a if q == 0 else jnp.where(lane < SIDE * q, e, a)
                    w = b if q == 0 else jnp.where(lane < SIDE * q, w, b)
                east_out[g, aligned(i * 8)] = e
                west_out[g, aligned(i * 8)] = w
            return carry

        steps(ROWS // 8, body, 4)

    def spread_columns(first, count, west_in, east_in):
        def body(i, carry):
            rows = aligned(HALO + i * 8)
            for g in range((count + 3) // 4):
                e = east_in[g, aligned(i * 8)]
                w = west_in[g, aligned(i * 8)]
                for q in range(min(4, count - 4 * g)):
                    right = pltpu.roll(e, 128 - SIDE * q, 1) if q else e
                    left = pltpu.roll(w, 128 - SIDE * (q + 1), 1) if q < 3 else w
                    ext[first + 4 * g + q, TILES_X, rows] = jnp.where(lane < 64, right, left)
            return carry

        steps(ROWS // 8, body, 4)

    def columns(east_out, west_out, west_in, east_in, sems):
        a = pltpu.make_async_remote_copy(
            east_out, west_in, halo_sem.at[sems], halo_sem.at[sems + 1],
            device_id=((gx + 1) % N_GX, gy), device_id_type=MESH)
        b = pltpu.make_async_remote_copy(
            west_out, east_in, halo_sem.at[sems + 2], halo_sem.at[sems + 3],
            device_id=((gx + N_GX - 1) % N_GX, gy), device_id_type=MESH)
        return a, b

    north_gy = jnp.minimum(gy + 1, N_GY - 1)
    south_gy = jnp.maximum(gy - 1, 0)

    def rows_north(upper, lower, south, north, sems):
        to_north = pltpu.make_async_remote_copy(
            upper, south, halo_sem.at[sems], halo_sem.at[sems + 1],
            device_id=(gx, north_gy), device_id_type=MESH)
        to_partner = pltpu.make_async_remote_copy(
            upper, north, halo_sem.at[sems], halo_sem.at[sems + 3],
            device_id=(N_GX - 1 - gx, gy), device_id_type=MESH)
        pl.when(jnp.logical_not(top))(to_north.start)
        pl.when(top)(to_partner.start)

    def rows_south(upper, lower, south, north, sems):
        to_south = pltpu.make_async_remote_copy(
            lower, north, halo_sem.at[sems + 2], halo_sem.at[sems + 3],
            device_id=(gx, south_gy), device_id_type=MESH)
        pl.when(gy > 0)(to_south.start)

    def rows_start(*args):
        rows_north(*args)
        rows_south(*args)

    def rows_wait(upper, lower, south, north, sems):
        wait_for(north, halo_sem.at[sems + 3])
        wait_for(upper, halo_sem.at[sems])

        @pl.when(gy > 0)
        def _():
            wait_for(south, halo_sem.at[sems + 1])
            wait_for(lower, halo_sem.at[sems + 2])

    def strips(first, count, tile=0, tiles=CT):
        return tuple(
            ext.at[pl.ds(first, count), pl.ds(tile, tiles), pl.ds(at, HALO)]
            for at in (ROWS, HALO, 0, HALO + ROWS))

    back_sub = 7 - lax.broadcasted_iota(jnp.int32, (8, 128), 0)
    back_lane = 127 - lane

    def turned(x):
        x = jnp.take_along_axis(x, back_lane, axis=1)
        return jnp.take_along_axis(x, back_sub, axis=0)

    def fold(ref, first, count, base, odd):
        tall = HALO // 8

        def body(f, carry):
            sign = jnp.where((f >= odd[0]) & (f < odd[1]), -1.0, 1.0)
            for j in range(TILES_X // 2 + 1):
                pair = (j, TILES_X - 1 - j) if j < TILES_X // 2 else (TILES_X,)
                old = [[ref[f, c, pl.ds(base + p * 8, 8)] for c in pair] for p in range(tall)]
                for p in range(tall):
                    for n, c in enumerate(pair):
                        ref[f, c, pl.ds(base + p * 8, 8)] = turned(old[tall - 1 - p][len(pair) - 1 - n]) * sign
            return carry

        lax.fori_loop(first, first + count, body, 0)

    static_cols = columns(to_east, to_west, from_west, from_east, 0)
    force_cols = columns(force_to_east, force_to_west, force_from_west, force_from_east, 4)
    static_rows = strips(0, STATIC)
    force_rows = strips(FORCE_X, 2)

    pl.semaphore_wait(barrier, N_DEV - 1)

    def send_mass(a, b):
        pltpu.make_async_remote_copy(
            mass_out.at[pl.ds((a * N_GY + b) * 2, 2)], mass_in.at[pl.ds(me * 2, 2)],
            a2a_sem.at[4], a2a_sem.at[5], device_id=(a, b), device_id_type=MESH,
        ).start()

    def pack_forces(d):
        for h in range(2):
            tile = oc[place[FIRST + h, d]]
            m = TILT * mass_in[d * 2 + h]
            outgoing[d * 2 + h, 0] = tile[0] + m * tile[2]
            outgoing[d * 2 + h, 1] = tile[1] + m * tile[3]

    def send_forces(a, b):
        d = a * N_GY + b
        pack_forces(d)
        pltpu.make_async_remote_copy(
            outgoing.at[pl.ds(d * 2, 2)], arrived.at[pl.ds(me * 2, 2)],
            a2a_sem.at[0], a2a_sem.at[1], device_id=(a, b), device_id_type=MESH,
        ).start()

    each_peer(send_mass, (
        lambda q: rows_north(*strips(2 * q, 1, 0, TILES_X), 8),
        lambda q: rows_south(*strips(2 * q, 1, 0, TILES_X), 8),
        lambda q: rows_north(*strips(2 * q + 1, 1, 0, TILES_X), 8),
        lambda q: rows_south(*strips(2 * q + 1, 1, 0, TILES_X), 8),
    ))
    for h in range(2):
        mass_in[me * 2 + h] = mass_out[me * 2 + h]
    gather_columns(0, STATIC, to_east, to_west)
    for copy in static_cols:
        copy.start()
    for copy in static_cols:
        copy.wait()
    spread_columns(0, STATIC, from_west, from_east)

    wait_for(oc, in_sem.at[0])
    wait_for(mass_in.at[pl.ds(0, 2 * N_DEV - 2)], a2a_sem.at[5])
    rows_start(*strips(0, STATIC, TILES_X, 1), 8)
    each_peer(send_forces)
    pack_forces(me)
    for h in range(2):
        arrived[me * 2 + h] = outgoing[me * 2 + h]
    wait_for(mass_out.at[pl.ds(0, 2 * N_DEV - 2)], a2a_sem.at[4])

    @pl.when(gy == 0)
    def _():
        zero = jnp.zeros((8, 128), jnp.float32)

        def clear(j, carry):
            for p in range(HALO // 8):
                for f in range(FIELDS):
                    ext[f, j, pl.ds(p * 8, 8)] = zero + 1.0 if f == MASS else zero
            return carry

        lax.fori_loop(0, CT, clear, 0)

    rows_wait(*static_rows, 8)

    @pl.when(top)
    def _():
        fold(ext, 0, STATIC, HALO + ROWS, (ZONAL, MERID + 1))

    def arrange(r, carry):
        rows = pl.ds(r, 8, stride=STEP)
        for j in range(CT):
            share = ext[SHARE, j, rows]
            m = ext[MASS, j, rows]
            strong = ext[STRENGTH, j, rows]
            a = m + DRAG
            b = TURN * m
            scale = share / (a * a + b * b)
            km[r, j] = m
            ka[r, j] = a * scale
            kb[r, j] = b * scale
            ks[r, j] = (0.0125 * KEEP) * strong
            cstr[r + 1, j] = strong
            cu[r + 1, j] = ext[ZONAL, j, rows] * share
            cv[r + 1, j] = ext[MERID, j, rows] * share
            both = 0.25 * (ext[SUM, j, rows] + strong)
            apart = 0.25 * ext[DIFF, j, rows]
            cxx[r + 1, j] = both + apart
            cyy[r + 1, j] = both - apart
            csh[r + 1, j] = 0.5 * ext[SHEAR, j, rows]
        return carry

    steps(STEP, arrange, 2)

    def ghosts(*refs):
        for ref in refs:
            for j in range(CT):
                ref[0, j] = pltpu.roll(ref[STEP, j], 1, 0)
                ref[STEP + 1, j] = pltpu.roll(ref[1, j], 7, 0)

    ghosts(cu, cv, cstr)

    def gradient(r, carry):
        left, right = left_right([cstr[r + 1, j] for j in range(CT)], lane)
        for j in range(CT):
            kfx[r, j] = -0.25 * (right[j] - left[j])
            kfy[r, j] = -0.25 * (cstr[r + 2, j] - cstr[r, j])
        return carry

    steps(STEP, gradient, 2)

    wait_for(arrived.at[pl.ds(0, 2 * N_DEV - 2)], a2a_sem.at[1])
    wait_for(outgoing.at[pl.ds(0, 2 * N_DEV - 2)], a2a_sem.at[0])

    def forces(i, carry):
        rows = aligned(HALO + i * 8)
        for j in range(TILES_X):
            tile = arrived[place[RECV_SLOT, i * TILES_X + j]]
            ext[FORCE_X, j, rows] = tile[0]
            ext[FORCE_Y, j, rows] = tile[1]
        return carry

    steps(ROWS // 8, forces, 4)
    gather_columns(FORCE_X, 2, force_to_east, force_to_west)
    for copy in force_cols:
        copy.start()
    rows_start(*strips(FORCE_X, 2, 0, TILES_X), 12)
    def arrange_forces(r, carry):
        rows = pl.ds(r, 8, stride=STEP)
        for j in range(CT):
            kfx[r, j] += ext[FORCE_X, j, rows]
            kfy[r, j] += ext[FORCE_Y, j, rows]
        return carry

    def take_forces():
        for copy in force_cols:
            copy.wait()
        spread_columns(FORCE_X, 2, force_from_west, force_from_east)
        rows_start(*strips(FORCE_X, 2, TILES_X, 1), 12)
        rows_wait(*force_rows, 12)

        @pl.when(top)
        def _():
            fold(ext, FORCE_X, 2, HALO + ROWS, (FORCE_X, FORCE_Y + 1))

        steps(STEP, arrange_forces, 5)

    def shifted(ref, r):
        def left(j):
            return pltpu.roll(jnp.where(lane == 127, ref[r, (j - 1) % CT], ref[r, j]), 1, 1)

        def right(j):
            return pltpu.roll(jnp.where(lane == 0, ref[r, (j + 1) % CT], ref[r, j]), 127, 1)

        return left, right

    def stresses(i, carry):
        for r in [i * UNROLL + h for h in range(UNROLL)]:
            u_left, u_right = shifted(cu, r + 1)
            v_left, v_right = shifted(cv, r + 1)
            for j in range(CT):
                ux = u_right(j) - u_left(j)
                vx = v_right(j) - v_left(j)
                uy = cu[r + 2, j] - cu[r, j]
                vy = cv[r + 2, j] - cv[r, j]
                div = ux + vy
                ten = ux - vy
                shr = uy + vx
                div2 = div + div
                w = ks[r, j] * lax.rsqrt(div2 * div2 + ten * ten + shr * shr + 16.0)
                div4 = div2 + div2
                cxx[r + 1, j] = KEEP * cxx[r + 1, j] + w * (div4 + ten)
                cyy[r + 1, j] = KEEP * cyy[r + 1, j] + w * (div4 - ten)
                csh[r + 1, j] = KEEP * csh[r + 1, j] + w * shr
        return carry

    def momentum(i, carry):
        for r in [i * UNROLL + h for h in range(UNROLL)]:
            xx_left, xx_right = shifted(cxx, r + 1)
            sh_left, sh_right = shifted(csh, r + 1)
            for j in range(CT):
                px = (xx_right(j) - xx_left(j)) + (csh[r + 2, j] - csh[r, j])
                py = (sh_right(j) - sh_left(j)) + (cyy[r + 2, j] - cyy[r, j])
                m = km[r, j]
                rx = m * cu[r + 1, j] + (px + kfx[r, j])
                ry = m * cv[r + 1, j] + (py + kfy[r, j])
                a = ka[r, j]
                b = kb[r, j]
                cu[r + 1, j] = a * rx + b * ry
                cv[r + 1, j] = a * ry - b * rx
        return carry

    carried = (cu, cv, cxx, cyy, csh)

    def to_grid_order(first, count):
        def body(r, carry):
            for f in range(first, first + count):
                for j in range(CT):
                    nat[f, j, pl.ds(r, 8, stride=STEP)] = carried[f][r + 1, j]
            return carry

        steps(STEP, body, 5)

    def from_grid_order(r, carry):
        for f, ref in enumerate(carried):
            for j in range(CT):
                ref[r + 1, j] = nat[f, j, pl.ds(r, 8, stride=STEP)]
        return carry

    state_rows = (nat.at[:, :, pl.ds(ROWS, HALO)], nat.at[:, :, pl.ds(HALO, HALO)], from_south, from_north)

    def take(strip, base):
        def body(j, carry):
            for f in range(5):
                for p in range(HALO // 8):
                    nat[f, j, pl.ds(base + p * 8, 8)] = strip[f, j, pl.ds(p * 8, 8)]
            return carry

        steps(CT, body, 3)

    def send_rows(first, count):
        for f in range(first, first + count):
            to_grid_order(f, 1)
            rows_start(
                nat.at[f, :, pl.ds(ROWS, HALO)], nat.at[f, :, pl.ds(HALO, HALO)],
                from_south.at[f], from_north.at[f], 16)

    def exchange_rows():
        send_rows(0, 2)
        rows_wait(*state_rows, 16)

        @pl.when(top)
        def _():
            fold(from_north, 0, 5, 0, (0, 2))

        take(from_north, HALO + ROWS)

        @pl.when(gy > 0)
        def _():
            take(from_south, 0)

        steps(STEP, from_grid_order, 4)
        ghosts(cu, cv)

    def subcycle(t, carry):
        lax.fori_loop(0, STEP // UNROLL, stresses, 0)
        pl.when(t == 0)(take_forces)
        pl.when(t == ITERS // LEGS - 1)(lambda: send_rows(2, 3))
        ghosts(cyy, csh)
        lax.fori_loop(0, STEP // UNROLL, momentum, 0)
        ghosts(cu, cv)
        pl.when(t == ITERS // LEGS - 1)(exchange_rows)
        return carry

    lax.fori_loop(0, ITERS, subcycle, 0)
    to_grid_order(0, 2)

    def to_tiles(i, carry):
        rows = aligned(HALO + i * 8)
        for j in range(TILES_X):
            tiles[i * TILES_X + j, 0] = nat[0, j, rows]
            tiles[i * TILES_X + j, 1] = nat[1, j, rows]
        return carry

    steps(ROWS // 8, to_tiles, 4)

    def pack_back(d):
        returning[d * 2] = tiles[place[EARLY, d]]
        returning[d * 2 + 1] = tiles[place[LATE, d]]

    def send_back(a, b):
        d = a * N_GY + b
        pack_back(d)
        pltpu.make_async_remote_copy(
            returning.at[pl.ds(d * 2, 2)], arrived_back.at[pl.ds(me * 2, 2)],
            a2a_sem.at[2], a2a_sem.at[3], device_id=(a, b), device_id_type=MESH,
        ).start()

    each_peer(send_back)
    pack_back(me)
    for h in range(2):
        arrived_back[me * 2 + h] = returning[me * 2 + h]
    to_grid_order(2, 3)

    def finish(i, carry):
        rows = aligned(HALO + i * 8)
        for j in range(TILES_X):
            xx = nat[2, j, rows]
            yy = nat[3, j, rows]
            final[0, j, aligned(i * 8)] = 2.0 * (xx + yy) - ext[STRENGTH, j, rows]
            final[1, j, aligned(i * 8)] = 2.0 * (xx - yy)
            final[2, j, aligned(i * 8)] = 2.0 * nat[4, j, rows]
        return carry

    steps(ROWS // 8, finish, 2)
    for j in range(TILES_X):
        pltpu.make_async_copy(final.at[:, j], out_stress.at[:, :, pl.ds(j * 128, 128)], in_sem.at[1]).start()

    wait_for(arrived_back.at[pl.ds(0, 2 * N_DEV - 2)], a2a_sem.at[3])
    wait_for(returning.at[pl.ds(0, 2 * N_DEV - 2)], a2a_sem.at[2])

    def unpack(i, carry):
        for h in range(8):
            out_velocity[i * 8 + h] = arrived_back[place[BACK_SLOT, i * 8 + h]]
        return carry

    steps(N_DEV // 8, unpack, 4)
    wait_for(final, in_sem.at[1])


def local(ocean_forcing, route, land_mask, mass, strength, velocity_start, stress_start):
    f32, i32 = jnp.float32, jnp.int32
    hbm = pl.BlockSpec(memory_space=pl.ANY)
    ghosted = pltpu.VMEM((STEP + 2, CT, 8, 128), f32)
    plain = pltpu.VMEM((STEP, CT, 8, 128), f32)
    side = pltpu.VMEM((STATIC // 4, ROWS, 128), f32)
    force_side = pltpu.VMEM((1, ROWS, 128), f32)
    strip = pltpu.VMEM((5, CT, HALO, 128), f32)
    return pl.pallas_call(
        kernel,
        out_shape=(
            jax.ShapeDtypeStruct((N_DEV, 2, 8, 128), f32),
            jax.ShapeDtypeStruct((3, ROWS, TILES_X * 128), f32),
        ),
        in_specs=[hbm] * 7,
        out_specs=(pl.BlockSpec(memory_space=pltpu.VMEM), hbm),
        scratch_shapes=[
            pltpu.VMEM((N_DEV, N_DEV), i32),
            pltpu.VMEM((8, N_DEV), i32),
            pltpu.SMEM((8, N_DEV), i32),
            pltpu.VMEM((N_DEV, 4, 8, 128), f32),
            pltpu.VMEM((N_DEV, 8, 128), f32),
            pltpu.VMEM((2 * N_DEV, 8, 128), f32),
            pltpu.VMEM((2 * N_DEV, 8, 128), f32),
            pltpu.VMEM((2 * N_DEV, 2, 8, 128), f32),
            pltpu.VMEM((2 * N_DEV, 2, 8, 128), f32),
            pltpu.VMEM((FIELDS, CT, EXT, 128), f32),
            pltpu.VMEM((TILES_X, ROWS, 128), i32),
            side, side, side, side,
            force_side, force_side, force_side, force_side,
            pltpu.VMEM((5, CT, EXT, 128), f32),
            strip, strip,
            pltpu.VMEM((3, TILES_X, ROWS, 128), f32),
            pltpu.VMEM((N_DEV, 2, 8, 128), f32),
            pltpu.VMEM((2 * N_DEV, 2, 8, 128), f32),
            pltpu.VMEM((2 * N_DEV, 2, 8, 128), f32),
            ghosted, ghosted, ghosted, ghosted, ghosted, ghosted,
            plain, plain, plain, plain, plain, plain,
            pltpu.SemaphoreType.DMA((6,)),
            pltpu.SemaphoreType.DMA((6,)),
            pltpu.SemaphoreType.DMA((20,)),
        ],
        compiler_params=pltpu.CompilerParams(
            collective_id=0, has_side_effects=True, vmem_limit_bytes=56 * 1024 * 1024),
    )(route.reshape(N_DEV, N_DEV), ocean_forcing, land_mask, mass, strength, velocity_start, stress_start)


def solution(mesh):
    placed = (
        P(("gx", "gy"), None, None, None),
        P(),
        P("gy", "gx"),
        P("gy", "gx"),
        P("gy", "gx"),
        P(None, "gy", "gx"),
        P(None, "gy", "gx"),
    )
    return jax.shard_map(
        local,
        mesh=mesh,
        in_specs=placed,
        out_specs=(P(("gx", "gy"), None, None, None), P(None, "gy", "gx")),
        check_vma=False,
    )
```
